32 devices in a mesh: rows: 16 (over z, x, core), dirs: 2 (over y).
Axes of the slice: x: 2, y: 2, z: 4, core: 2. Of those that a mesh axis runs over, the one named last changes fastest.
Arguments:
- previous: bfloat16 [24, 32, 128, 512], P('dirs', None, 'rows'), may hold values from -12 to 12
- boundary: float32 [24, 32, 512], P('dirs'), may hold values from -6 to 6
- row_coupling: float32 [24, 128, 512], P('dirs', 'rows'), may hold values from 0 to 1
- cross_gain: float32 [24], P('dirs'), may hold values from 0.5 to 3
- block_inverse: float32 [24, 128, 128], P('dirs'), may hold values from 0 to 1, as said below
- quadrant: int32 [24], P('dirs'), may hold values from 0 to 3
- sea_mask: int32 [128, 512], P('rows'), may hold values from 0 to 1, as said below
- wet_tiles: int32 [128, 4], P('rows'), may hold values 0 or 1
- quad_coef: float32 [32], replicated, may hold values from 0.05 to 0.5
Outputs:
- action: bfloat16 [24, 32, 128, 512], P('dirs', None, 'rows')
The draws below stay inside these ranges and needn't reach their ends.
Inputs may be any that keep to these rules, and one draw needn't show every extreme that they name: `sea_mask`: in each row the land cells, if any, are the last ones, from a coastline column to the end of the row. block_inverse[d] is the inverse of the 128 x 128 lower bidiagonal matrix with 1 + cross_gain[d] on its diagonal and -cross_gain[d] just below it.
All inputs are finite; a program needn't handle non-finite values. No bound on the sum of `wet_tiles` on one device may be relied on, other than what follows from the above.
Results may differ from the reference program's by a relative error of at most 0.0027.
Values may be sent and summed in bfloat16 or wider, within the bound.
A program may use at most 128 MiB of HBM per device.

```python
import math
import jax
import jax.numpy as jnp
from jax import lax

SPECTRAL_ANGLES = 24
FREQ = 32
BLOCK = 128
SHIFT = 2
CX = 8
NY = 512
GRID_ROW_TOTAL = 128


def coupling_gains(key):
    unit = jax.random.uniform(jax.random.fold_in(key, 11), (SPECTRAL_ANGLES,), jnp.float32)
    return jnp.exp(jnp.log(0.5) + unit * (jnp.log(3.0) - jnp.log(0.5)))


def draw_cross_gain(key, part):
    return coupling_gains(key)


def draw_block_inverse(key, part):
    gains = coupling_gains(key)
    ratio = gains / (1.0 + gains)
    lower = jnp.arange(BLOCK)[:, None]
    upper = jnp.arange(BLOCK)[None, :]
    offset = jnp.maximum(lower - upper, 0).astype(jnp.float32)
    power = jnp.exp(offset[None] * jnp.log(ratio)[:, None, None])
    return jnp.where((lower >= upper)[None], power / (1.0 + gains)[:, None, None], 0.0).astype(jnp.float32)


def draw_sea_mask(key, part):
    stretch_count = 4
    coast_widths = jax.random.randint(jax.random.fold_in(key, 21), (stretch_count,), 1, NY // 2)
    ranking = jax.random.permutation(jax.random.fold_in(key, 22), stretch_count)
    coast_widths = jnp.where(ranking < 2, 0, coast_widths)
    stretch_of_row = jnp.arange(GRID_ROW_TOTAL) * stretch_count // GRID_ROW_TOTAL
    matching = stretch_of_row[:, None] == jnp.arange(stretch_count)[None, :]
    row_widths = jnp.sum(jnp.where(matching, coast_widths[None, :], 0), axis=1)
    column = jnp.arange(NY)[None, :]
    return (column < NY - row_widths[:, None]).astype(jnp.int32)


def draw_row_coupling(key, part):
    random_keys = jax.random.split(jax.random.fold_in(key, 31), 6)
    slow_pick = jax.random.bernoulli(random_keys[0], 0.5, (SPECTRAL_ANGLES,))
    slow_unit = jax.random.uniform(random_keys[1], (SPECTRAL_ANGLES,), jnp.float32)
    slow_rate = jnp.exp(jnp.log(0.1 / GRID_ROW_TOTAL) + slow_unit * (jnp.log(0.6 / GRID_ROW_TOTAL) - jnp.log(0.1 / GRID_ROW_TOTAL)))
    fast_unit = jax.random.uniform(random_keys[2], (SPECTRAL_ANGLES,), jnp.float32)
    fast_rate = jnp.exp(jnp.log(1.0 / 50.0) + fast_unit * (jnp.log(1.0 / 30.0) - jnp.log(1.0 / 50.0)))
    rates = jnp.where(slow_pick, slow_rate, fast_rate)
    spread = jax.random.uniform(random_keys[3], (SPECTRAL_ANGLES, GRID_ROW_TOTAL, NY), jnp.float32, 0.5, 2.0)
    gusty_rows = jax.random.randint(random_keys[4], (SPECTRAL_ANGLES, 2), 0, GRID_ROW_TOTAL)
    impacted_cells = jnp.any(jnp.arange(GRID_ROW_TOTAL)[None, None, :] == gusty_rows[:, :, None], axis=1)
    depth = jax.random.uniform(random_keys[5], (SPECTRAL_ANGLES, GRID_ROW_TOTAL), jnp.float32, 0.6, 0.85)
    factor = jnp.where(impacted_cells, depth, 1.0)
    return (jnp.exp(-rates[:, None, None] * spread) * factor[:, :, None]).astype(jnp.float32)


def set_ends(array, key, low, top_value):
    longest = array.shape.index(max(array.shape))
    spots = []
    for shift in (0, 1):
        where = [jax.random.randint(jax.random.fold_in(key, axis), (), 0, length) for axis, length in enumerate(array.shape)]
        where[longest] = (where[longest] + shift) % array.shape[longest]
        spots.append(tuple(where))
    return array.at[spots[0]].set(low).at[spots[1]].set(top_value)


def block_scale(rng, dims, shards, least, high):
    level, own = 1.0, jax.random.fold_in(rng, 6)
    for axis_at, shards_of in shards:
        steps = jnp.exp(jax.random.uniform(jax.random.fold_in(own, axis_at), (shards_of,), jnp.float32, least / len(shards), high / len(shards)))
        level = level * jnp.repeat(steps, dims[axis_at] // shards_of).reshape([-1 if axis == axis_at else 1 for axis in range(len(dims))])
    return level


def centred(stream_key, shape, scale, reach, shards=(), dtype=jnp.bfloat16):
    entries = jax.random.normal(stream_key, shape, jnp.float32) * scale
    if len(shards) > 0:
        entries = block_scale(stream_key, shape, shards, -0.22, 0.18) * entries
    return jnp.clip(entries, min=-reach, max=reach).astype(dtype)


def setup_inputs(seed: int = 0) -> dict:
    key_list = jax.random.split(jax.random.key(seed), 10)
    previous = centred(key_list[0], (SPECTRAL_ANGLES, FREQ, GRID_ROW_TOTAL, NY), 2.0, 12.0, ((0, 2), (2, 16)))
    boundary = centred(key_list[1], (SPECTRAL_ANGLES, FREQ, NY), 1.0, 6.0, ((0, 2),), jnp.float32)
    row_coupling = draw_row_coupling(jax.random.fold_in(key_list[9], 71), 0)
    cross_gain = draw_cross_gain(jax.random.fold_in(key_list[9], 71), 0)
    block_inverse = draw_block_inverse(jax.random.fold_in(key_list[9], 71), 0)
    quadrant = set_ends(jax.random.randint(key_list[5], (SPECTRAL_ANGLES,), 0, 4), jax.random.fold_in(key_list[5], 1), 0, 3).astype(jnp.int32)
    sea_mask = draw_sea_mask(jax.random.fold_in(key_list[9], 71), 0)
    wet_tiles = set_ends((jax.random.randint(key_list[7], (GRID_ROW_TOTAL, NY // BLOCK), 0, 4) < 3).astype(jnp.int32), jax.random.fold_in(key_list[7], 1), 0, 1)
    quad_coef = jnp.clip(jnp.exp(jax.random.uniform(key_list[8], (FREQ,), jnp.float32, math.log(0.05), math.log(0.5))), 0.05, 0.5)
    return dict(previous=previous, boundary=boundary, row_coupling=row_coupling, cross_gain=cross_gain, block_inverse=block_inverse, quadrant=quadrant, sea_mask=sea_mask, wet_tiles=wet_tiles, quad_coef=quad_coef)


highest = lax.Precision.HIGHEST


def higher_band(field):
    return jnp.concatenate([field[:, 1:], jnp.zeros_like(field[:, :1])], axis=1)


def lower_band(field):
    return jnp.concatenate([jnp.zeros_like(field[:, :1]), field[:, :-1]], axis=1)


def quad_terms(center, onward, against, coefficients):
    nonlinear = center * center * (onward + against) - 2.0 * center * onward * against
    return coefficients[None, :, None, None] * nonlinear


def full_source(spectra, coefficients):
    energy = spectra.astype(jnp.float32)
    onward = higher_band(jnp.roll(energy, -SHIFT, axis=0))
    against = lower_band(jnp.roll(energy, SHIFT, axis=0))
    return quad_terms(energy, onward, against, coefficients)


def reference(previous, boundary, row_coupling, cross_gain, block_inverse, quadrant, sea_mask, wet_tiles, quad_coef):
    sea_cells = sea_mask.astype(jnp.float32)

    def sweep_one(members):
        prior, inflow, coupling, gain, inverse, corner = members
        couple = coupling * sea_cells
        forcing = sea_cells[None] * (1.0 - coupling)[None] * prior.astype(jnp.float32)
        rows_first = (couple, jnp.moveaxis(forcing, 1, 0))

        def advance(state_in, member):
            state_out = member[0][None] * state_in + member[1]
            return state_out, state_out

        _, onward = lax.scan(advance, inflow, rows_first)
        _, against = lax.scan(advance, inflow, rows_first, reverse=True)
        swept_rows = jnp.where(corner % 2 == 1, against, onward)
        sideways = corner // 2 == 1
        flipped = jnp.where(sideways, jnp.flip(swept_rows, -1), swept_rows)
        blocks = flipped.reshape(GRID_ROW_TOTAL, FREQ, NY // BLOCK, BLOCK)
        solved = jnp.einsum('ij,xfkj->xfki', inverse, blocks, precision=highest)
        pieces = [solved[:, :, 0]]
        for section in range(1, NY // BLOCK):
            pieces.append(solved[:, :, section] + gain * pieces[-1][..., -1:] * inverse[:, 0])
        settled = jnp.stack(pieces, 2).reshape(GRID_ROW_TOTAL, FREQ, NY)
        settled = jnp.where(sideways, jnp.flip(settled, -1), settled) * sea_cells[:, None, :]
        return jnp.moveaxis(settled, 0, 1)

    settled = lax.map(sweep_one, (previous, boundary, row_coupling, cross_gain, block_inverse, quadrant))
    rounded = lax.optimization_barrier(settled.astype(jnp.bfloat16))
    grouped = jnp.moveaxis(rounded.reshape(SPECTRAL_ANGLES, FREQ, GRID_ROW_TOTAL // CX, CX, NY), 2, 0)
    source = lax.map(lambda row_group: full_source(row_group, quad_coef).astype(jnp.bfloat16), grouped)
    source = jnp.moveaxis(source, 0, 2).reshape(SPECTRAL_ANGLES, FREQ, GRID_ROW_TOTAL, NY)
    source = lax.optimization_barrier(source)
    wet_cells = jnp.repeat(wet_tiles.astype(jnp.float32), BLOCK, axis=1)
    return (settled + wet_cells[None, None] * source.astype(jnp.float32)).astype(jnp.bfloat16)
```

```python
import functools

import jax
import jax.numpy as jnp
from jax import lax
from jax.experimental import pallas as pl
from jax.experimental.pallas import tpu as pltpu
from jax.sharding import PartitionSpec as P

SHIFT = 2
f32 = jnp.float32
bf16 = jnp.bfloat16
MESH = pl.DeviceIdType.MESH
SCAN_VMEM = 56 * 1024 * 1024
STEP_VMEM = 32 * 1024 * 1024
BLOCK = 128


def cost(microseconds):
    return pl.CostEstimate(
        flops=0, bytes_accessed=int(microseconds * 3_000_000), transcendentals=0
    )


def weights(coupling, sea):
    return coupling * sea, sea * (1.0 - coupling)


def visit_order(shape, backward):
    row = lax.broadcasted_iota(jnp.int32, shape, 0)
    return shape[0] - 1 - row if backward else row


def rolled(x, steps, backward):
    rows = x.shape[0]
    return pltpu.roll(x, (rows - steps if backward else steps) % rows, 0)


def row_weights(coupling, sea, backward):
    couple, weight = weights(coupling, sea)
    rows = couple.shape[0]
    order = visit_order(couple.shape, backward)
    after = jnp.where(order < rows - 1, rolled(couple, rows - 1, backward), 1.0)
    span = 1
    while span < rows - 1:
        after = after * jnp.where(order < rows - span, rolled(after, rows - span, backward), 1.0)
        span *= 2
    gain = jnp.sum(jnp.where(order == 0, couple * after, 0.0), axis=0, keepdims=True)
    return weight * after, gain


def scan_kernel(
    count, dir_count, chunks, quadrant, cross_gain, boundary_in, sea_in, previous_in, coupling_in,
    out, edges, halo_previous, halo_coupling, halo_marks,
    gain, state, shares, marks, boundary, sea_mask, previous, coupling,
    gains, got_core, half_total, got_pair, plane, chain_in, chain_out, pair_in, pair_out, core_out,
    load_sem, gain_send, gain_recv, core_send, core_recv, pair_send, pair_recv,
    chain_send, chain_recv, back_send, back_recv, last_send, last_recv, halo_send, halo_recv,
):
    me = lax.axis_index("rows")
    c, x, z = me % 2, (me // 2) % 2, me // 4
    depth = count // 4
    core_peer = me + 1 - 2 * c
    pair_peer = me + 2 - 4 * x
    cross_peer = core_peer + 2 - 4 * x
    dirs = gain.shape[0]
    size = dirs // chunks
    peers = (core_peer, pair_peer, cross_peer)

    def part(j):
        return pl.ds(j * size, size)

    barrier = pltpu.get_barrier_semaphore()
    for peer in peers:
        pl.semaphore_signal(barrier, inc=1, device_id={"rows": peer}, device_id_type=MESH)

    @pl.when(z > 0)
    def _():
        pl.semaphore_signal(barrier, inc=1, device_id={"rows": me - 4}, device_id_type=MESH)

    @pl.when(z < depth - 1)
    def _():
        pl.semaphore_signal(barrier, inc=1, device_id={"rows": me + 4}, device_id_type=MESH)

    mine = lax.axis_index("dirs")
    higher, lower = (mine + 1) % dir_count, (mine + dir_count - 1) % dir_count
    neighbours = (higher, lower) if dir_count > 2 else (higher,)
    for peer in neighbours:
        pl.semaphore_signal(barrier, inc=1, device_id={"dirs": peer}, device_id_type=MESH)

    order = [0] + list(range(chunks - 1, 0, -1))
    coupling_load = pltpu.make_async_copy(coupling_in, coupling, load_sem.at[0])
    sea_load = pltpu.make_async_copy(sea_in, sea_mask, load_sem.at[1])
    boundary_load = pltpu.make_async_copy(boundary_in, boundary, load_sem.at[2])
    previous_loads = [
        pltpu.make_async_copy(previous_in.at[part(j)], previous.at[part(j)], load_sem.at[3 + j])
        for j in range(chunks)
    ]
    sea_load.start()
    coupling_load.start()
    for j in order:
        previous_loads[j].start()
    boundary_load.start()
    for d in range(dirs):
        marks[d, 0:1] = jnp.full((1, marks.shape[2]), cross_gain[d], f32)
        marks[d, 1:2] = jnp.full((1, marks.shape[2]), quadrant[d].astype(f32), f32)
    pl.semaphore_wait(
        barrier, 3 + len(neighbours) + (z > 0).astype(jnp.int32) + (z < depth - 1).astype(jnp.int32)
    )

    def remote(src, dst, send, recv, peer):
        return pltpu.make_async_remote_copy(
            src_ref=src, dst_ref=dst, send_sem=send, recv_sem=recv,
            device_id={"rows": peer}, device_id_type=MESH,
        )

    gain_copies = [
        remote(gain, gains.at[i], gain_send.at[i], gain_recv.at[i], peer) for i, peer in enumerate(peers)
    ]
    core_copies = [
        remote(state.at[1 - c, :, part(j)], got_core.at[:, part(j)], core_send.at[j], core_recv.at[j], core_peer)
        for j in range(chunks)
    ]
    pair_copies = [
        remote(half_total.at[1 - x, part(j)], got_pair.at[part(j)], pair_send.at[j], pair_recv.at[j], pair_peer)
        for j in range(chunks)
    ]
    back_copies = [
        remote(pair_out.at[part(j)], pair_in.at[x, part(j)], back_send.at[j], back_recv.at[j], pair_peer)
        for j in range(chunks)
    ]
    last_copies = [
        remote(core_out.at[:, part(j)], out.at[c, :, part(j)], last_send.at[j], last_recv.at[j], core_peer)
        for j in range(chunks)
    ]

    halo_copies = []
    for way, (peer, start, to) in enumerate(((lower, 0, SHIFT), (higher, dirs - SHIFT, 0))):
        for i, (array, halo) in enumerate(
            ((previous_in, halo_previous), (coupling_in, halo_coupling), (marks, halo_marks))
        ):
            halo_copies.append(
                pltpu.make_async_remote_copy(
                    src_ref=array.at[pl.ds(start, SHIFT)], dst_ref=halo.at[pl.ds(to, SHIFT)],
                    send_sem=halo_send.at[way, i], recv_sem=halo_recv.at[way, i],
                    device_id={"dirs": peer}, device_id_type=MESH,
                )
            )
            halo_copies[-1].start()

    flags = marks[:, 1:2, :]
    flags = flags - 2.0 * jnp.floor(0.5 * flags)
    back = jnp.concatenate([flags] * (gain.shape[-1] // flags.shape[-1]), axis=2)
    sea_load.wait()
    coupling_load.wait()
    sea = sea_mask[...].astype(f32)
    for d in range(dirs):
        onward, onward_gain = row_weights(coupling[d], sea, False)
        against, _ = row_weights(coupling[d], sea, True)
        shares[d] = jnp.where(back[d] > 0.5, against, onward)
        gain[d] = onward_gain
    for copy in gain_copies:
        copy.start()

    def compose(h, d, _):
        share = shares[d]
        for q in range(2):
            values = previous[d, pl.ds((2 * h + q) * state.shape[3], state.shape[3])].astype(f32)
            state[h, q, d] = jnp.sum(values * share[None], axis=1)
        return 0

    for j in order:
        previous_loads[j].wait()
        lax.fori_loop(j * size, (j + 1) * size, functools.partial(compose, 1 - c), 0)
        core_copies[j].start()
    for j in order:
        lax.fori_loop(j * size, (j + 1) * size, functools.partial(compose, c), 0)
    boundary_load.wait()
    c_bit, x_bit = c.astype(f32), x.astype(f32)
    core_after = c_bit + back - 2.0 * c_bit * back
    pair_after = x_bit + back - 2.0 * x_bit * back
    for copy in gain_copies:
        copy.wait_recv()
    core_mine, core_theirs = gain[...], gains[0]
    pair_mine, pair_theirs = core_mine * core_theirs, gains[1] * gains[2]
    plane_gain = pair_mine * pair_theirs

    def total(after, mine, theirs):
        return after * mine + (1.0 - after), (1.0 - after) * theirs + after

    core_a, core_b = total(core_after, core_mine, core_theirs)
    pair_a, pair_b = total(pair_after, pair_mine, pair_theirs)

    def cut(v, j):
        return v[j * size : (j + 1) * size]

    for j in order:
        core_copies[j].wait_recv()
        half_total[:, part(j)] = (
            cut(core_a, j)[None] * got_core[:, part(j)] + cut(core_b, j)[None] * state[c, :, part(j)]
        )
        pair_copies[j].start()
    for j in order:
        pair_copies[j].wait_recv()
        plane[part(j)] = cut(pair_a, j) * got_pair[part(j)] + cut(pair_b, j) * half_total[x, part(j)]

    upper = (2 * z >= depth).astype(jnp.int32)
    mine_at = 2 * c + x

    def chain(j, way):
        step = 1 - 2 * way
        has_before = jnp.where(way == 0, z > 0, z < depth - 1)
        has_after = jnp.where(way == 0, z < depth - 1, z > 0)
        copy = remote(
            chain_out.at[way, part(j)], chain_in.at[way, part(j)],
            chain_send.at[way, j], chain_recv.at[way, j], me + 4 * step,
        )

        @pl.when(has_before)
        def _():
            copy.wait_recv()

        @pl.when(jnp.logical_not(has_before))
        def _():
            chain_in[way, part(j)] = boundary[part(j), mine_at]

        @pl.when(has_after)
        def _():
            chain_out[way, part(j)] = cut(plane_gain, j) * chain_in[way, part(j)] + plane[part(j)]
            copy.start()

    def split(after, mine, theirs):
        return after * theirs + (1.0 - after), (1.0 - after) * mine + after

    pair_p, pair_q = split(pair_after, pair_mine, pair_theirs)
    core_p, core_q = split(core_after, core_mine, core_theirs)
    for j in order:
        chain(j, upper)
    for j in order:
        chain(j, 1 - upper)
        entering = jnp.where(cut(back, j) > 0.5, chain_in[1, part(j)], chain_in[0, part(j)])
        pair_out[part(j)] = cut(pair_q, j) * entering + (1.0 - cut(pair_after, j)) * half_total[x, part(j)]
        back_copies[j].start()
        pair_in[x, part(j)] = cut(pair_p, j) * entering + cut(pair_after, j) * got_pair[part(j)]
    for j in order:
        back_copies[j].wait_recv()
        entering = pair_in[:, part(j)]
        core_out[:, part(j)] = (
            cut(core_q, j)[None] * entering + (1.0 - cut(core_after, j))[None] * state[c, :, part(j)]
        )
        last_copies[j].start()
        out[c, :, part(j)] = cut(core_p, j)[None] * entering + cut(core_after, j)[None] * got_core[:, part(j)]
    for j in order:
        last_copies[j].wait_recv()
    edges[0] = out[:, :, 0:SHIFT]
    edges[1] = out[:, :, dirs - SHIFT : dirs]
    for copy in halo_copies:
        copy.wait_recv()
    for copy in halo_copies + gain_copies + core_copies + pair_copies + back_copies + last_copies:
        copy.wait_send()

    def drain(j, way):
        copy = remote(
            chain_out.at[way, part(j)], chain_in.at[way, part(j)],
            chain_send.at[way, j], chain_recv.at[way, j], me + 4 * (1 - 2 * way),
        )

        @pl.when(z < depth - 1 if way == 0 else z > 0)
        def _():
            copy.wait_send()

    for j in range(chunks):
        drain(j, 0)
        drain(j, 1)


def scan_devices(count, dir_count, quadrant, cross_gain, boundary, sea_mask, previous, coupling):
    dirs, bands, rows, columns = previous.shape
    chunks = 4 if dirs % 4 == 0 else 3 if dirs % 3 == 0 else 1
    quarter = bands // 4
    boundary = boundary.reshape(dirs, 4, quarter, columns)
    vmem = pl.BlockSpec(memory_space=pltpu.VMEM)
    smem = pl.BlockSpec(memory_space=pltpu.SMEM)
    part = (dirs, quarter, columns)
    dma = pltpu.SemaphoreType.DMA
    anywhere = pl.BlockSpec(memory_space=pl.ANY)
    marks = (dirs, 2, 128)

    def halo(a):
        return jax.ShapeDtypeStruct((2 * SHIFT,) + a.shape[1:], a.dtype)

    out, edges, *halos = pl.pallas_call(
        functools.partial(scan_kernel, count, dir_count, chunks),
        in_specs=[smem, smem] + [anywhere] * 4,
        out_specs=[vmem, vmem] + [anywhere] * 3,
        out_shape=[
            jax.ShapeDtypeStruct((2, 2) + part, f32),
            jax.ShapeDtypeStruct((2, 2, 2, SHIFT, quarter, columns), f32),
            halo(previous),
            halo(coupling),
            jax.ShapeDtypeStruct((2 * SHIFT,) + marks[1:], f32),
        ],
        scratch_shapes=[
            pltpu.VMEM((dirs, 1, columns), f32),
            pltpu.VMEM((2, 2) + part, f32),
            pltpu.VMEM(coupling.shape, f32),
            pltpu.VMEM(marks, f32),
            pltpu.VMEM(boundary.shape, f32),
            pltpu.VMEM(sea_mask.shape, jnp.int32),
            pltpu.VMEM(previous.shape, bf16),
            pltpu.VMEM(coupling.shape, f32),
            pltpu.VMEM((3, dirs, 1, columns), f32),
            pltpu.VMEM((2,) + part, f32),
            pltpu.VMEM((2,) + part, f32),
            pltpu.VMEM(part, f32),
            pltpu.VMEM(part, f32),
            pltpu.VMEM((2,) + part, f32),
            pltpu.VMEM((2,) + part, f32),
            pltpu.VMEM((2,) + part, f32),
            pltpu.VMEM(part, f32),
            pltpu.VMEM((2,) + part, f32),
            dma((3 + chunks,)),
            dma((3,)), dma((3,)),
            dma((chunks,)), dma((chunks,)),
            dma((chunks,)), dma((chunks,)),
            dma((2, chunks)), dma((2, chunks)),
            dma((chunks,)), dma((chunks,)),
            dma((chunks,)), dma((chunks,)),
            dma((2, 3)), dma((2, 3)),
        ],
        compiler_params=pltpu.CompilerParams(
            collective_id=0, has_side_effects=True, vmem_limit_bytes=SCAN_VMEM
        ),
        cost_estimate=cost(30),
        name="scan_devices",
    )(quadrant, cross_gain, boundary, sea_mask, previous, coupling)
    return out.reshape(4, dirs, quarter, columns), edges, halos


def sweep(previous, coupling, inflow_of, swept, sea, backward):
    bands = previous.shape[0]
    quarter = bands // 4
    couple, weight = weights(coupling, sea)
    rows = couple.shape[0]
    order = visit_order(couple.shape, backward)
    first = jnp.where(order == 0, couple, 0.0)
    spans, reach, span = [], couple, 1
    while span < rows:
        spans.append((span, jnp.where(order >= span, reach, 0.0)))
        reach = jnp.where(order >= span, reach * rolled(reach, span, backward), reach)
        span *= 2

    def group(q, _):
        inflow = inflow_of(q)
        for r in range(quarter):
            value = weight * previous[q * quarter + r].astype(f32) + first * inflow[r : r + 1]
            for span, factor in spans:
                value = value + factor * rolled(value, span, backward)
            swept[q * quarter + r] = value
        return 0

    lax.fori_loop(0, 4, group, 0)


def columns_solve(gain, sea, swept, rounded, settled, sideways):
    bands, rows, columns = swept.shape
    block = BLOCK
    pieces = columns // block
    gains = jnp.full((1, block), gain, f32)
    slope, scale = jnp.log(gains / (1.0 + gains)), 1.0 / (1.0 + gains)
    row = lax.broadcasted_iota(jnp.int32, (block, block), 0)
    column = lax.broadcasted_iota(jnp.int32, (block, block), 1)
    offset = row - column if sideways else column - row
    matrix = jnp.where(offset >= 0, jnp.exp(offset.astype(f32) * slope) * scale, 0.0)
    carry = gains * (matrix[block - 1 :] if sideways else matrix[:1])
    high = matrix.astype(bf16)
    low = (matrix - high.astype(f32)).astype(bf16)
    whole = jnp.concatenate(
        [
            jnp.concatenate([high, low], axis=1),
            jnp.concatenate([high, jnp.zeros_like(low)], axis=1),
        ],
        axis=0,
    )
    before = None
    for k in range(pieces - 1, -1, -1) if sideways else range(pieces):
        here = slice(k * block, (k + 1) * block)
        x = swept[:, :, here].reshape(bands * rows, block)
        upper = x.astype(bf16)
        lower = (x - upper.astype(f32)).astype(bf16)
        both = jnp.dot(
            jnp.concatenate([upper, lower], axis=1), whole, preferred_element_type=f32
        )
        y = both[:, :block] + both[:, block:]
        if before is not None:
            y = y + (before[:, :1] if sideways else before[:, block - 1 :]) * carry
        before = y
        masked = y.reshape(bands, rows, block) * sea[:, here][None]
        rounded[:, :, here] = masked.astype(bf16)
        if settled is not None:
            settled[:, :, here] = masked


def settle(previous, coupling, inflow_of, corner, gain, sea, swept, rounded, settled):
    for flag in (0, 1):
        pl.when(corner % 2 == flag)(
            functools.partial(sweep, previous, coupling, inflow_of, swept, sea, flag == 1)
        )
    for flag in (0, 1):
        pl.when(corner // 2 == flag)(
            functools.partial(columns_solve, gain, sea, swept, rounded, settled, flag == 1)
        )


def own_kernel(
    quadrant, cross_gain, sea_mask, previous_in, coupling, entering, rounded, settled,
    previous, swept, sea, load_sem,
):
    dirs = previous.shape[0]
    loads = [
        pltpu.make_async_copy(previous_in.at[d], previous.at[d], load_sem.at[d]) for d in range(dirs)
    ]
    for load in loads:
        load.start()
    sea[...] = sea_mask[...].astype(f32)
    for load in loads:
        load.wait()

    def one(d, _):
        settle(
            previous.at[d], coupling[d], lambda q: entering[q, d], quadrant[d], cross_gain[d], sea[...],
            swept, rounded.at[d], settled.at[d],
        )
        return 0

    lax.fori_loop(0, dirs, one, 0)


def settle_own(quadrant, cross_gain, sea_mask, previous, coupling, entering):
    dirs, bands, rows, columns = previous.shape
    vmem = pl.BlockSpec(memory_space=pltpu.VMEM)
    smem = pl.BlockSpec(memory_space=pltpu.SMEM)
    anywhere = pl.BlockSpec(memory_space=pl.ANY)
    return pl.pallas_call(
        own_kernel,
        in_specs=[smem, smem, vmem, anywhere, vmem, vmem],
        out_specs=[vmem, vmem],
        out_shape=[
            jax.ShapeDtypeStruct(previous.shape, bf16),
            jax.ShapeDtypeStruct(previous.shape, f32),
        ],
        scratch_shapes=[
            pltpu.VMEM(previous.shape, bf16),
            pltpu.VMEM((bands, rows, columns), f32),
            pltpu.VMEM((rows, columns), f32),
            pltpu.SemaphoreType.DMA((dirs,)),
        ],
        compiler_params=pltpu.CompilerParams(vmem_limit_bytes=STEP_VMEM),
        cost_estimate=cost(12),
        name="settle_own",
    )(quadrant, cross_gain, sea_mask, previous, coupling, entering)


def source_kernel(
    halo_marks, coef, sea_mask, wet_tiles, halo_previous, halo_coupling, incoming, own, settled,
    out, halo, swept, sea, wet, result, store_sem,
):
    dirs, bands, rows, columns = settled.shape
    pieces = columns // BLOCK
    sea[...] = sea_mask[...].astype(f32)
    for k in range(pieces):
        flag = wet_tiles[:, k : k + 1].astype(f32)
        wet[:, k * BLOCK : (k + 1) * BLOCK] = jnp.broadcast_to(flag, (rows, BLOCK))
    stores = [pltpu.make_async_copy(result.at[d], out.at[d], store_sem.at[d]) for d in range(dirs)]

    def source(d):
        wet_cells = wet[...]
        onward_of = own.at[d + SHIFT] if d + SHIFT < dirs else halo.at[2 * SHIFT + d - dirs]
        against_of = own.at[d - SHIFT] if d >= SHIFT else halo.at[d]

        def one(f, onward, against):
            energy = own[d, f].astype(f32)
            value = coef[f] * (
                energy * energy * (onward + against) - 2.0 * energy * onward * against
            )
            result[d, f] = (settled[d, f] + wet_cells * value.astype(bf16).astype(f32)).astype(bf16)

        def above(f):
            return onward_of[f + 1].astype(f32)

        def below(f):
            return against_of[f - 1].astype(f32)

        nothing = jnp.zeros(wet.shape, f32)
        one(0, above(0), nothing)
        one(bands - 1, nothing, below(bands - 1))

        def body(f, _):
            one(f, above(f), below(f))
            return 0

        lax.fori_loop(1, bands - 1, body, 0, unroll=6 if (bands - 2) % 6 == 0 else 1)
        stores[d].start()

    inner = [d for d in range(dirs) if SHIFT <= d < dirs - SHIFT]
    for d in inner:
        source(d)

    def one_halo(t, _):
        way, at = 1 - t // SHIFT, t % SHIFT
        settle(
            halo_previous.at[t], halo_coupling[t], lambda q: incoming[way, q, at],
            halo_marks[t, 1, 0].astype(jnp.int32), halo_marks[t, 0, 0], sea[...],
            swept, halo.at[t], None,
        )
        return 0

    lax.fori_loop(0, 2 * SHIFT, one_halo, 0)
    for d in range(dirs):
        if d not in inner:
            source(d)
    for store in stores:
        store.wait()


def add_source(
    halo_marks, quad_coef, sea_mask, wet_tiles, halo_previous, halo_coupling, incoming, rounded, settled
):
    dirs, bands, rows, columns = settled.shape
    vmem = pl.BlockSpec(memory_space=pltpu.VMEM)
    smem = pl.BlockSpec(memory_space=pltpu.SMEM)
    return pl.pallas_call(
        source_kernel,
        in_specs=[smem, smem] + [vmem] * 7,
        out_specs=pl.BlockSpec(memory_space=pl.ANY),
        out_shape=jax.ShapeDtypeStruct(settled.shape, bf16),
        scratch_shapes=[
            pltpu.VMEM((2 * SHIFT, bands, rows, columns), bf16),
            pltpu.VMEM((bands, rows, columns), f32),
            pltpu.VMEM((rows, columns), f32),
            pltpu.VMEM((rows, columns), f32),
            pltpu.VMEM(settled.shape, bf16),
            pltpu.SemaphoreType.DMA((dirs,)),
        ],
        compiler_params=pltpu.CompilerParams(vmem_limit_bytes=STEP_VMEM),
        cost_estimate=cost(8),
        name="add_source",
    )(halo_marks, quad_coef, sea_mask, wet_tiles, halo_previous, halo_coupling, incoming, rounded, settled)


def exchange(edges, dir_count):
    if dir_count == 2:
        return lax.ppermute(edges, "dirs", [(0, 1), (1, 0)])
    down = [(i, (i - 1) % dir_count) for i in range(dir_count)]
    up = [(i, (i + 1) % dir_count) for i in range(dir_count)]
    return jnp.stack([lax.ppermute(edges[0], "dirs", down), lax.ppermute(edges[1], "dirs", up)])


def on_device(
    row_devices, dir_devices,
    previous, boundary, row_coupling, cross_gain, block_inverse, quadrant, sea_mask, wet_tiles, quad_coef,
):
    entering, edges, (halo_previous, halo_coupling, halo_marks) = scan_devices(
        row_devices, dir_devices, quadrant, cross_gain, boundary, sea_mask, previous, row_coupling
    )
    incoming = exchange(edges, dir_devices)
    incoming = incoming.reshape((2, 4) + incoming.shape[3:])
    rounded, settled = settle_own(quadrant, cross_gain, sea_mask, previous, row_coupling, entering)
    return add_source(
        halo_marks, quad_coef, sea_mask, wet_tiles, halo_previous, halo_coupling, incoming, rounded, settled
    )


def solution(mesh):
    in_specs = (
        P("dirs", None, "rows", None),
        P("dirs", None, None),
        P("dirs", "rows", None),
        P("dirs"),
        P("dirs", None, None),
        P("dirs"),
        P("rows", None),
        P("rows", None),
        P(),
    )
    out_specs = P("dirs", None, "rows", None)
    return jax.shard_map(
        functools.partial(on_device, mesh.shape["rows"], mesh.shape["dirs"]),
        mesh=mesh, in_specs=in_specs, out_specs=out_specs, check_vma=False,
    )
```

```python
import functools

import jax
import jax.numpy as jnp
from jax import lax
from jax.experimental import pallas as pl
from jax.experimental.pallas import tpu as pltpu
from jax.sharding import PartitionSpec as P

SHIFT = 2
f32 = jnp.float32
bf16 = jnp.bfloat16
MESH = pl.DeviceIdType.MESH
SCAN_VMEM = 56 * 1024 * 1024
STEP_VMEM = 16 * 1024 * 1024
BLOCK = 128


def cost(microseconds):
    return pl.CostEstimate(
        flops=0, bytes_accessed=int(microseconds * 3_000_000), transcendentals=0
    )


def weights(coupling, sea):
    return coupling * sea, sea * (1.0 - coupling)


def visit_order(shape, backward):
    row = lax.broadcasted_iota(jnp.int32, shape, 0)
    return shape[0] - 1 - row if backward else row


def rolled(x, steps, backward):
    rows = x.shape[0]
    return pltpu.roll(x, (rows - steps if backward else steps) % rows, 0)


def row_weights(coupling, sea, backward):
    couple, weight = weights(coupling, sea)
    rows = couple.shape[0]
    order = visit_order(couple.shape, backward)
    after = jnp.where(order < rows - 1, rolled(couple, rows - 1, backward), 1.0)
    span = 1
    while span < rows - 1:
        after = after * jnp.where(order < rows - span, rolled(after, rows - span, backward), 1.0)
        span *= 2
    gain = jnp.sum(jnp.where(order == 0, couple * after, 0.0), axis=0, keepdims=True)
    return weight * after, gain


def scan_kernel(
    count, dir_count, chunks, quadrant, cross_gain, boundary_in, sea_in, previous_in, coupling_in,
    entering_out, edges, halo_previous, halo_marks,
    out,
    gain, state, shares, marks, boundary, sea_mask, previous, coupling,
    gains, got_core, half_total, got_pair, plane, chain_in, chain_out, pair_in, pair_out, core_out,
    load_sem, store_sem, gain_send, gain_recv, core_send, core_recv, pair_send, pair_recv,
    chain_send, chain_recv, back_send, back_recv, last_send, last_recv, halo_send, halo_recv,
):
    me = lax.axis_index("rows")
    c, x, z = me % 2, (me // 2) % 2, me // 4
    depth = count // 4
    half = (c + x + z) % 2
    core_peer = me + 1 - 2 * c
    side_peer = me + 2 - 4 * x
    pair_peer = core_peer + 2 - 4 * x
    dirs = gain.shape[0]
    size = dirs // chunks
    peers = (core_peer, side_peer, pair_peer)

    def part(j):
        return pl.ds(j * size, size)

    barrier = pltpu.get_barrier_semaphore()
    for peer in peers:
        pl.semaphore_signal(barrier, inc=1, device_id={"rows": peer}, device_id_type=MESH)

    @pl.when(z > 0)
    def _():
        pl.semaphore_signal(barrier, inc=1, device_id={"rows": core_peer - 4}, device_id_type=MESH)

    @pl.when(z < depth - 1)
    def _():
        pl.semaphore_signal(barrier, inc=1, device_id={"rows": core_peer + 4}, device_id_type=MESH)

    mine = lax.axis_index("dirs")
    higher, lower = (mine + 1) % dir_count, (mine + dir_count - 1) % dir_count
    neighbours = (higher, lower) if dir_count > 2 else (higher,)
    for peer in neighbours:
        pl.semaphore_signal(barrier, inc=1, device_id={"dirs": peer}, device_id_type=MESH)

    order = [0] + list(range(chunks - 1, 0, -1))
    coupling_load = pltpu.make_async_copy(coupling_in, coupling, load_sem.at[0])
    sea_load = pltpu.make_async_copy(sea_in, sea_mask, load_sem.at[1])
    boundary_load = pltpu.make_async_copy(boundary_in, boundary, load_sem.at[2])
    previous_loads = [
        pltpu.make_async_copy(previous_in.at[part(j)], previous.at[part(j)], load_sem.at[3 + j])
        for j in range(chunks)
    ]
    sea_load.start()
    coupling_load.start()
    for j in order:
        previous_loads[j].start()
    boundary_load.start()
    for d in range(dirs):
        marks[d, 0:1] = jnp.full((1, marks.shape[2]), cross_gain[d], f32)
        marks[d, 1:2] = jnp.full((1, marks.shape[2]), quadrant[d].astype(f32), f32)
    def remote(src, dst, send, recv, peer):
        return pltpu.make_async_remote_copy(
            src_ref=src, dst_ref=dst, send_sem=send, recv_sem=recv,
            device_id={"rows": peer}, device_id_type=MESH,
        )

    gain_copies = [
        remote(gain, gains.at[i], gain_send.at[i], gain_recv.at[i], peer) for i, peer in enumerate(peers)
    ]
    core_copies = [
        remote(state.at[1 - half, :, part(j)], got_core.at[:, part(j)], core_send.at[j], core_recv.at[j], core_peer)
        for j in range(chunks)
    ]
    pair_copies = [
        remote(half_total.at[1 - x, part(j)], got_pair.at[part(j)], pair_send.at[j], pair_recv.at[j], pair_peer)
        for j in range(chunks)
    ]
    back_copies = [
        remote(pair_out.at[part(j)], pair_in.at[x, part(j)], back_send.at[j], back_recv.at[j], pair_peer)
        for j in range(chunks)
    ]
    last_copies = [
        remote(core_out.at[:, part(j)], out.at[half, :, part(j)], last_send.at[j], last_recv.at[j], core_peer)
        for j in range(chunks)
    ]

    flags = marks[:, 1:2, :]
    flags = flags - 2.0 * jnp.floor(0.5 * flags)
    back = jnp.concatenate([flags] * (gain.shape[-1] // flags.shape[-1]), axis=2)
    sea_load.wait()
    coupling_load.wait()
    sea = sea_mask[...].astype(f32)
    for d in range(dirs):
        onward, onward_gain = row_weights(coupling[d], sea, False)
        against, _ = row_weights(coupling[d], sea, True)
        shares[d] = jnp.where(back[d] > 0.5, against, onward)
        gain[d] = onward_gain
    pl.semaphore_wait(
        barrier, 3 + len(neighbours) + (z > 0).astype(jnp.int32) + (z < depth - 1).astype(jnp.int32)
    )

    stores = []

    def keep(src, dst):
        stores.append(pltpu.make_async_copy(src, dst, store_sem.at[len(stores)]))
        stores[-1].start()

    halo_copies = []
    for way, (peer, start, to) in enumerate(((lower, 0, SHIFT), (higher, dirs - SHIFT, 0))):
        bands = pl.ds(1 - way, previous.shape[1] - 1)
        for i, (src, dst) in enumerate(
            (
                (previous_in.at[pl.ds(start, SHIFT), bands], halo_previous.at[pl.ds(to, SHIFT), bands]),
                (marks.at[pl.ds(start, SHIFT)], halo_marks.at[pl.ds(to, SHIFT)]),
            )
        ):
            halo_copies.append(
                pltpu.make_async_remote_copy(
                    src_ref=src, dst_ref=dst,
                    send_sem=halo_send.at[way, i], recv_sem=halo_recv.at[way, i],
                    device_id={"dirs": peer}, device_id_type=MESH,
                )
            )
            halo_copies[-1].start()

    for copy in gain_copies:
        copy.start()
    for way, start in enumerate((0, dirs - SHIFT)):
        keep(coupling.at[pl.ds(start, SHIFT)], edges.at[way, 4])

    def compose(h, d, _):
        share = shares[d]
        for q in range(2):
            values = previous[d, pl.ds((2 * h + q) * state.shape[3], state.shape[3])].astype(f32)
            state[h, q, d] = jnp.sum(values * share[None], axis=1)
        return 0

    for j in order:
        previous_loads[j].wait()
        lax.fori_loop(j * size, (j + 1) * size, functools.partial(compose, 1 - half), 0)
        core_copies[j].start()
    for j in order:
        lax.fori_loop(j * size, (j + 1) * size, functools.partial(compose, half), 0)
    boundary_load.wait()
    c_bit, x_bit = c.astype(f32), x.astype(f32)
    core_after = c_bit + back - 2.0 * c_bit * back
    pair_after = x_bit + back - 2.0 * x_bit * back
    for copy in gain_copies:
        copy.wait_recv()
    core_mine, core_theirs = gain[...], gains[0]
    pair_mine, pair_theirs = core_mine * core_theirs, gains[1] * gains[2]
    plane_gain = pair_mine * pair_theirs

    def total(after, mine, theirs):
        return after * mine + (1.0 - after), (1.0 - after) * theirs + after

    core_a, core_b = total(core_after, core_mine, core_theirs)
    pair_a, pair_b = total(pair_after, pair_mine, pair_theirs)

    def cut(v, j):
        return v[j * size : (j + 1) * size]

    for j in order:
        core_copies[j].wait_recv()
        half_total[:, part(j)] = (
            cut(core_a, j)[None] * got_core[:, part(j)] + cut(core_b, j)[None] * state[half, :, part(j)]
        )
        pair_copies[j].start()
    upper = (2 * z >= depth).astype(jnp.int32)
    mine_at = 2 * half + x

    def chain(j, way):
        step = 1 - 2 * way
        has_before = jnp.where(way == 0, z > 0, z < depth - 1)
        has_after = jnp.where(way == 0, z < depth - 1, z > 0)
        copy = remote(
            chain_out.at[way, part(j)], chain_in.at[way, part(j)],
            chain_send.at[way, j], chain_recv.at[way, j], core_peer + 4 * step,
        )

        @pl.when(has_before)
        def _():
            copy.wait_recv()

        @pl.when(jnp.logical_not(has_before))
        def _():
            chain_in[way, part(j)] = boundary[part(j), mine_at]

        @pl.when(has_after)
        def _():
            chain_out[way, part(j)] = cut(plane_gain, j) * chain_in[way, part(j)] + plane[part(j)]
            copy.start()

    def split(after, mine, theirs):
        return after * theirs + (1.0 - after), (1.0 - after) * mine + after

    pair_p, pair_q = split(pair_after, pair_mine, pair_theirs)
    core_p, core_q = split(core_after, core_mine, core_theirs)

    def leave(j):
        entering = jnp.where(cut(back, j) > 0.5, chain_in[1, part(j)], chain_in[0, part(j)])
        pair_out[part(j)] = cut(pair_q, j) * entering + (1.0 - cut(pair_after, j)) * half_total[x, part(j)]
        back_copies[j].start()
        pair_in[x, part(j)] = cut(pair_p, j) * entering + cut(pair_after, j) * got_pair[part(j)]

    def finish(j):
        back_copies[j].wait_recv()
        entering = pair_in[:, part(j)]
        core_out[:, part(j)] = (
            cut(core_q, j)[None] * entering + (1.0 - cut(core_after, j))[None] * state[half, :, part(j)]
        )
        last_copies[j].start()
        out[half, :, part(j)] = cut(core_p, j)[None] * entering + cut(core_after, j)[None] * got_core[:, part(j)]

    for i in range(2 * chunks + 1):
        if i < chunks:
            j = order[i]
            pair_copies[j].wait_recv()
            plane[part(j)] = cut(pair_a, j) * got_pair[part(j)] + cut(pair_b, j) * half_total[x, part(j)]
            chain(j, upper)
        if chunks <= i < 2 * chunks:
            chain(order[i - chunks], 1 - upper)
            leave(order[i - chunks])
        if chunks < i:
            finish(order[i - chunks - 1])
    for j in order:
        last_copies[j].wait_recv()
        keep(out.at[:, :, part(j)], entering_out.at[:, :, part(j)])
        for way, (at, start) in enumerate(((0, 0), (chunks - 1, dirs - SHIFT))):
            if j == at:
                for h in range(2):
                    keep(out.at[h, :, pl.ds(start, SHIFT)], edges.at[way, pl.ds(2 * h, 2)])
    for copy in halo_copies:
        copy.wait_recv()
    for store in stores:
        store.wait()
    for copy in halo_copies + gain_copies + core_copies + pair_copies + back_copies + last_copies:
        copy.wait_send()

    def drain(j, way):
        copy = remote(
            chain_out.at[way, part(j)], chain_in.at[way, part(j)],
            chain_send.at[way, j], chain_recv.at[way, j], core_peer + 4 * (1 - 2 * way),
        )

        @pl.when(z < depth - 1 if way == 0 else z > 0)
        def _():
            copy.wait_send()

    for j in range(chunks):
        drain(j, 0)
        drain(j, 1)


def scan_devices(count, dir_count, quadrant, cross_gain, boundary, sea_mask, previous, coupling):
    dirs, bands, rows, columns = previous.shape
    chunks = 4 if dirs % 4 == 0 else 3 if dirs % 3 == 0 else 1
    quarter = bands // 4
    boundary = boundary.reshape(dirs, 4, quarter, columns)
    vmem = pl.BlockSpec(memory_space=pltpu.VMEM)
    smem = pl.BlockSpec(memory_space=pltpu.SMEM)
    part = (dirs, quarter, columns)
    dma = pltpu.SemaphoreType.DMA
    anywhere = pl.BlockSpec(memory_space=pl.ANY)
    marks = (dirs, 2, 128)

    def halo(a):
        return jax.ShapeDtypeStruct((2 * SHIFT,) + a.shape[1:], a.dtype)

    out, edges, *halos = pl.pallas_call(
        functools.partial(scan_kernel, count, dir_count, chunks),
        in_specs=[smem, smem] + [anywhere] * 4,
        out_specs=[anywhere] * 4,
        out_shape=[
            jax.ShapeDtypeStruct((2, 2) + part, f32),
            jax.ShapeDtypeStruct((2, 5, SHIFT, quarter, columns), f32),
            halo(previous),
            jax.ShapeDtypeStruct((2 * SHIFT,) + marks[1:], f32),
        ],
        scratch_shapes=[
            pltpu.VMEM((2, 2) + part, f32),
            pltpu.VMEM((dirs, 1, columns), f32),
            pltpu.VMEM((2, 2) + part, f32),
            pltpu.VMEM(coupling.shape, f32),
            pltpu.VMEM(marks, f32),
            pltpu.VMEM(boundary.shape, f32),
            pltpu.VMEM(sea_mask.shape, jnp.int32),
            pltpu.VMEM(previous.shape, bf16),
            pltpu.VMEM(coupling.shape, f32),
            pltpu.VMEM((3, dirs, 1, columns), f32),
            pltpu.VMEM((2,) + part, f32),
            pltpu.VMEM((2,) + part, f32),
            pltpu.VMEM(part, f32),
            pltpu.VMEM(part, f32),
            pltpu.VMEM((2,) + part, f32),
            pltpu.VMEM((2,) + part, f32),
            pltpu.VMEM((2,) + part, f32),
            pltpu.VMEM(part, f32),
            pltpu.VMEM((2,) + part, f32),
            dma((3 + chunks,)),
            dma((6 + chunks,)),
            dma((3,)), dma((3,)),
            dma((chunks,)), dma((chunks,)),
            dma((chunks,)), dma((chunks,)),
            dma((2, chunks)), dma((2, chunks)),
            dma((chunks,)), dma((chunks,)),
            dma((chunks,)), dma((chunks,)),
            dma((2, 2)), dma((2, 2)),
        ],
        compiler_params=pltpu.CompilerParams(
            collective_id=0, has_side_effects=True, vmem_limit_bytes=SCAN_VMEM
        ),
        cost_estimate=cost(30),
        name="scan_devices",
    )(quadrant, cross_gain, boundary, sea_mask, previous, coupling)
    return out.reshape(4, dirs, quarter, columns), edges, halos


def sweep(previous, coupling, inflow_of, swept, sea, backward):
    bands = previous.shape[0]
    quarter = bands // 4
    couple, weight = weights(coupling, sea)
    rows = couple.shape[0]
    order = visit_order(couple.shape, backward)
    first = jnp.where(order == 0, couple, 0.0)
    spans, reach, span = [], couple, 1
    while span < rows:
        spans.append((span, jnp.where(order >= span, reach, 0.0)))
        reach = jnp.where(order >= span, reach * rolled(reach, span, backward), reach)
        span *= 2

    def group(q, _):
        inflow = inflow_of(q)
        for r in range(quarter):
            value = weight * previous[q * quarter + r].astype(f32) + first * inflow[r : r + 1]
            for span, factor in spans:
                value = value + factor * rolled(value, span, backward)
            swept[q * quarter + r] = value
        return 0

    for q in range(4):
        group(q, 0)


def columns_solve(gain, sea, swept, rounded, settled, sideways):
    bands, rows, columns = swept.shape
    block = BLOCK
    pieces = columns // block
    gains = jnp.full((1, block), gain, f32)
    slope, scale = jnp.log(gains / (1.0 + gains)), 1.0 / (1.0 + gains)
    row = lax.broadcasted_iota(jnp.int32, (block, block), 0)
    column = lax.broadcasted_iota(jnp.int32, (block, block), 1)
    offset = row - column if sideways else column - row
    matrix = jnp.where(offset >= 0, jnp.exp(offset.astype(f32) * slope) * scale, 0.0)
    carry = gains * (matrix[block - 1 :] if sideways else matrix[:1])
    carry_last = carry[:, :1] if sideways else carry[:, block - 1 :]
    high = matrix.astype(bf16)
    low = (matrix - high.astype(f32)).astype(bf16)
    whole = jnp.concatenate(
        [
            jnp.concatenate([high, low], axis=1),
            jnp.concatenate([high, jnp.zeros_like(low)], axis=1),
        ],
        axis=0,
    )
    before = None
    for k in range(pieces - 1, -1, -1) if sideways else range(pieces):
        here = slice(k * block, (k + 1) * block)
        x = swept[:, :, here].reshape(bands * rows, block)
        upper = x.astype(bf16)
        lower = (x - upper.astype(f32)).astype(bf16)
        both = jnp.dot(
            jnp.concatenate([upper, lower], axis=1), whole, preferred_element_type=f32
        )
        y = both[:, :block] + both[:, block:]
        last = jnp.broadcast_to(y[:, :1] if sideways else y[:, block - 1 :], y.shape)
        if before is not None:
            y = y + before * carry
            last = last + before * carry_last
        before = last
        masked = y.reshape(bands, rows, block) * sea[:, here][None]
        rounded[:, :, here] = masked.astype(bf16)
        if settled is not None:
            settled[:, :, here] = masked


def settle(previous, coupling, inflow_of, corner, gain, sea, swept, rounded, settled):
    for flag in (0, 1):
        pl.when(corner % 2 == flag)(
            functools.partial(sweep, previous, coupling, inflow_of, swept, sea, flag == 1)
        )
    for flag in (0, 1):
        pl.when(corner // 2 == flag)(
            functools.partial(columns_solve, gain, sea, swept, rounded, settled, flag == 1)
        )


def own_kernel(
    quadrant, cross_gain, sea_mask, previous, coupling, entering, rounded, settled, swept, sea,
):
    sea[...] = sea_mask[...].astype(f32)

    def one(d, _):
        settle(
            previous.at[d], coupling[d], lambda q: entering[q, d], quadrant[d], cross_gain[d], sea[...],
            swept, rounded.at[d], settled.at[d],
        )
        return 0

    lax.fori_loop(0, previous.shape[0], one, 0)


def settle_own(quadrant, cross_gain, sea_mask, previous, coupling, entering):
    dirs, bands, rows, columns = previous.shape
    vmem = pl.BlockSpec(memory_space=pltpu.VMEM)
    smem = pl.BlockSpec(memory_space=pltpu.SMEM)
    return pl.pallas_call(
        own_kernel,
        in_specs=[smem, smem] + [vmem] * 4,
        out_specs=[vmem, vmem],
        out_shape=[
            jax.ShapeDtypeStruct(previous.shape, bf16),
            jax.ShapeDtypeStruct(previous.shape, f32),
        ],
        scratch_shapes=[
            pltpu.VMEM((bands, rows, columns), f32),
            pltpu.VMEM((rows, columns), f32),
        ],
        compiler_params=pltpu.CompilerParams(vmem_limit_bytes=STEP_VMEM),
        cost_estimate=cost(12),
        name="settle_own",
    )(quadrant, cross_gain, sea_mask, previous, coupling, entering)


def source_kernel(
    halo_marks, coef, sea_mask, wet_tiles, halo_previous, incoming_in, own, settled,
    out, halo, incoming, swept, sea, wet, result, load_sem, store_sem,
):
    dirs, bands, rows, columns = settled.shape
    pieces = columns // BLOCK
    load = pltpu.make_async_copy(incoming_in, incoming, load_sem.at[0])
    load.start()
    sea[...] = sea_mask[...].astype(f32)
    for k in range(pieces):
        flag = wet_tiles[:, k : k + 1].astype(f32)
        wet[:, k * BLOCK : (k + 1) * BLOCK] = jnp.broadcast_to(flag, (rows, BLOCK))
    stores = [pltpu.make_async_copy(result.at[d], out.at[d], store_sem.at[d]) for d in range(dirs)]

    def source(d):
        wet_cells = wet[...]
        onward_of = own.at[d + SHIFT] if d + SHIFT < dirs else halo.at[2 * SHIFT + d - dirs]
        against_of = own.at[d - SHIFT] if d >= SHIFT else halo.at[d]

        def one(f, onward, against):
            energy = own[d, f].astype(f32)
            value = coef[f] * (
                energy * energy * (onward + against) - 2.0 * energy * onward * against
            )
            result[d, f] = (settled[d, f] + wet_cells * value.astype(bf16).astype(f32)).astype(bf16)

        def above(f):
            return onward_of[f + 1].astype(f32)

        def below(f):
            return against_of[f - 1].astype(f32)

        nothing = jnp.zeros(wet.shape, f32)
        one(0, above(0), nothing)
        one(bands - 1, nothing, below(bands - 1))

        def body(f, _):
            one(f, above(f), below(f))
            return 0

        lax.fori_loop(1, bands - 1, body, 0, unroll=True)
        stores[d].start()

    inner = [d for d in range(dirs) if SHIFT <= d < dirs - SHIFT]
    for d in inner:
        source(d)

    def one_halo(t, _):
        way, at = 1 - t // SHIFT, t % SHIFT
        settle(
            halo_previous.at[t], incoming[way, 4, at], lambda q: incoming[way, q, at],
            halo_marks[t, 1, 0].astype(jnp.int32), halo_marks[t, 0, 0], sea[...],
            swept, halo.at[t], None,
        )
        return 0

    load.wait()
    lax.fori_loop(0, 2 * SHIFT, one_halo, 0)
    for d in range(dirs):
        if d not in inner:
            source(d)
    for store in stores:
        store.wait()


def add_source(
    halo_marks, quad_coef, sea_mask, wet_tiles, halo_previous, incoming, rounded, settled
):
    dirs, bands, rows, columns = settled.shape
    vmem = pl.BlockSpec(memory_space=pltpu.VMEM)
    smem = pl.BlockSpec(memory_space=pltpu.SMEM)
    return pl.pallas_call(
        source_kernel,
        in_specs=[smem, smem, vmem, vmem, vmem, pl.BlockSpec(memory_space=pl.ANY), vmem, vmem],
        out_specs=pl.BlockSpec(memory_space=pl.ANY),
        out_shape=jax.ShapeDtypeStruct(settled.shape, bf16),
        scratch_shapes=[
            pltpu.VMEM((2 * SHIFT, bands, rows, columns), bf16),
            pltpu.VMEM(incoming.shape, f32),
            pltpu.VMEM((bands, rows, columns), f32),
            pltpu.VMEM((rows, columns), f32),
            pltpu.VMEM((rows, columns), f32),
            pltpu.VMEM(settled.shape, bf16),
            pltpu.SemaphoreType.DMA((1,)),
            pltpu.SemaphoreType.DMA((dirs,)),
        ],
        compiler_params=pltpu.CompilerParams(vmem_limit_bytes=STEP_VMEM),
        cost_estimate=cost(8),
        name="add_source",
    )(halo_marks, quad_coef, sea_mask, wet_tiles, halo_previous, incoming, rounded, settled)


def exchange(edges, dir_count):
    if dir_count == 2:
        return lax.ppermute(edges, "dirs", [(0, 1), (1, 0)])
    down = [(i, (i - 1) % dir_count) for i in range(dir_count)]
    up = [(i, (i + 1) % dir_count) for i in range(dir_count)]
    return jnp.stack([lax.ppermute(edges[0], "dirs", down), lax.ppermute(edges[1], "dirs", up)])


def on_device(
    row_devices, dir_devices,
    previous, boundary, row_coupling, cross_gain, block_inverse, quadrant, sea_mask, wet_tiles, quad_coef,
):
    entering, edges, (halo_previous, halo_marks) = scan_devices(
        row_devices, dir_devices, quadrant, cross_gain, boundary, sea_mask, previous, row_coupling
    )
    incoming = exchange(edges, dir_devices)
    rounded, settled = settle_own(quadrant, cross_gain, sea_mask, previous, row_coupling, entering)
    return add_source(
        halo_marks, quad_coef, sea_mask, wet_tiles, halo_previous, incoming, rounded, settled
    )


def solution(mesh):
    in_specs = (
        P("dirs", None, "rows", None),
        P("dirs", None, None),
        P("dirs", "rows", None),
        P("dirs"),
        P("dirs", None, None),
        P("dirs"),
        P("rows", None),
        P("rows", None),
        P(),
    )
    out_specs = P("dirs", None, "rows", None)
    return jax.shard_map(
        functools.partial(on_device, mesh.shape["rows"], mesh.shape["dirs"]),
        mesh=mesh, in_specs=in_specs, out_specs=out_specs, check_vma=False,
    )
```

```python
import functools

import jax
import jax.numpy as jnp
from jax import lax
from jax.experimental import pallas as pl
from jax.experimental.pallas import tpu as pltpu
from jax.sharding import PartitionSpec as P

SHIFT = 2
f32 = jnp.float32
bf16 = jnp.bfloat16
MESH = pl.DeviceIdType.MESH
SCAN_VMEM = 56 * 1024 * 1024
STEP_VMEM = 16 * 1024 * 1024
BLOCK = 128


def cost(microseconds):
    return pl.CostEstimate(
        flops=0, bytes_accessed=int(microseconds * 3_000_000), transcendentals=0
    )


def weights(coupling, sea):
    return coupling * sea, sea * (1.0 - coupling)


def visit_order(shape, backward):
    row = lax.broadcasted_iota(jnp.int32, shape, 0)
    return shape[0] - 1 - row if backward else row


def rolled(x, steps, backward):
    rows = x.shape[0]
    return pltpu.roll(x, (rows - steps if backward else steps) % rows, 0)


def row_weights(coupling, sea, backward):
    couple, weight = weights(coupling, sea)
    rows = couple.shape[0]
    order = visit_order(couple.shape, backward)
    after = jnp.where(order < rows - 1, rolled(couple, rows - 1, backward), 1.0)
    span = 1
    while span < rows - 1:
        after = after * jnp.where(order < rows - span, rolled(after, rows - span, backward), 1.0)
        span *= 2
    gain = jnp.sum(jnp.where(order == 0, couple * after, 0.0), axis=0, keepdims=True)
    return weight * after, gain


def scan_kernel(
    count, dir_count, chunks, quadrant, cross_gain, boundary_in, sea_in, previous_in, coupling_in,
    entering_out, edges, halo_previous, halo_marks,
    out,
    gain, state, shares, marks, boundary, sea_mask, previous, coupling,
    gains, got_core, half_total, got_pair, plane, chain_in, chain_out, pair_in, pair_out, core_out,
    load_sem, store_sem, gain_send, gain_recv, core_send, core_recv, pair_send, pair_recv,
    chain_send, chain_recv, back_send, back_recv, last_send, last_recv, halo_send, halo_recv,
):
    me = lax.axis_index("rows")
    c, x, z = me % 2, (me // 2) % 2, me // 4
    depth = count // 4
    half = (c + x + z) % 2
    core_peer = me + 1 - 2 * c
    side_peer = me + 2 - 4 * x
    pair_peer = core_peer + 2 - 4 * x
    dirs = gain.shape[0]
    size = dirs // chunks
    peers = (core_peer, side_peer, pair_peer)

    def part(j):
        return pl.ds(j * size, size)

    barrier = pltpu.get_barrier_semaphore()
    for peer in peers:
        pl.semaphore_signal(barrier, inc=1, device_id={"rows": peer}, device_id_type=MESH)

    @pl.when(z > 0)
    def _():
        pl.semaphore_signal(barrier, inc=1, device_id={"rows": core_peer - 4}, device_id_type=MESH)

    @pl.when(z < depth - 1)
    def _():
        pl.semaphore_signal(barrier, inc=1, device_id={"rows": core_peer + 4}, device_id_type=MESH)

    mine = lax.axis_index("dirs")
    higher, lower = (mine + 1) % dir_count, (mine + dir_count - 1) % dir_count
    neighbours = (higher, lower) if dir_count > 2 else (higher,)
    for peer in neighbours:
        pl.semaphore_signal(barrier, inc=1, device_id={"dirs": peer}, device_id_type=MESH)

    order = [0] + list(range(chunks - 1, 0, -1))
    coupling_load = pltpu.make_async_copy(coupling_in, coupling, load_sem.at[0])
    sea_load = pltpu.make_async_copy(sea_in, sea_mask, load_sem.at[1])
    boundary_load = pltpu.make_async_copy(boundary_in, boundary, load_sem.at[2])
    previous_loads = [
        pltpu.make_async_copy(previous_in.at[part(j)], previous.at[part(j)], load_sem.at[3 + j])
        for j in range(chunks)
    ]
    sea_load.start()
    coupling_load.start()
    for j in order:
        previous_loads[j].start()
    boundary_load.start()
    for d in range(dirs):
        marks[d, 0:1] = jnp.full((1, marks.shape[2]), cross_gain[d], f32)
        marks[d, 1:2] = jnp.full((1, marks.shape[2]), quadrant[d].astype(f32), f32)
    def remote(src, dst, send, recv, peer):
        return pltpu.make_async_remote_copy(
            src_ref=src, dst_ref=dst, send_sem=send, recv_sem=recv,
            device_id={"rows": peer}, device_id_type=MESH,
        )

    gain_copies = [
        remote(gain, gains.at[i], gain_send.at[i], gain_recv.at[i], peer) for i, peer in enumerate(peers)
    ]
    core_copies = [
        remote(state.at[1 - half, :, part(j)], got_core.at[:, part(j)], core_send.at[j], core_recv.at[j], core_peer)
        for j in range(chunks)
    ]
    pair_copies = [
        remote(half_total.at[1 - x, part(j)], got_pair.at[part(j)], pair_send.at[j], pair_recv.at[j], pair_peer)
        for j in range(chunks)
    ]
    back_copies = [
        remote(pair_out.at[part(j)], pair_in.at[x, part(j)], back_send.at[j], back_recv.at[j], pair_peer)
        for j in range(chunks)
    ]
    last_copies = [
        remote(core_out.at[:, part(j)], out.at[half, :, part(j)], last_send.at[j], last_recv.at[j], core_peer)
        for j in range(chunks)
    ]

    flags = marks[:, 1:2, :]
    flags = flags - 2.0 * jnp.floor(0.5 * flags)
    back = jnp.concatenate([flags] * (gain.shape[-1] // flags.shape[-1]), axis=2)
    sea_load.wait()
    coupling_load.wait()
    sea = sea_mask[...].astype(f32)
    for d in range(dirs):
        onward, onward_gain = row_weights(coupling[d], sea, False)
        against, _ = row_weights(coupling[d], sea, True)
        shares[d] = jnp.where(back[d] > 0.5, against, onward)
        gain[d] = onward_gain
    pl.semaphore_wait(
        barrier, 3 + len(neighbours) + (z > 0).astype(jnp.int32) + (z < depth - 1).astype(jnp.int32)
    )

    stores = []

    def keep(src, dst):
        stores.append(pltpu.make_async_copy(src, dst, store_sem.at[len(stores)]))
        stores[-1].start()

    halo_copies = []
    for way, (peer, start, to) in enumerate(((lower, 0, SHIFT), (higher, dirs - SHIFT, 0))):
        bands = pl.ds(1 - way, previous.shape[1] - 1)
        for i, (src, dst) in enumerate(
            (
                (previous_in.at[pl.ds(start, SHIFT), bands], halo_previous.at[pl.ds(to, SHIFT), bands]),
                (marks.at[pl.ds(start, SHIFT)], halo_marks.at[pl.ds(to, SHIFT)]),
            )
        ):
            halo_copies.append(
                pltpu.make_async_remote_copy(
                    src_ref=src, dst_ref=dst,
                    send_sem=halo_send.at[way, i], recv_sem=halo_recv.at[way, i],
                    device_id={"dirs": peer}, device_id_type=MESH,
                )
            )
            halo_copies[-1].start()

    for copy in gain_copies:
        copy.start()
    for way, start in enumerate((0, dirs - SHIFT)):
        keep(coupling.at[pl.ds(start, SHIFT)], edges.at[way, 4])

    def compose(h, d, _):
        share = shares[d]
        for q in range(2):
            values = previous[d, pl.ds((2 * h + q) * state.shape[3], state.shape[3])].astype(f32)
            state[h, q, d] = jnp.sum(values * share[None], axis=1)
        return 0

    for j in order:
        previous_loads[j].wait()
        lax.fori_loop(j * size, (j + 1) * size, functools.partial(compose, 1 - half), 0)
        core_copies[j].start()
    for j in order:
        lax.fori_loop(j * size, (j + 1) * size, functools.partial(compose, half), 0)
    boundary_load.wait()
    c_bit, x_bit = c.astype(f32), x.astype(f32)
    core_after = c_bit + back - 2.0 * c_bit * back
    pair_after = x_bit + back - 2.0 * x_bit * back
    for copy in gain_copies:
        copy.wait_recv()
    core_mine, core_theirs = gain[...], gains[0]
    pair_mine, pair_theirs = core_mine * core_theirs, gains[1] * gains[2]
    plane_gain = pair_mine * pair_theirs

    def total(after, mine, theirs):
        return after * mine + (1.0 - after), (1.0 - after) * theirs + after

    core_a, core_b = total(core_after, core_mine, core_theirs)
    pair_a, pair_b = total(pair_after, pair_mine, pair_theirs)

    def cut(v, j):
        return v[j * size : (j + 1) * size]

    for j in order:
        core_copies[j].wait_recv()
        half_total[:, part(j)] = (
            cut(core_a, j)[None] * got_core[:, part(j)] + cut(core_b, j)[None] * state[half, :, part(j)]
        )
        pair_copies[j].start()
    upper = (2 * z >= depth).astype(jnp.int32)
    mine_at = 2 * half + x

    def chain(j, way):
        step = 1 - 2 * way
        has_before = jnp.where(way == 0, z > 0, z < depth - 1)
        has_after = jnp.where(way == 0, z < depth - 1, z > 0)
        copy = remote(
            chain_out.at[way, part(j)], chain_in.at[way, part(j)],
            chain_send.at[way, j], chain_recv.at[way, j], core_peer + 4 * step,
        )

        @pl.when(has_before)
        def _():
            copy.wait_recv()

        @pl.when(jnp.logical_not(has_before))
        def _():
            chain_in[way, part(j)] = boundary[part(j), mine_at]

        @pl.when(has_after)
        def _():
            chain_out[way, part(j)] = cut(plane_gain, j) * chain_in[way, part(j)] + plane[part(j)]
            copy.start()

    def split(after, mine, theirs):
        return after * theirs + (1.0 - after), (1.0 - after) * mine + after

    pair_p, pair_q = split(pair_after, pair_mine, pair_theirs)
    core_p, core_q = split(core_after, core_mine, core_theirs)

    def leave(j):
        entering = jnp.where(cut(back, j) > 0.5, chain_in[1, part(j)], chain_in[0, part(j)])
        pair_out[part(j)] = cut(pair_q, j) * entering + (1.0 - cut(pair_after, j)) * half_total[x, part(j)]
        back_copies[j].start()
        pair_in[x, part(j)] = cut(pair_p, j) * entering + cut(pair_after, j) * got_pair[part(j)]

    def finish(j):
        back_copies[j].wait_recv()
        entering = pair_in[:, part(j)]
        core_out[:, part(j)] = (
            cut(core_q, j)[None] * entering + (1.0 - cut(core_after, j))[None] * state[half, :, part(j)]
        )
        last_copies[j].start()
        out[half, :, part(j)] = cut(core_p, j)[None] * entering + cut(core_after, j)[None] * got_core[:, part(j)]

    for i in range(2 * chunks + 1):
        if i < chunks:
            j = order[i]
            pair_copies[j].wait_recv()
            plane[part(j)] = cut(pair_a, j) * got_pair[part(j)] + cut(pair_b, j) * half_total[x, part(j)]
            chain(j, upper)
        if chunks <= i < 2 * chunks:
            chain(order[i - chunks], 1 - upper)
            leave(order[i - chunks])
        if chunks < i:
            finish(order[i - chunks - 1])
    for j in order:
        last_copies[j].wait_recv()
        keep(out.at[:, :, part(j)], entering_out.at[:, :, part(j)])
        for way, (at, start) in enumerate(((0, 0), (chunks - 1, dirs - SHIFT))):
            if j == at:
                for h in range(2):
                    keep(out.at[h, :, pl.ds(start, SHIFT)], edges.at[way, pl.ds(2 * h, 2)])
    for copy in halo_copies:
        copy.wait_recv()
    for store in stores:
        store.wait()
    for copy in halo_copies + gain_copies + core_copies + pair_copies + back_copies + last_copies:
        copy.wait_send()

    def drain(j, way):
        copy = remote(
            chain_out.at[way, part(j)], chain_in.at[way, part(j)],
            chain_send.at[way, j], chain_recv.at[way, j], core_peer + 4 * (1 - 2 * way),
        )

        @pl.when(z < depth - 1 if way == 0 else z > 0)
        def _():
            copy.wait_send()

    for j in range(chunks):
        drain(j, 0)
        drain(j, 1)


def scan_devices(count, dir_count, quadrant, cross_gain, boundary, sea_mask, previous, coupling):
    dirs, bands, rows, columns = previous.shape
    chunks = 4 if dirs % 4 == 0 else 3 if dirs % 3 == 0 else 1
    quarter = bands // 4
    boundary = boundary.reshape(dirs, 4, quarter, columns)
    vmem = pl.BlockSpec(memory_space=pltpu.VMEM)
    smem = pl.BlockSpec(memory_space=pltpu.SMEM)
    part = (dirs, quarter, columns)
    dma = pltpu.SemaphoreType.DMA
    anywhere = pl.BlockSpec(memory_space=pl.ANY)
    marks = (dirs, 2, 128)

    def halo(a):
        return jax.ShapeDtypeStruct((2 * SHIFT,) + a.shape[1:], a.dtype)

    out, edges, *halos = pl.pallas_call(
        functools.partial(scan_kernel, count, dir_count, chunks),
        in_specs=[smem, smem] + [anywhere] * 4,
        out_specs=[anywhere] * 4,
        out_shape=[
            jax.ShapeDtypeStruct((2, 2) + part, f32),
            jax.ShapeDtypeStruct((2, 5, SHIFT, quarter, columns), f32),
            halo(previous),
            jax.ShapeDtypeStruct((2 * SHIFT,) + marks[1:], f32),
        ],
        scratch_shapes=[
            pltpu.VMEM((2, 2) + part, f32),
            pltpu.VMEM((dirs, 1, columns), f32),
            pltpu.VMEM((2, 2) + part, f32),
            pltpu.VMEM(coupling.shape, f32),
            pltpu.VMEM(marks, f32),
            pltpu.VMEM(boundary.shape, f32),
            pltpu.VMEM(sea_mask.shape, jnp.int32),
            pltpu.VMEM(previous.shape, bf16),
            pltpu.VMEM(coupling.shape, f32),
            pltpu.VMEM((3, dirs, 1, columns), f32),
            pltpu.VMEM((2,) + part, f32),
            pltpu.VMEM((2,) + part, f32),
            pltpu.VMEM(part, f32),
            pltpu.VMEM(part, f32),
            pltpu.VMEM((2,) + part, f32),
            pltpu.VMEM((2,) + part, f32),
            pltpu.VMEM((2,) + part, f32),
            pltpu.VMEM(part, f32),
            pltpu.VMEM((2,) + part, f32),
            dma((3 + chunks,)),
            dma((6 + chunks,)),
            dma((3,)), dma((3,)),
            dma((chunks,)), dma((chunks,)),
            dma((chunks,)), dma((chunks,)),
            dma((2, chunks)), dma((2, chunks)),
            dma((chunks,)), dma((chunks,)),
            dma((chunks,)), dma((chunks,)),
            dma((2, 2)), dma((2, 2)),
        ],
        compiler_params=pltpu.CompilerParams(
            collective_id=0, has_side_effects=True, vmem_limit_bytes=SCAN_VMEM
        ),
        cost_estimate=cost(30),
        name="scan_devices",
    )(quadrant, cross_gain, boundary, sea_mask, previous, coupling)
    return out.reshape(4, dirs, quarter, columns), edges, halos


def settle_one(previous, coupling, inflow_of, gain, sea, rounded, settled, backward, sideways):
    bands, rows, columns = previous.shape
    block = BLOCK
    quarter = bands // 4
    pieces = columns // block
    gains = jnp.full((1, block), gain, f32)
    slope, scale = jnp.log(gains / (1.0 + gains)), 1.0 / (1.0 + gains)
    row = lax.broadcasted_iota(jnp.int32, (block, block), 0)
    column = lax.broadcasted_iota(jnp.int32, (block, block), 1)
    offset = row - column if sideways else column - row
    matrix = jnp.where(offset >= 0, jnp.exp(offset.astype(f32) * slope) * scale, 0.0)
    carry = gains * (matrix[block - 1 :] if sideways else matrix[:1])
    carry_last = carry[:, :1] if sideways else carry[:, block - 1 :]
    high = matrix.astype(bf16)
    low = (matrix - high.astype(f32)).astype(bf16)
    whole = jnp.concatenate(
        [
            jnp.concatenate([high, low], axis=1),
            jnp.concatenate([high, jnp.zeros_like(low)], axis=1),
        ],
        axis=0,
    )
    order = visit_order((rows, block), backward)
    before = None
    for k in range(pieces - 1, -1, -1) if sideways else range(pieces):
        here = slice(k * block, (k + 1) * block)
        couple, weight = weights(coupling[:, here], sea[:, here])
        first = jnp.where(order == 0, couple, 0.0)
        spans, reach, span = [], couple, 1
        while span < rows:
            spans.append((span, jnp.where(order >= span, reach, 0.0)))
            reach = jnp.where(order >= span, reach * rolled(reach, span, backward), reach)
            span *= 2
        values = []
        for f in range(bands):
            value = weight * previous[f, :, here].astype(f32) + first * inflow_of(
                f // quarter, f % quarter, here
            )
            for span, factor in spans:
                value = value + factor * rolled(value, span, backward)
            values.append(value)
        x = jnp.concatenate(values, axis=0)
        upper = x.astype(bf16)
        lower = (x - upper.astype(f32)).astype(bf16)
        both = jnp.dot(
            jnp.concatenate([upper, lower], axis=1), whole, preferred_element_type=f32
        )
        y = both[:, :block] + both[:, block:]
        last = jnp.broadcast_to(y[:, :1] if sideways else y[:, block - 1 :], y.shape)
        if before is not None:
            y = y + before * carry
            last = last + before * carry_last
        before = last
        masked = y.reshape(bands, rows, block) * sea[:, here][None]
        rounded[:, :, here] = masked.astype(bf16)
        if settled is not None:
            settled[:, :, here] = masked


def settle(previous, coupling, inflow_of, corner, gain, sea, rounded, settled):
    for flag in range(4):
        pl.when(corner == flag)(
            functools.partial(
                settle_one, previous, coupling, inflow_of, gain, sea, rounded, settled,
                flag % 2 == 1, flag // 2 == 1,
            )
        )


def wet_field(wet_tiles, wet):
    rows, columns = wet.shape
    for k in range(columns // BLOCK):
        flag = wet_tiles[:, k : k + 1].astype(f32)
        wet[:, k * BLOCK : (k + 1) * BLOCK] = jnp.broadcast_to(flag, (rows, BLOCK))


def source(coef, own, onward_of, against_of, settled, wet, result):
    bands = own.shape[0]
    wet_cells = wet[...]

    def one(f, onward, against):
        energy = own[f].astype(f32)
        value = coef[f] * (
            energy * energy * (onward + against) - 2.0 * energy * onward * against
        )
        result[f] = (settled[f] + wet_cells * value.astype(bf16).astype(f32)).astype(bf16)

    def above(f):
        return onward_of[f + 1].astype(f32)

    def below(f):
        return against_of[f - 1].astype(f32)

    nothing = jnp.zeros(wet.shape, f32)
    one(0, above(0), nothing)
    one(bands - 1, nothing, below(bands - 1))

    def body(f, _):
        one(f, above(f), below(f))
        return 0

    lax.fori_loop(1, bands - 1, body, 0, unroll=True)


def own_kernel(
    quadrant, cross_gain, coef, sea_mask, wet_tiles, previous, coupling, entering, rounded, settled, *refs
):
    dirs = previous.shape[0]
    *inner, sea, wet = refs
    sea[...] = sea_mask[...].astype(f32)
    wet_field(wet_tiles, wet)

    def one(d, _):
        settle(
            previous.at[d], coupling.at[d], lambda q, r, here: entering[q, d, r : r + 1, here],
            quadrant[d], cross_gain[d], sea, rounded.at[d], settled.at[d],
        )
        return 0

    def inner_source(d, _):
        source(
            coef, rounded.at[d], rounded.at[d + SHIFT], rounded.at[d - SHIFT], settled.at[d], wet,
            inner[0].at[d - SHIFT],
        )
        return 0

    lax.fori_loop(0, dirs, one, 0)
    if inner:
        lax.fori_loop(SHIFT, dirs - SHIFT, inner_source, 0)


def settle_own(quadrant, cross_gain, quad_coef, sea_mask, wet_tiles, previous, coupling, entering):
    dirs, bands, rows, columns = previous.shape
    vmem = pl.BlockSpec(memory_space=pltpu.VMEM)
    smem = pl.BlockSpec(memory_space=pltpu.SMEM)
    out_shape = [
        jax.ShapeDtypeStruct(previous.shape, bf16),
        jax.ShapeDtypeStruct(previous.shape, f32),
    ]
    if dirs > 2 * SHIFT:
        out_shape.append(jax.ShapeDtypeStruct((dirs - 2 * SHIFT,) + previous.shape[1:], bf16))
    return pl.pallas_call(
        own_kernel,
        in_specs=[smem, smem, smem] + [vmem] * 5,
        out_specs=[vmem] * len(out_shape),
        out_shape=out_shape,
        scratch_shapes=[
            pltpu.VMEM((rows, columns), f32),
            pltpu.VMEM((rows, columns), f32),
        ],
        compiler_params=pltpu.CompilerParams(vmem_limit_bytes=STEP_VMEM),
        cost_estimate=cost(12),
        name="settle_own",
    )(quadrant, cross_gain, quad_coef, sea_mask, wet_tiles, previous, coupling, entering)


def source_kernel(halo_marks, coef, sea_mask, wet_tiles, halo_previous, incoming_in, own, settled, *refs):
    *inner, out, halo, incoming, sea, wet, result, load_sem, store_sem = refs
    dirs, bands, rows, columns = settled.shape
    load = pltpu.make_async_copy(incoming_in, incoming, load_sem.at[0])
    load.start()
    edge = [d for d in range(dirs) if d < SHIFT or d >= dirs - SHIFT]
    stores = [pltpu.make_async_copy(result.at[i], out.at[d], store_sem.at[i]) for i, d in enumerate(edge)]
    if inner:
        copy = pltpu.make_async_copy(
            inner[0], out.at[pl.ds(SHIFT, dirs - 2 * SHIFT)], store_sem.at[len(edge)]
        )
        copy.start()
    sea[...] = sea_mask[...].astype(f32)
    wet_field(wet_tiles, wet)
    load.wait()

    def one_halo(t, _):
        way, at = 1 - t // SHIFT, t % SHIFT
        settle(
            halo_previous.at[t], incoming.at[way, 4, at],
            lambda q, r, here: incoming[way, q, at, r : r + 1, here],
            halo_marks[t, 1, 0].astype(jnp.int32), halo_marks[t, 0, 0], sea, halo.at[t], None,
        )
        return 0

    lax.fori_loop(0, 2 * SHIFT, one_halo, 0)
    for i, d in enumerate(edge):
        source(
            coef, own.at[d],
            own.at[d + SHIFT] if d + SHIFT < dirs else halo.at[2 * SHIFT + d - dirs],
            own.at[d - SHIFT] if d >= SHIFT else halo.at[d],
            settled.at[d], wet, result.at[i],
        )
        stores[i].start()
    for store in stores:
        store.wait()
    if inner:
        copy.wait()


def add_source(halo_marks, quad_coef, sea_mask, wet_tiles, halo_previous, incoming, rounded, settled, *inner):
    dirs, bands, rows, columns = settled.shape
    vmem = pl.BlockSpec(memory_space=pltpu.VMEM)
    smem = pl.BlockSpec(memory_space=pltpu.SMEM)
    anywhere = pl.BlockSpec(memory_space=pl.ANY)
    edges = min(dirs, 2 * SHIFT)
    return pl.pallas_call(
        source_kernel,
        in_specs=[smem, smem, vmem, vmem, vmem, anywhere, vmem, vmem] + [anywhere] * len(inner),
        out_specs=anywhere,
        out_shape=jax.ShapeDtypeStruct(settled.shape, bf16),
        scratch_shapes=[
            pltpu.VMEM((2 * SHIFT, bands, rows, columns), bf16),
            pltpu.VMEM(incoming.shape, f32),
            pltpu.VMEM((rows, columns), f32),
            pltpu.VMEM((rows, columns), f32),
            pltpu.VMEM((edges, bands, rows, columns), bf16),
            pltpu.SemaphoreType.DMA((1,)),
            pltpu.SemaphoreType.DMA((edges + 1,)),
        ],
        compiler_params=pltpu.CompilerParams(vmem_limit_bytes=STEP_VMEM),
        cost_estimate=cost(8),
        name="add_source",
    )(halo_marks, quad_coef, sea_mask, wet_tiles, halo_previous, incoming, rounded, settled, *inner)


def exchange(edges, dir_count):
    if dir_count == 2:
        return lax.ppermute(edges, "dirs", [(0, 1), (1, 0)])
    down = [(i, (i - 1) % dir_count) for i in range(dir_count)]
    up = [(i, (i + 1) % dir_count) for i in range(dir_count)]
    return jnp.stack([lax.ppermute(edges[0], "dirs", down), lax.ppermute(edges[1], "dirs", up)])


def on_device(
    row_devices, dir_devices,
    previous, boundary, row_coupling, cross_gain, block_inverse, quadrant, sea_mask, wet_tiles, quad_coef,
):
    entering, edges, (halo_previous, halo_marks) = scan_devices(
        row_devices, dir_devices, quadrant, cross_gain, boundary, sea_mask, previous, row_coupling
    )
    incoming = exchange(edges, dir_devices)
    rounded, settled, *inner = settle_own(
        quadrant, cross_gain, quad_coef, sea_mask, wet_tiles, previous, row_coupling, entering
    )
    return add_source(
        halo_marks, quad_coef, sea_mask, wet_tiles, halo_previous, incoming, rounded, settled, *inner
    )


def solution(mesh):
    in_specs = (
        P("dirs", None, "rows", None),
        P("dirs", None, None),
        P("dirs", "rows", None),
        P("dirs"),
        P("dirs", None, None),
        P("dirs"),
        P("rows", None),
        P("rows", None),
        P(),
    )
    out_specs = P("dirs", None, "rows", None)
    return jax.shard_map(
        functools.partial(on_device, mesh.shape["rows"], mesh.shape["dirs"]),
        mesh=mesh, in_specs=in_specs, out_specs=out_specs, check_vma=False,
    )
```

```python
import functools

import jax
import jax.numpy as jnp
from jax import lax
from jax.experimental import pallas as pl
from jax.experimental.pallas import tpu as pltpu
from jax.sharding import PartitionSpec as P

SHIFT = 2
f32 = jnp.float32
bf16 = jnp.bfloat16
MESH = pl.DeviceIdType.MESH
SCAN_VMEM = 56 * 1024 * 1024
STEP_VMEM = 56 * 1024 * 1024
BLOCK = 128


def cost(microseconds):
    return pl.CostEstimate(
        flops=0, bytes_accessed=int(microseconds * 3_000_000), transcendentals=0
    )


def weights(coupling, sea):
    return coupling * sea, sea * (1.0 - coupling)


def visit_order(shape, backward):
    row = lax.broadcasted_iota(jnp.int32, shape, 0)
    return shape[0] - 1 - row if backward else row


def rolled(x, steps, backward):
    rows = x.shape[0]
    return pltpu.roll(x, (rows - steps if backward else steps) % rows, 0)


def row_weights(coupling, sea, backward):
    couple, weight = weights(coupling, sea)
    rows = couple.shape[0]
    order = visit_order(couple.shape, backward)
    after = jnp.where(order < rows - 1, rolled(couple, rows - 1, backward), 1.0)
    span = 1
    while span < rows - 1:
        after = after * jnp.where(order < rows - span, rolled(after, rows - span, backward), 1.0)
        span *= 2
    gain = jnp.sum(jnp.where(order == 0, couple * after, 0.0), axis=0, keepdims=True)
    return weight * after, gain


def scan_kernel(
    count, dir_count, chunks, quadrant, cross_gain, coef, boundary_in, sea_in, previous_in, coupling_in, wet_in,
    own_out, settled_out, inner_out, halo_previous, halo_entering, halo_coupling, halo_marks,
    out, back_rows, cumulated, settled, rounded, result, wet_tiles, wet, sea_field,
    gain, state, shares, marks, boundary, sea_mask, previous, coupling,
    gains, got_core, half_total, got_pair, plane, chain_in, chain_out, pair_in, pair_out, core_out,
    load_sem, gain_send, gain_recv, core_send, core_recv, pair_send, pair_recv,
    chain_send, chain_recv, back_send, back_recv, last_send, last_recv, halo_send, halo_recv,
    edge_send, edge_recv, own_sem, settled_sem, inner_sem,
):
    me = lax.axis_index("rows")
    c, x, z = me % 2, (me // 2) % 2, me // 4
    depth = count // 4
    half = (c + x + z) % 2
    core_peer = me + 1 - 2 * c
    side_peer = me + 2 - 4 * x
    pair_peer = core_peer + 2 - 4 * x
    dirs = gain.shape[0]
    size = dirs // chunks
    peers = (core_peer, side_peer, pair_peer)

    def part(j):
        return pl.ds(j * size, size)

    barrier = pltpu.get_barrier_semaphore()
    for peer in peers:
        pl.semaphore_signal(barrier, inc=1, device_id={"rows": peer}, device_id_type=MESH)

    @pl.when(z > 0)
    def _():
        pl.semaphore_signal(barrier, inc=1, device_id={"rows": core_peer - 4}, device_id_type=MESH)

    @pl.when(z < depth - 1)
    def _():
        pl.semaphore_signal(barrier, inc=1, device_id={"rows": core_peer + 4}, device_id_type=MESH)

    mine = lax.axis_index("dirs")
    higher, lower = (mine + 1) % dir_count, (mine + dir_count - 1) % dir_count
    neighbours = (higher, lower) if dir_count > 2 else (higher,)
    for peer in neighbours:
        pl.semaphore_signal(barrier, inc=1, device_id={"dirs": peer}, device_id_type=MESH)

    order = [0] + list(range(chunks - 1, 0, -1))
    wet_load = pltpu.make_async_copy(wet_in, wet_tiles, load_sem.at[3 + chunks])
    coupling_load = pltpu.make_async_copy(coupling_in, coupling, load_sem.at[0])
    sea_load = pltpu.make_async_copy(sea_in, sea_mask, load_sem.at[1])
    boundary_load = pltpu.make_async_copy(boundary_in, boundary, load_sem.at[2])
    previous_loads = [
        pltpu.make_async_copy(previous_in.at[part(j)], previous.at[part(j)], load_sem.at[3 + j])
        for j in range(chunks)
    ]
    sea_load.start()
    coupling_load.start()
    for j in order:
        previous_loads[j].start()
    boundary_load.start()
    wet_load.start()
    for d in range(dirs):
        marks[d, 0:1] = jnp.full((1, marks.shape[2]), cross_gain[d], f32)
        marks[d, 1:2] = jnp.full((1, marks.shape[2]), quadrant[d].astype(f32), f32)
    def remote(src, dst, send, recv, peer):
        return pltpu.make_async_remote_copy(
            src_ref=src, dst_ref=dst, send_sem=send, recv_sem=recv,
            device_id={"rows": peer}, device_id_type=MESH,
        )

    gain_copies = [
        remote(gain, gains.at[i], gain_send.at[i], gain_recv.at[i], peer) for i, peer in enumerate(peers)
    ]
    core_copies = [
        remote(state.at[1 - half, :, part(j)], got_core.at[:, part(j)], core_send.at[j], core_recv.at[j], core_peer)
        for j in range(chunks)
    ]
    pair_copies = [
        remote(half_total.at[1 - x, part(j)], got_pair.at[part(j)], pair_send.at[j], pair_recv.at[j], pair_peer)
        for j in range(chunks)
    ]
    back_copies = [
        remote(pair_out.at[part(j)], pair_in.at[x, part(j)], back_send.at[j], back_recv.at[j], pair_peer)
        for j in range(chunks)
    ]
    last_copies = [
        remote(core_out.at[:, part(j)], out.at[half, :, part(j)], last_send.at[j], last_recv.at[j], core_peer)
        for j in range(chunks)
    ]

    flags = marks[:, 1:2, :]
    flags = flags - 2.0 * jnp.floor(0.5 * flags)
    back = jnp.concatenate([flags] * (gain.shape[-1] // flags.shape[-1]), axis=2)
    sea_load.wait()
    coupling_load.wait()
    sea = sea_mask[...].astype(f32)
    sea_field[...] = sea
    back_rows[...] = back
    for d in range(dirs):
        onward, onward_gain = row_weights(coupling[d], sea, False)
        against, _ = row_weights(coupling[d], sea, True)
        shares[d] = jnp.where(back[d] > 0.5, against, onward)
        gain[d] = onward_gain
    pl.semaphore_wait(
        barrier, 3 + len(neighbours) + (z > 0).astype(jnp.int32) + (z < depth - 1).astype(jnp.int32)
    )

    edge_copies = []
    for way, (peer, start) in enumerate(((lower, 0), (higher, dirs - SHIFT))):
        for i, (src, dst) in enumerate(
            (
                (coupling.at[pl.ds(start, SHIFT)], halo_coupling.at[way]),
                (out.at[:, :, pl.ds(start, SHIFT)], halo_entering.at[way]),
            )
        ):
            edge_copies.append(
                pltpu.make_async_remote_copy(
                    src_ref=src, dst_ref=dst,
                    send_sem=edge_send.at[way, i], recv_sem=edge_recv.at[way, i],
                    device_id={"dirs": peer}, device_id_type=MESH,
                )
            )

    halo_copies = []
    for way, (peer, start, to) in enumerate(((lower, 0, SHIFT), (higher, dirs - SHIFT, 0))):
        bands = pl.ds(1 - way, previous.shape[1] - 1)
        for i, (src, dst) in enumerate(
            (
                (previous_in.at[pl.ds(start, SHIFT), bands], halo_previous.at[pl.ds(to, SHIFT), bands]),
                (marks.at[pl.ds(start, SHIFT)], halo_marks.at[pl.ds(to, SHIFT)]),
            )
        ):
            halo_copies.append(
                pltpu.make_async_remote_copy(
                    src_ref=src, dst_ref=dst,
                    send_sem=halo_send.at[way, i], recv_sem=halo_recv.at[way, i],
                    device_id={"dirs": peer}, device_id_type=MESH,
                )
            )
            halo_copies[-1].start()

    for copy in gain_copies:
        copy.start()

    def compose(h, d, _):
        share = shares[d]
        for q in range(2):
            values = previous[d, pl.ds((2 * h + q) * state.shape[3], state.shape[3])].astype(f32)
            state[h, q, d] = jnp.sum(values * share[None], axis=1)
        return 0

    for j in order:
        previous_loads[j].wait()
        lax.fori_loop(j * size, (j + 1) * size, functools.partial(compose, 1 - half), 0)
        core_copies[j].start()
    for j in order:
        lax.fori_loop(j * size, (j + 1) * size, functools.partial(compose, half), 0)
    boundary_load.wait()
    wet_load.wait()
    wet_field(wet_tiles, wet)
    c_bit, x_bit = c.astype(f32), x.astype(f32)
    core_after = c_bit + back - 2.0 * c_bit * back
    pair_after = x_bit + back - 2.0 * x_bit * back
    for copy in gain_copies:
        copy.wait_recv()
    core_mine, core_theirs = gain[...], gains[0]
    pair_mine, pair_theirs = core_mine * core_theirs, gains[1] * gains[2]
    plane_gain = pair_mine * pair_theirs

    def total(after, mine, theirs):
        return after * mine + (1.0 - after), (1.0 - after) * theirs + after

    core_a, core_b = total(core_after, core_mine, core_theirs)
    pair_a, pair_b = total(pair_after, pair_mine, pair_theirs)

    def cut(v, j):
        return v[j * size : (j + 1) * size]

    for j in order:
        core_copies[j].wait_recv()
        half_total[:, part(j)] = (
            cut(core_a, j)[None] * got_core[:, part(j)] + cut(core_b, j)[None] * state[half, :, part(j)]
        )
        pair_copies[j].start()
    def local(d, _):
        local_sweep(previous.at[d], coupling.at[d], back_rows.at[d], sea_field, cumulated.at[d], settled.at[d])
        return 0

    early = min(dirs, 4)
    at_end = (z == 0) | (z == depth - 1)
    middle = jnp.where(at_end, dirs, early)
    lax.fori_loop(0, early, local, 0)
    upper = (2 * z >= depth).astype(jnp.int32)
    mine_at = 2 * half + x

    def chain(j, way):
        step = 1 - 2 * way
        has_before = jnp.where(way == 0, z > 0, z < depth - 1)
        has_after = jnp.where(way == 0, z < depth - 1, z > 0)
        copy = remote(
            chain_out.at[way, part(j)], chain_in.at[way, part(j)],
            chain_send.at[way, j], chain_recv.at[way, j], core_peer + 4 * step,
        )

        @pl.when(has_before)
        def _():
            copy.wait_recv()

        @pl.when(jnp.logical_not(has_before))
        def _():
            chain_in[way, part(j)] = boundary[part(j), mine_at]

        @pl.when(has_after)
        def _():
            chain_out[way, part(j)] = cut(plane_gain, j) * chain_in[way, part(j)] + plane[part(j)]
            copy.start()

    def split(after, mine, theirs):
        return after * theirs + (1.0 - after), (1.0 - after) * mine + after

    pair_p, pair_q = split(pair_after, pair_mine, pair_theirs)
    core_p, core_q = split(core_after, core_mine, core_theirs)

    def leave(j):
        entering = jnp.where(cut(back, j) > 0.5, chain_in[1, part(j)], chain_in[0, part(j)])
        pair_out[part(j)] = cut(pair_q, j) * entering + (1.0 - cut(pair_after, j)) * half_total[x, part(j)]
        back_copies[j].start()
        pair_in[x, part(j)] = cut(pair_p, j) * entering + cut(pair_after, j) * got_pair[part(j)]

    def finish(j):
        back_copies[j].wait_recv()
        entering = pair_in[:, part(j)]
        core_out[:, part(j)] = (
            cut(core_q, j)[None] * entering + (1.0 - cut(core_after, j))[None] * state[half, :, part(j)]
        )
        last_copies[j].start()
        out[half, :, part(j)] = cut(core_p, j)[None] * entering + cut(core_after, j)[None] * got_core[:, part(j)]

    for i in range(2 * chunks + 2):
        if i == chunks:
            lax.fori_loop(early, middle, local, 0)
        if i < chunks:
            j = order[i]
            pair_copies[j].wait_recv()
            plane[part(j)] = cut(pair_a, j) * got_pair[part(j)] + cut(pair_b, j) * half_total[x, part(j)]
            chain(j, upper)
        if chunks <= i < 2 * chunks:
            chain(order[i - chunks], 1 - upper)
            leave(order[i - chunks])
        if chunks + 2 <= i:
            finish(order[i - chunks - 2])
    lax.fori_loop(middle, dirs, local, 0)
    def own_copy(d):
        return pltpu.make_async_copy(rounded.at[d], own_out.at[d], own_sem.at[d])

    def settled_copy(d):
        return pltpu.make_async_copy(settled.at[d], settled_out.at[d], settled_sem.at[d])

    def inner_copy(d):
        return pltpu.make_async_copy(result.at[d], inner_out.at[d], inner_sem.at[d])

    def own(d, _):
        solve_free(
            out.at[:, :, d], cumulated.at[d], marks.at[d], sea_field, rounded.at[d], settled.at[d]
        )
        own_copy(d).start()
        settled_copy(d).start()
        return 0

    def inner(d, _):
        source(
            coef, rounded.at[d], rounded.at[d + SHIFT], rounded.at[d - SHIFT], settled.at[d], wet, result.at[d]
        )
        inner_copy(d).start()
        return 0

    def leave_own(d, _):
        own_copy(d).wait()
        settled_copy(d).wait()
        return 0

    def leave_inner(d, _):
        inner_copy(d).wait()
        return 0

    def chunk(i, _):
        j = (chunks - i) % chunks
        remote(
            core_out.at[:, part(j)], out.at[half, :, part(j)], last_send.at[j], last_recv.at[j], core_peer
        ).wait_recv()

        @pl.when(j == 0)
        def _():
            for copy in edge_copies[:2]:
                copy.start()

        @pl.when(j == chunks - 1)
        def _():
            for copy in edge_copies[2:]:
                copy.start()

        lax.fori_loop(j * size, (j + 1) * size, own, 0)
        return 0

    lax.fori_loop(0, chunks, chunk, 0)
    if dirs > 2 * SHIFT:
        lax.fori_loop(SHIFT, dirs - SHIFT, inner, 0)
        lax.fori_loop(SHIFT, dirs - SHIFT, leave_inner, 0)
    lax.fori_loop(0, dirs, leave_own, 0)
    for copy in halo_copies + edge_copies:
        copy.wait_recv()
    for copy in halo_copies + edge_copies + gain_copies + core_copies + pair_copies + back_copies + last_copies:
        copy.wait_send()

    def drain(j, way):
        copy = remote(
            chain_out.at[way, part(j)], chain_in.at[way, part(j)],
            chain_send.at[way, j], chain_recv.at[way, j], core_peer + 4 * (1 - 2 * way),
        )

        @pl.when(z < depth - 1 if way == 0 else z > 0)
        def _():
            copy.wait_send()

    for j in range(chunks):
        drain(j, 0)
        drain(j, 1)


def scan_devices(
    count, dir_count, quadrant, cross_gain, quad_coef, boundary, sea_mask, previous, coupling, wet_tiles
):
    dirs, bands, rows, columns = previous.shape
    chunks = 4 if dirs % 4 == 0 else 3 if dirs % 3 == 0 else 1
    quarter = bands // 4
    boundary = boundary.reshape(dirs, 4, quarter, columns)
    vmem = pl.BlockSpec(memory_space=pltpu.VMEM)
    smem = pl.BlockSpec(memory_space=pltpu.SMEM)
    part = (dirs, quarter, columns)
    dma = pltpu.SemaphoreType.DMA
    anywhere = pl.BlockSpec(memory_space=pl.ANY)
    hbm = pl.BlockSpec(memory_space=pltpu.HBM)
    marks = (dirs, 2, 128)

    def halo(a):
        return jax.ShapeDtypeStruct((2 * SHIFT,) + a.shape[1:], a.dtype)

    return pl.pallas_call(
        functools.partial(scan_kernel, count, dir_count, chunks),
        in_specs=[smem, smem, smem] + [hbm] * 5,
        out_specs=[anywhere] * 7,
        out_shape=[
            jax.ShapeDtypeStruct(previous.shape, bf16),
            jax.ShapeDtypeStruct(previous.shape, f32),
            jax.ShapeDtypeStruct(previous.shape, bf16),
            halo(previous),
            jax.ShapeDtypeStruct((2, 2, 2, SHIFT, quarter, columns), f32),
            jax.ShapeDtypeStruct((2, SHIFT, rows, columns), f32),
            jax.ShapeDtypeStruct((2 * SHIFT,) + marks[1:], f32),
        ],
        scratch_shapes=[
            pltpu.VMEM((2, 2) + part, f32),
            pltpu.VMEM((dirs, 1, columns), f32),
            pltpu.VMEM(coupling.shape, f32),
            pltpu.VMEM(previous.shape, f32),
            pltpu.VMEM(previous.shape, bf16),
            pltpu.VMEM(previous.shape, bf16),
            pltpu.VMEM(wet_tiles.shape, jnp.int32),
            pltpu.VMEM(sea_mask.shape, f32),
            pltpu.VMEM(sea_mask.shape, f32),
            pltpu.VMEM((dirs, 1, columns), f32),
            pltpu.VMEM((2, 2) + part, f32),
            pltpu.VMEM(coupling.shape, f32),
            pltpu.VMEM(marks, f32),
            pltpu.VMEM(boundary.shape, f32),
            pltpu.VMEM(sea_mask.shape, jnp.int32),
            pltpu.VMEM(previous.shape, bf16),
            pltpu.VMEM(coupling.shape, f32),
            pltpu.VMEM((3, dirs, 1, columns), f32),
            pltpu.VMEM((2,) + part, f32),
            pltpu.VMEM((2,) + part, f32),
            pltpu.VMEM(part, f32),
            pltpu.VMEM(part, f32),
            pltpu.VMEM((2,) + part, f32),
            pltpu.VMEM((2,) + part, f32),
            pltpu.VMEM((2,) + part, f32),
            pltpu.VMEM(part, f32),
            pltpu.VMEM((2,) + part, f32),
            dma((4 + chunks,)),
            dma((3,)), dma((3,)),
            dma((chunks,)), dma((chunks,)),
            dma((chunks,)), dma((chunks,)),
            dma((2, chunks)), dma((2, chunks)),
            dma((chunks,)), dma((chunks,)),
            dma((chunks,)), dma((chunks,)),
            dma((2, 2)), dma((2, 2)),
            dma((2, 2)), dma((2, 2)),
            dma((dirs,)), dma((dirs,)), dma((dirs,)),
        ],
        compiler_params=pltpu.CompilerParams(
            collective_id=0, has_side_effects=True, vmem_limit_bytes=SCAN_VMEM
        ),
        cost_estimate=cost(30),
        name="scan_devices",
    )(quadrant, cross_gain, quad_coef, boundary, sea_mask, previous, coupling, wet_tiles)


def spans_of(couple, backward):
    rows = couple.shape[0]
    order = visit_order(couple.shape, backward)
    spans, reach, span = [], couple, 1
    while span < rows:
        spans.append((span, jnp.where(order >= span, reach, 0.0)))
        reach = jnp.where(order >= span, reach * rolled(reach, span, backward), reach)
        span *= 2
    return spans, reach


def local_sweep(previous, coupling, back, sea, cumulated, local):
    bands, rows, columns = previous.shape
    for k in range(columns // BLOCK):
        here = slice(k * BLOCK, (k + 1) * BLOCK)
        couple, weight = weights(coupling[:, here], sea[:, here])
        flag = jnp.broadcast_to(back[:, here], couple.shape) > 0.5
        ways = [spans_of(couple, backward) for backward in (False, True)]
        cumulated[:, here] = jnp.where(flag, ways[1][1], ways[0][1])
        for f in range(bands):
            start = weight * previous[f, :, here].astype(f32)
            values = []
            for backward in (False, True):
                value = start
                for span, factor in ways[backward][0]:
                    value = value + factor * rolled(value, span, backward)
                values.append(value)
            local[f, :, here] = jnp.where(flag, values[1], values[0])


def solve_free(entering, cumulated, marks, sea, rounded, settled):
    bands, rows, columns = settled.shape
    block = BLOCK
    quarter = bands // 4
    pieces = columns // block
    gains, corner = marks[0:1], marks[1:2]
    side = corner > 1.5
    slope, scale = jnp.log(gains / (1.0 + gains)), 1.0 / (1.0 + gains)
    row = lax.broadcasted_iota(jnp.int32, (block, block), 0)
    column = lax.broadcasted_iota(jnp.int32, (block, block), 1)
    sides = jnp.broadcast_to(side, (block, block))
    offset = jnp.where(sides, row - column, column - row)
    matrix = jnp.where(offset >= 0, jnp.exp(offset.astype(f32) * slope) * scale, 0.0)
    lane = lax.broadcasted_iota(jnp.int32, (1, block), 1)
    reach = jnp.where(side, block - 1 - lane, lane).astype(f32)
    carry = gains * scale * jnp.exp(reach * slope)
    carry_last = gains * scale * jnp.exp((block - 1) * slope)
    high = matrix.astype(bf16)
    low = (matrix - high.astype(f32)).astype(bf16)
    whole = jnp.concatenate(
        [
            jnp.concatenate([high, low], axis=1),
            jnp.concatenate([high, jnp.zeros_like(low)], axis=1),
        ],
        axis=0,
    )
    solved, ends = [], []
    for k in range(pieces):
        here = slice(k * block, (k + 1) * block)
        growth = cumulated[:, here]
        x = jnp.concatenate(
            [
                settled[f, :, here]
                + growth * entering[f // quarter // 2, f // quarter % 2, f % quarter : f % quarter + 1, here]
                for f in range(bands)
            ],
            axis=0,
        )
        upper = x.astype(bf16)
        lower = (x - upper.astype(f32)).astype(bf16)
        both = jnp.dot(
            jnp.concatenate([upper, lower], axis=1), whole, preferred_element_type=f32
        )
        y = both[:, :block] + both[:, block:]
        solved.append(y)
        ends.append(
            jnp.where(
                jnp.broadcast_to(side, y.shape),
                jnp.broadcast_to(y[:, :1], y.shape),
                jnp.broadcast_to(y[:, block - 1 :], y.shape),
            )
        )
    onward, against = [None] * pieces, [None] * pieces
    for k in range(1, pieces):
        onward[k] = ends[k - 1] if k == 1 else ends[k - 1] + carry_last * onward[k - 1]
    for k in range(pieces - 2, -1, -1):
        against[k] = ends[k + 1] if k == pieces - 2 else ends[k + 1] + carry_last * against[k + 1]
    onward_carry = jnp.where(side, 0.0, carry)
    against_carry = jnp.where(side, carry, 0.0)
    for k in range(pieces):
        here = slice(k * block, (k + 1) * block)
        y = solved[k]
        if k > 0:
            y = y + onward[k] * onward_carry
        if k < pieces - 1:
            y = y + against[k] * against_carry
        masked = y.reshape(bands, rows, block) * sea[:, here][None]
        rounded[:, :, here] = masked.astype(bf16)
        settled[:, :, here] = masked


def settle_one(previous, coupling, inflow_of, gain, sea, rounded, settled, backward, sideways):
    bands, rows, columns = previous.shape
    block = BLOCK
    quarter = bands // 4
    pieces = columns // block
    gains = jnp.full((1, block), gain, f32)
    slope, scale = jnp.log(gains / (1.0 + gains)), 1.0 / (1.0 + gains)
    row = lax.broadcasted_iota(jnp.int32, (block, block), 0)
    column = lax.broadcasted_iota(jnp.int32, (block, block), 1)
    offset = row - column if sideways else column - row
    matrix = jnp.where(offset >= 0, jnp.exp(offset.astype(f32) * slope) * scale, 0.0)
    carry = gains * (matrix[block - 1 :] if sideways else matrix[:1])
    carry_last = carry[:, :1] if sideways else carry[:, block - 1 :]
    high = matrix.astype(bf16)
    low = (matrix - high.astype(f32)).astype(bf16)
    whole = jnp.concatenate(
        [
            jnp.concatenate([high, low], axis=1),
            jnp.concatenate([high, jnp.zeros_like(low)], axis=1),
        ],
        axis=0,
    )
    order = visit_order((rows, block), backward)
    before = None
    for k in range(pieces - 1, -1, -1) if sideways else range(pieces):
        here = slice(k * block, (k + 1) * block)
        couple, weight = weights(coupling[:, here], sea[:, here])
        first = jnp.where(order == 0, couple, 0.0)
        spans, reach, span = [], couple, 1
        while span < rows:
            spans.append((span, jnp.where(order >= span, reach, 0.0)))
            reach = jnp.where(order >= span, reach * rolled(reach, span, backward), reach)
            span *= 2
        values = []
        for f in range(bands):
            value = weight * previous[f, :, here].astype(f32) + first * inflow_of(
                f // quarter, f % quarter, here
            )
            for span, factor in spans:
                value = value + factor * rolled(value, span, backward)
            values.append(value)
        x = jnp.concatenate(values, axis=0)
        upper = x.astype(bf16)
        lower = (x - upper.astype(f32)).astype(bf16)
        both = jnp.dot(
            jnp.concatenate([upper, lower], axis=1), whole, preferred_element_type=f32
        )
        y = both[:, :block] + both[:, block:]
        last = jnp.broadcast_to(y[:, :1] if sideways else y[:, block - 1 :], y.shape)
        if before is not None:
            y = y + before * carry
            last = last + before * carry_last
        before = last
        masked = y.reshape(bands, rows, block) * sea[:, here][None]
        rounded[:, :, here] = masked.astype(bf16)
        if settled is not None:
            settled[:, :, here] = masked


def settle(previous, coupling, inflow_of, corner, gain, sea, rounded, settled):
    for flag in range(4):
        pl.when(corner == flag)(
            functools.partial(
                settle_one, previous, coupling, inflow_of, gain, sea, rounded, settled,
                flag % 2 == 1, flag // 2 == 1,
            )
        )


def wet_field(wet_columns, wet):
    rows, columns = wet.shape
    row = lax.broadcasted_iota(jnp.int32, (rows, rows), 0)
    column = lax.broadcasted_iota(jnp.int32, (rows, rows), 1)
    for k in range(columns // BLOCK):
        flags = jnp.broadcast_to(wet_columns[k : k + 1].astype(f32), (rows, rows))
        flag = jnp.sum(jnp.where(row == column, flags, 0.0), axis=1, keepdims=True)
        wet[:, k * BLOCK : (k + 1) * BLOCK] = jnp.broadcast_to(flag, (rows, BLOCK))


def source(coef, own, onward_of, against_of, settled, wet, result):
    bands = own.shape[0]
    wet_cells = wet[...]

    def one(f, onward, against):
        energy = own[f].astype(f32)
        value = coef[f] * (
            energy * energy * (onward + against) - 2.0 * energy * onward * against
        )
        result[f] = (settled[f] + wet_cells * value.astype(bf16).astype(f32)).astype(bf16)

    def above(f):
        return onward_of[f + 1].astype(f32)

    def below(f):
        return against_of[f - 1].astype(f32)

    nothing = jnp.zeros(wet.shape, f32)
    one(0, above(0), nothing)
    one(bands - 1, nothing, below(bands - 1))

    def body(f, _):
        one(f, above(f), below(f))
        return 0

    lax.fori_loop(1, bands - 1, body, 0, unroll=True)


def source_kernel(
    halo_marks, coef, sea_in, wet_in, previous_in, entering_in, coupling_in, own_in, settled_in, inner_in,
    out, previous, entering, coupling, own, settled, halo, sea_mask, wet_tiles, sea, wet, result, bounce,
    load_sem, own_sem, settled_sem, store_sem,
):
    dirs, bands, rows, columns = own.shape
    edge = [d for d in range(dirs) if d < SHIFT or d >= dirs - SHIFT]
    near = [d for d in range(dirs) if d < 2 * SHIFT or d >= dirs - 2 * SHIFT]
    small = [
        pltpu.make_async_copy(src, dst, load_sem.at[i])
        for i, (src, dst) in enumerate(
            ((sea_in, sea_mask), (wet_in, wet_tiles), (coupling_in, coupling), (entering_in, entering), (previous_in, previous))
        )
    ]
    own_loads = {d: pltpu.make_async_copy(own_in.at[d], own.at[d], own_sem.at[d]) for d in near}
    settled_loads = [
        pltpu.make_async_copy(settled_in.at[d], settled.at[i], settled_sem.at[i]) for i, d in enumerate(edge)
    ]
    stores = [pltpu.make_async_copy(result.at[i], out.at[d], store_sem.at[i]) for i, d in enumerate(edge)]
    inner = []
    if dirs > 2 * SHIFT:
        middle = pl.ds(SHIFT, dirs - 2 * SHIFT)
        inner.append(pltpu.make_async_copy(inner_in.at[middle], bounce, load_sem.at[5]))
        stores.append(pltpu.make_async_copy(bounce, out.at[middle], store_sem.at[len(edge)]))
    for load in small + list(own_loads.values()) + settled_loads + inner:
        load.start()
    for load in small[:2]:
        load.wait()
    sea[...] = sea_mask[...].astype(f32)
    wet_field(wet_tiles, wet)
    for load in small[2:]:
        load.wait()

    def one_halo(t, _):
        way, at = 1 - t // SHIFT, t % SHIFT
        settle(
            previous.at[t], coupling.at[way, at],
            lambda q, r, here: entering[way, q // 2, q % 2, at, r : r + 1, here],
            halo_marks[t, 1, 0].astype(jnp.int32), halo_marks[t, 0, 0], sea, halo.at[t], None,
        )
        return 0

    lax.fori_loop(0, 2 * SHIFT, one_halo, 0)
    for load in inner:
        load.wait()
        stores[-1].start()
    for load in list(own_loads.values()) + settled_loads:
        load.wait()
    for i, d in enumerate(edge):
        source(
            coef, own.at[d],
            own.at[d + SHIFT] if d + SHIFT < dirs else halo.at[2 * SHIFT + d - dirs],
            own.at[d - SHIFT] if d >= SHIFT else halo.at[d],
            settled.at[i], wet, result.at[i],
        )
        stores[i].start()
    for store in stores:
        store.wait()


def add_source(
    halo_marks, quad_coef, sea_mask, wet_tiles, halo_previous, halo_entering, halo_coupling, own, settled, inner
):
    dirs, bands, rows, columns = settled.shape
    smem = pl.BlockSpec(memory_space=pltpu.SMEM)
    anywhere = pl.BlockSpec(memory_space=pl.ANY)
    edges = min(dirs, 2 * SHIFT)
    dma = pltpu.SemaphoreType.DMA
    return pl.pallas_call(
        source_kernel,
        in_specs=[smem, smem] + [anywhere] * 8,
        out_specs=anywhere,
        out_shape=jax.ShapeDtypeStruct(settled.shape, bf16),
        scratch_shapes=[
            pltpu.VMEM(halo_previous.shape, bf16),
            pltpu.VMEM(halo_entering.shape, f32),
            pltpu.VMEM(halo_coupling.shape, f32),
            pltpu.VMEM(own.shape, bf16),
            pltpu.VMEM((edges, bands, rows, columns), f32),
            pltpu.VMEM(halo_previous.shape, bf16),
            pltpu.VMEM(sea_mask.shape, jnp.int32),
            pltpu.VMEM(wet_tiles.shape, jnp.int32),
            pltpu.VMEM((rows, columns), f32),
            pltpu.VMEM((rows, columns), f32),
            pltpu.VMEM((edges, bands, rows, columns), bf16),
            pltpu.VMEM((max(dirs - 2 * SHIFT, 1), bands, rows, columns), bf16),
            dma((6,)), dma((dirs,)), dma((edges,)), dma((edges + 1,)),
        ],
        compiler_params=pltpu.CompilerParams(vmem_limit_bytes=STEP_VMEM),
        cost_estimate=cost(6),
        name="add_source",
    )(halo_marks, quad_coef, sea_mask, wet_tiles, halo_previous, halo_entering, halo_coupling, own, settled, inner)


def on_device(
    row_devices, dir_devices,
    previous, boundary, row_coupling, cross_gain, block_inverse, quadrant, sea_mask, wet_tiles, quad_coef,
):
    wet_tiles = wet_tiles.T
    own, settled, inner, halo_previous, halo_entering, halo_coupling, halo_marks = scan_devices(
        row_devices, dir_devices, quadrant, cross_gain, quad_coef, boundary, sea_mask, previous, row_coupling,
        wet_tiles,
    )
    return add_source(
        halo_marks, quad_coef, sea_mask, wet_tiles, halo_previous, halo_entering, halo_coupling, own, settled, inner
    )


def solution(mesh):
    in_specs = (
        P("dirs", None, "rows", None),
        P("dirs", None, None),
        P("dirs", "rows", None),
        P("dirs"),
        P("dirs", None, None),
        P("dirs"),
        P("rows", None),
        P("rows", None),
        P(),
    )
    out_specs = P("dirs", None, "rows", None)
    return jax.shard_map(
        functools.partial(on_device, mesh.shape["rows"], mesh.shape["dirs"]),
        mesh=mesh, in_specs=in_specs, out_specs=out_specs, check_vma=False,
    )
```

```python
import functools

import jax
import jax.numpy as jnp
from jax import lax
from jax.experimental import pallas as pl
from jax.experimental.pallas import tpu as pltpu
from jax.sharding import PartitionSpec as P

SHIFT = 2
f32 = jnp.float32
bf16 = jnp.bfloat16
MESH = pl.DeviceIdType.MESH
SCAN_VMEM = 56 * 1024 * 1024
STEP_VMEM = 56 * 1024 * 1024
BLOCK = 128


def cost(microseconds):
    return pl.CostEstimate(
        flops=0, bytes_accessed=int(microseconds * 3_000_000), transcendentals=0
    )


def weights(coupling, sea):
    return coupling * sea, sea * (1.0 - coupling)


def visit_order(shape, backward):
    row = lax.broadcasted_iota(jnp.int32, shape, 0)
    return shape[0] - 1 - row if backward else row


def rolled(x, steps, backward):
    rows = x.shape[0]
    return pltpu.roll(x, (rows - steps if backward else steps) % rows, 0)


def row_weights(coupling, sea, backward):
    couple, weight = weights(coupling, sea)
    rows = couple.shape[0]
    order = visit_order(couple.shape, backward)
    after = jnp.where(order < rows - 1, rolled(couple, rows - 1, backward), 1.0)
    span = 1
    while span < rows - 1:
        after = after * jnp.where(order < rows - span, rolled(after, rows - span, backward), 1.0)
        span *= 2
    gain = jnp.sum(jnp.where(order == 0, couple * after, 0.0), axis=0, keepdims=True)
    return weight * after, gain


def scan_kernel(
    count, dir_count, chunks, quadrant, cross_gain, coef, boundary_in, sea_in, previous_in, coupling_in, wet_in,
    own_out, rest_out, inner_out, halo_previous, halo_entering, halo_coupling, halo_marks,
    out, rest, inflow, edge_state, back_rows, cumulated, settled, rounded, result, wet_tiles, wet, sea_field,
    gain, state, shares, marks, boundary, sea_mask, previous, coupling,
    gains, got_core, half_total, got_pair, plane, chain_in, chain_out, pair_in, pair_out, core_out,
    load_sem, gain_send, gain_recv, core_send, core_recv, pair_send, pair_recv,
    chain_send, chain_recv, back_send, back_recv, last_send, last_recv, halo_send, halo_recv,
    edge_send, edge_recv, own_sem, rest_sem, inner_sem,
):
    me = lax.axis_index("rows")
    c, x, z = me % 2, (me // 2) % 2, me // 4
    depth = count // 4
    half = (c + x + z) % 2
    core_peer = me + 1 - 2 * c
    side_peer = me + 2 - 4 * x
    pair_peer = core_peer + 2 - 4 * x
    dirs = gain.shape[0]
    size = dirs // chunks
    peers = (core_peer, side_peer, pair_peer)

    def part(j):
        return pl.ds(j * size, size)

    barrier = pltpu.get_barrier_semaphore()
    for peer in peers:
        pl.semaphore_signal(barrier, inc=1, device_id={"rows": peer}, device_id_type=MESH)

    @pl.when(z > 0)
    def _():
        pl.semaphore_signal(barrier, inc=1, device_id={"rows": core_peer - 4}, device_id_type=MESH)

    @pl.when(z < depth - 1)
    def _():
        pl.semaphore_signal(barrier, inc=1, device_id={"rows": core_peer + 4}, device_id_type=MESH)

    mine = lax.axis_index("dirs")
    higher, lower = (mine + 1) % dir_count, (mine + dir_count - 1) % dir_count
    neighbours = (higher, lower) if dir_count > 2 else (higher,)
    for peer in neighbours:
        pl.semaphore_signal(barrier, inc=1, device_id={"dirs": peer}, device_id_type=MESH)

    order = [0] + list(range(chunks - 1, 0, -1))
    wet_load = pltpu.make_async_copy(wet_in, wet_tiles, load_sem.at[3 + chunks])
    coupling_load = pltpu.make_async_copy(coupling_in, coupling, load_sem.at[0])
    sea_load = pltpu.make_async_copy(sea_in, sea_mask, load_sem.at[1])
    boundary_load = pltpu.make_async_copy(boundary_in, boundary, load_sem.at[2])
    previous_loads = [
        pltpu.make_async_copy(previous_in.at[part(j)], previous.at[part(j)], load_sem.at[3 + j])
        for j in range(chunks)
    ]
    sea_load.start()
    coupling_load.start()
    for j in order:
        previous_loads[j].start()
    boundary_load.start()
    wet_load.start()
    for d in range(dirs):
        marks[d, 0:1] = jnp.full((1, marks.shape[2]), cross_gain[d], f32)
        marks[d, 1:2] = jnp.full((1, marks.shape[2]), quadrant[d].astype(f32), f32)
    def remote(src, dst, send, recv, peer):
        return pltpu.make_async_remote_copy(
            src_ref=src, dst_ref=dst, send_sem=send, recv_sem=recv,
            device_id={"rows": peer}, device_id_type=MESH,
        )

    gain_copies = [
        remote(gain, gains.at[i], gain_send.at[i], gain_recv.at[i], peer) for i, peer in enumerate(peers)
    ]
    core_copies = [
        remote(state.at[1 - half, :, part(j)], got_core.at[:, part(j)], core_send.at[j], core_recv.at[j], core_peer)
        for j in range(chunks)
    ]
    pair_copies = [
        remote(half_total.at[1 - x, part(j)], got_pair.at[part(j)], pair_send.at[j], pair_recv.at[j], pair_peer)
        for j in range(chunks)
    ]
    back_copies = [
        remote(pair_out.at[part(j)], pair_in.at[x, part(j)], back_send.at[j], back_recv.at[j], pair_peer)
        for j in range(chunks)
    ]
    last_copies = [
        remote(core_out.at[:, part(j)], out.at[half, :, part(j)], last_send.at[j], last_recv.at[j], core_peer)
        for j in range(chunks)
    ]

    flags = marks[:, 1:2, :]
    flags = flags - 2.0 * jnp.floor(0.5 * flags)
    back = jnp.concatenate([flags] * (gain.shape[-1] // flags.shape[-1]), axis=2)
    sea_load.wait()
    coupling_load.wait()
    sea = sea_mask[...].astype(f32)
    sea_field[...] = sea
    back_rows[...] = back
    for d in range(dirs):
        onward, onward_gain = row_weights(coupling[d], sea, False)
        against, _ = row_weights(coupling[d], sea, True)
        shares[d] = jnp.where(back[d] > 0.5, against, onward)
        gain[d] = onward_gain
    pl.semaphore_wait(
        barrier, 3 + len(neighbours) + (z > 0).astype(jnp.int32) + (z < depth - 1).astype(jnp.int32)
    )

    edge_copies = []
    for way, (peer, start) in enumerate(((lower, 0), (higher, dirs - SHIFT))):
        edge_copies.append(
            pltpu.make_async_remote_copy(
                src_ref=edge_state.at[way], dst_ref=halo_entering.at[way],
                send_sem=edge_send.at[way], recv_sem=edge_recv.at[way],
                device_id={"dirs": peer}, device_id_type=MESH,
            )
        )

    halo_copies = []
    for way, (peer, start, to) in enumerate(((lower, 0, SHIFT), (higher, dirs - SHIFT, 0))):
        bands = pl.ds(1 - way, previous.shape[1] - 1)
        for i, (src, dst) in enumerate(
            (
                (previous_in.at[pl.ds(start, SHIFT), bands], halo_previous.at[pl.ds(to, SHIFT), bands]),
                (marks.at[pl.ds(start, SHIFT)], halo_marks.at[pl.ds(to, SHIFT)]),
                (coupling_in.at[pl.ds(start, SHIFT)], halo_coupling.at[way]),
            )
        ):
            halo_copies.append(
                pltpu.make_async_remote_copy(
                    src_ref=src, dst_ref=dst,
                    send_sem=halo_send.at[way, i], recv_sem=halo_recv.at[way, i],
                    device_id={"dirs": peer}, device_id_type=MESH,
                )
            )
            halo_copies[-1].start()

    for copy in gain_copies:
        copy.start()

    def compose(h, d, _):
        share = shares[d]
        for q in range(2):
            values = previous[d, pl.ds((2 * h + q) * state.shape[3], state.shape[3])].astype(f32)
            state[h, q, d] = jnp.sum(values * share[None], axis=1)
        return 0

    for j in order:
        previous_loads[j].wait()
        lax.fori_loop(j * size, (j + 1) * size, functools.partial(compose, 1 - half), 0)
        core_copies[j].start()
    for j in order:
        lax.fori_loop(j * size, (j + 1) * size, functools.partial(compose, half), 0)
    boundary_load.wait()
    wet_load.wait()
    wet_field(wet_tiles, wet)
    c_bit, x_bit = c.astype(f32), x.astype(f32)
    core_after = c_bit + back - 2.0 * c_bit * back
    pair_after = x_bit + back - 2.0 * x_bit * back
    for copy in gain_copies:
        copy.wait_recv()
    core_mine, core_theirs = gain[...], gains[0]
    pair_mine, pair_theirs = core_mine * core_theirs, gains[1] * gains[2]
    plane_gain = pair_mine * pair_theirs

    def total(after, mine, theirs):
        return after * mine + (1.0 - after), (1.0 - after) * theirs + after

    core_a, core_b = total(core_after, core_mine, core_theirs)
    pair_a, pair_b = total(pair_after, pair_mine, pair_theirs)

    def cut(v, j):
        return v[j * size : (j + 1) * size]

    for j in order:
        core_copies[j].wait_recv()
        half_total[:, part(j)] = (
            cut(core_a, j)[None] * got_core[:, part(j)] + cut(core_b, j)[None] * state[half, :, part(j)]
        )
        pair_copies[j].start()
    def local(d, _):
        side = jnp.where(marks[d, 1:2] > 1.5, 1.0, 0.0)
        local_sweep(
            previous.at[d], coupling.at[d], back_rows.at[d], side, sea_field, cumulated.at[d], settled.at[d]
        )
        return 0

    early = min(dirs, 4)
    at_end = (z == 0) | (z == depth - 1)
    middle = jnp.where(at_end, dirs, early)
    lax.fori_loop(0, early, local, 0)
    upper = (2 * z >= depth).astype(jnp.int32)
    mine_at = 2 * half + x

    def chain(j, way):
        step = 1 - 2 * way
        has_before = jnp.where(way == 0, z > 0, z < depth - 1)
        has_after = jnp.where(way == 0, z < depth - 1, z > 0)
        copy = remote(
            chain_out.at[way, part(j)], chain_in.at[way, part(j)],
            chain_send.at[way, j], chain_recv.at[way, j], core_peer + 4 * step,
        )

        @pl.when(has_before)
        def _():
            copy.wait_recv()

        @pl.when(jnp.logical_not(has_before))
        def _():
            chain_in[way, part(j)] = boundary[part(j), mine_at]

        @pl.when(has_after)
        def _():
            chain_out[way, part(j)] = cut(plane_gain, j) * chain_in[way, part(j)] + plane[part(j)]
            copy.start()

    def split(after, mine, theirs):
        return after * theirs + (1.0 - after), (1.0 - after) * mine + after

    pair_p, pair_q = split(pair_after, pair_mine, pair_theirs)
    core_p, core_q = split(core_after, core_mine, core_theirs)

    def leave(j):
        entering = jnp.where(cut(back, j) > 0.5, chain_in[1, part(j)], chain_in[0, part(j)])
        pair_out[part(j)] = cut(pair_q, j) * entering + (1.0 - cut(pair_after, j)) * half_total[x, part(j)]
        back_copies[j].start()
        pair_in[x, part(j)] = cut(pair_p, j) * entering + cut(pair_after, j) * got_pair[part(j)]

    def finish(j):
        back_copies[j].wait_recv()
        entering = pair_in[:, part(j)]
        core_out[:, part(j)] = (
            cut(core_q, j)[None] * entering + (1.0 - cut(core_after, j))[None] * state[half, :, part(j)]
        )
        last_copies[j].start()
        out[half, :, part(j)] = cut(core_p, j)[None] * entering + cut(core_after, j)[None] * got_core[:, part(j)]

    for i in range(2 * chunks + 2):
        if i == chunks:
            lax.fori_loop(early, middle, local, 0)
        if i < chunks:
            j = order[i]
            pair_copies[j].wait_recv()
            plane[part(j)] = cut(pair_a, j) * got_pair[part(j)] + cut(pair_b, j) * half_total[x, part(j)]
            chain(j, upper)
        if chunks <= i < 2 * chunks:
            chain(order[i - chunks], 1 - upper)
            leave(order[i - chunks])
        if chunks + 2 <= i:
            finish(order[i - chunks - 2])
    lax.fori_loop(middle, dirs, local, 0)
    def own_copy(j):
        return pltpu.make_async_copy(rounded.at[part(j)], own_out.at[part(j)], own_sem.at[j])

    rest_copy = pltpu.make_async_copy(rest, rest_out, rest_sem.at[0])

    count = dirs - 2 * SHIFT
    step = 2 if count % 2 == 0 else 1

    def inner_copy(i):
        piece = pl.ds(SHIFT + i * step, step)
        return pltpu.make_async_copy(result.at[piece], inner_out.at[piece], inner_sem.at[i])

    def own(d, _):
        solve_free(
            out.at[:, :, d], inflow, cumulated.at[d], marks.at[d], sea_field, rounded.at[d], settled.at[d]
        )
        return 0

    def inner(d, _):
        source(
            coef, rounded.at[d], rounded.at[d + SHIFT], rounded.at[d - SHIFT], settled.at[d], None, wet,
            result.at[d],
        )
        return 0

    def inner_piece(i, _):
        lax.fori_loop(SHIFT + i * step, SHIFT + (i + 1) * step, inner, 0)
        inner_copy(i).start()
        return 0

    def edge_rest(i, _):
        d = jnp.where(i < SHIFT, i, i + dirs - edges)

        def band(f, _):
            rest[i, f] = (settled[d, f] - rounded[d, f].astype(f32)).astype(bf16)
            return 0

        lax.fori_loop(0, bands, band, 0, unroll=8)
        return 0

    def chunk(i, _):
        j = (chunks - i) % chunks
        remote(
            core_out.at[:, part(j)], out.at[half, :, part(j)], last_send.at[j], last_recv.at[j], core_peer
        ).wait_recv()

        for way, (at, start) in enumerate(((0, 0), (chunks - 1, dirs - SHIFT))):

            @pl.when(j == at if size >= SHIFT else i == chunks - 1)
            def _(way=way, start=start):
                edge_state[way] = out[:, :, start : start + SHIFT].astype(bf16)
                edge_copies[way].start()

        lax.fori_loop(j * size, (j + 1) * size, own, 0)
        own_copy(j).start()
        return 0

    lax.fori_loop(0, chunks, chunk, 0)
    bands, edges = previous.shape[1], rest.shape[0]
    lax.fori_loop(0, edges, edge_rest, 0)
    rest_copy.start()
    if count > 0:
        lax.fori_loop(0, count // step, inner_piece, 0)
        for i in range(count // step):
            inner_copy(i).wait()
    for j in range(chunks):
        own_copy(j).wait()
    rest_copy.wait()
    for copy in halo_copies + edge_copies:
        copy.wait_recv()
    for copy in halo_copies + edge_copies + gain_copies + core_copies + pair_copies + back_copies + last_copies:
        copy.wait_send()

    def drain(j, way):
        copy = remote(
            chain_out.at[way, part(j)], chain_in.at[way, part(j)],
            chain_send.at[way, j], chain_recv.at[way, j], core_peer + 4 * (1 - 2 * way),
        )

        @pl.when(z < depth - 1 if way == 0 else z > 0)
        def _():
            copy.wait_send()

    for j in range(chunks):
        drain(j, 0)
        drain(j, 1)


def scan_devices(
    count, dir_count, quadrant, cross_gain, quad_coef, boundary, sea_mask, previous, coupling, wet_tiles
):
    dirs, bands, rows, columns = previous.shape
    chunks = 4 if dirs % 4 == 0 else 3 if dirs % 3 == 0 else 1
    quarter = bands // 4
    boundary = boundary.reshape(dirs, 4, quarter, columns)
    vmem = pl.BlockSpec(memory_space=pltpu.VMEM)
    smem = pl.BlockSpec(memory_space=pltpu.SMEM)
    part = (dirs, quarter, columns)
    dma = pltpu.SemaphoreType.DMA
    anywhere = pl.BlockSpec(memory_space=pl.ANY)
    hbm = pl.BlockSpec(memory_space=pltpu.HBM)
    marks = (dirs, 2, 128)

    def halo(a):
        return jax.ShapeDtypeStruct((2 * SHIFT,) + a.shape[1:], a.dtype)

    return pl.pallas_call(
        functools.partial(scan_kernel, count, dir_count, chunks),
        in_specs=[smem, smem, smem] + [hbm] * 5,
        out_specs=[anywhere] * 7,
        out_shape=[
            jax.ShapeDtypeStruct(previous.shape, bf16),
            jax.ShapeDtypeStruct((min(dirs, 2 * SHIFT),) + previous.shape[1:], bf16),
            jax.ShapeDtypeStruct(previous.shape, bf16),
            halo(previous),
            jax.ShapeDtypeStruct((2, 2, 2, SHIFT, quarter, columns), bf16),
            jax.ShapeDtypeStruct((2, SHIFT, rows, columns), f32),
            jax.ShapeDtypeStruct((2 * SHIFT,) + marks[1:], f32),
        ],
        scratch_shapes=[
            pltpu.VMEM((2, 2) + part, f32),
            pltpu.VMEM((min(dirs, 2 * SHIFT),) + previous.shape[1:], bf16),
            pltpu.VMEM((4, quarter, columns), f32),
            pltpu.VMEM((2, 2, 2, SHIFT, quarter, columns), bf16),
            pltpu.VMEM((dirs, 1, columns), f32),
            pltpu.VMEM(coupling.shape, f32),
            pltpu.VMEM(previous.shape, f32),
            pltpu.VMEM(previous.shape, bf16),
            pltpu.VMEM(previous.shape, bf16),
            pltpu.VMEM(wet_tiles.shape, jnp.int32),
            pltpu.VMEM(sea_mask.shape, f32),
            pltpu.VMEM(sea_mask.shape, f32),
            pltpu.VMEM((dirs, 1, columns), f32),
            pltpu.VMEM((2, 2) + part, f32),
            pltpu.VMEM(coupling.shape, f32),
            pltpu.VMEM(marks, f32),
            pltpu.VMEM(boundary.shape, f32),
            pltpu.VMEM(sea_mask.shape, jnp.int32),
            pltpu.VMEM(previous.shape, bf16),
            pltpu.VMEM(coupling.shape, f32),
            pltpu.VMEM((3, dirs, 1, columns), f32),
            pltpu.VMEM((2,) + part, f32),
            pltpu.VMEM((2,) + part, f32),
            pltpu.VMEM(part, f32),
            pltpu.VMEM(part, f32),
            pltpu.VMEM((2,) + part, f32),
            pltpu.VMEM((2,) + part, f32),
            pltpu.VMEM((2,) + part, f32),
            pltpu.VMEM(part, f32),
            pltpu.VMEM((2,) + part, f32),
            dma((4 + chunks,)),
            dma((3,)), dma((3,)),
            dma((chunks,)), dma((chunks,)),
            dma((chunks,)), dma((chunks,)),
            dma((2, chunks)), dma((2, chunks)),
            dma((chunks,)), dma((chunks,)),
            dma((chunks,)), dma((chunks,)),
            dma((2, 3)), dma((2, 3)),
            dma((2,)), dma((2,)),
            dma((dirs,)), dma((dirs,)), dma((dirs,)),
        ],
        compiler_params=pltpu.CompilerParams(
            collective_id=0, has_side_effects=True, vmem_limit_bytes=SCAN_VMEM
        ),
        cost_estimate=cost(30),
        name="scan_devices",
    )(quadrant, cross_gain, quad_coef, boundary, sea_mask, previous, coupling, wet_tiles)


def spans_of(couple, backward):
    rows = couple.shape[0]
    order = visit_order(couple.shape, backward)
    spans, reach, span = [], couple, 1
    while span < rows:
        spans.append((span, jnp.where(order >= span, reach, 0.0)))
        reach = jnp.where(order >= span, reach * rolled(reach, span, backward), reach)
        span *= 2
    return spans, reach


def local_sweep(previous, coupling, back, side, sea, cumulated, local):
    bands, rows, columns = previous.shape
    pieces = columns // BLOCK

    def blocks(f, here, weight, ways, flag):
        start = weight * previous[f, :, here].astype(f32)
        values = []
        for backward in (False, True):
            value = start
            for span, factor in ways[backward][0]:
                value = value + factor * rolled(value, span, backward)
            values.append(value)
        return jnp.where(flag, values[1], values[0])

    shape = (rows, BLOCK)
    flag = jnp.broadcast_to(back[:, :BLOCK], shape) > 0.5
    sides = jnp.broadcast_to(side, shape) > 0.5
    for k in range(pieces // 2):
        pair = [slice(at * BLOCK, (at + 1) * BLOCK) for at in (k, pieces - 1 - k)]
        held = []
        for here in pair:
            couple, weight = weights(coupling[:, here], sea[:, here])
            ways = [spans_of(couple, backward) for backward in (False, True)]
            held.append((weight, ways, jnp.where(flag, ways[1][1], ways[0][1])))
        for at, here in enumerate(pair):
            cumulated[:, here] = jnp.where(sides, held[1 - at][2], held[at][2])
        for f in range(bands):
            values = [blocks(f, here, *held[at][:2], flag) for at, here in enumerate(pair)]
            for at, here in enumerate(pair):
                local[f, :, here] = jnp.where(sides, values[1 - at], values[at])


def solve_free(entering, inflow, cumulated, marks, sea, rounded, settled):
    bands, rows, columns = settled.shape
    block = BLOCK
    quarter = bands // 4
    pieces = columns // block
    gains, corner = marks[0:1], marks[1:2]
    side = corner > 1.5
    slope, scale = jnp.log(gains / (1.0 + gains)), 1.0 / (1.0 + gains)
    row = lax.broadcasted_iota(jnp.int32, (block, block), 0)
    column = lax.broadcasted_iota(jnp.int32, (block, block), 1)
    sides = jnp.broadcast_to(side, (block, block))
    offset = jnp.where(sides, row - column, column - row)
    matrix = jnp.where(offset >= 0, jnp.exp(offset.astype(f32) * slope) * scale, 0.0)
    lane = lax.broadcasted_iota(jnp.int32, (1, block), 1)
    reach = jnp.where(side, block - 1 - lane, lane).astype(f32)
    carry = gains * scale * jnp.exp(reach * slope)
    carry_last = gains * scale * jnp.exp((block - 1) * slope)
    high = matrix.astype(bf16)
    low = (matrix - high.astype(f32)).astype(bf16)
    whole = jnp.concatenate(
        [
            jnp.concatenate([high, low], axis=1),
            jnp.concatenate([high, jnp.zeros_like(low)], axis=1),
        ],
        axis=0,
    )
    pairs = [
        [slice(at * block, (at + 1) * block) for at in (k, pieces - 1 - k)] for k in range(pieces // 2)
    ]
    flip = jnp.broadcast_to(side, (quarter, block))
    for q in range(4):
        for pair in pairs:
            values = [entering[q // 2, q % 2, :, here] for here in pair]
            for at, here in enumerate(pair):
                inflow[q, :, here] = jnp.where(flip, values[1 - at], values[at])
    before = None
    for k in range(pieces):
        here = slice(k * block, (k + 1) * block)
        growth = cumulated[:, here]
        x = jnp.concatenate(
            [
                settled[f, :, here] + growth * inflow[f // quarter, f % quarter : f % quarter + 1, here]
                for f in range(bands)
            ],
            axis=0,
        )
        upper = x.astype(bf16)
        lower = (x - upper.astype(f32)).astype(bf16)
        both = jnp.dot(
            jnp.concatenate([upper, lower], axis=1), whole, preferred_element_type=f32
        )
        y = both[:, :block] + both[:, block:]
        if k < pieces - 1:
            last = jnp.where(
                jnp.broadcast_to(side, y.shape),
                jnp.broadcast_to(y[:, :1], y.shape),
                jnp.broadcast_to(y[:, block - 1 :], y.shape),
            )
        if before is not None:
            y = y + before * carry
            last = last + before * carry_last
        before = last
        settled[:, :, here] = y.reshape(bands, rows, block)
    flip = jnp.broadcast_to(side, (rows, block))
    for pair in pairs:
        field = [sea[:, here] for here in pair]
        for f in range(bands):
            values = [settled[f, :, here] for here in pair]
            for at, here in enumerate(pair):
                masked = jnp.where(flip, values[1 - at], values[at]) * field[at]
                settled[f, :, here] = masked
                rounded[f, :, here] = masked.astype(bf16)


def settle_one(previous, coupling, inflow_of, gain, sea, rounded, settled, backward, sideways):
    bands, rows, columns = previous.shape
    block = BLOCK
    quarter = bands // 4
    pieces = columns // block
    gains = jnp.full((1, block), gain, f32)
    slope, scale = jnp.log(gains / (1.0 + gains)), 1.0 / (1.0 + gains)
    row = lax.broadcasted_iota(jnp.int32, (block, block), 0)
    column = lax.broadcasted_iota(jnp.int32, (block, block), 1)
    offset = row - column if sideways else column - row
    matrix = jnp.where(offset >= 0, jnp.exp(offset.astype(f32) * slope) * scale, 0.0)
    carry = gains * (matrix[block - 1 :] if sideways else matrix[:1])
    carry_last = carry[:, :1] if sideways else carry[:, block - 1 :]
    high = matrix.astype(bf16)
    low = (matrix - high.astype(f32)).astype(bf16)
    whole = jnp.concatenate(
        [
            jnp.concatenate([high, low], axis=1),
            jnp.concatenate([high, jnp.zeros_like(low)], axis=1),
        ],
        axis=0,
    )
    order = visit_order((rows, block), backward)
    before = None
    for k in range(pieces - 1, -1, -1) if sideways else range(pieces):
        here = slice(k * block, (k + 1) * block)
        couple, weight = weights(coupling[:, here], sea[:, here])
        first = jnp.where(order == 0, couple, 0.0)
        spans, reach, span = [], couple, 1
        while span < rows:
            spans.append((span, jnp.where(order >= span, reach, 0.0)))
            reach = jnp.where(order >= span, reach * rolled(reach, span, backward), reach)
            span *= 2
        values = []
        for f in range(bands):
            value = weight * previous[f, :, here].astype(f32) + first * inflow_of(
                f // quarter, f % quarter, here
            )
            for span, factor in spans:
                value = value + factor * rolled(value, span, backward)
            values.append(value)
        x = jnp.concatenate(values, axis=0)
        upper = x.astype(bf16)
        lower = (x - upper.astype(f32)).astype(bf16)
        both = jnp.dot(
            jnp.concatenate([upper, lower], axis=1), whole, preferred_element_type=f32
        )
        y = both[:, :block] + both[:, block:]
        last = jnp.broadcast_to(y[:, :1] if sideways else y[:, block - 1 :], y.shape)
        if before is not None:
            y = y + before * carry
            last = last + before * carry_last
        before = last
        masked = y.reshape(bands, rows, block) * sea[:, here][None]
        rounded[:, :, here] = masked.astype(bf16)
        if settled is not None:
            settled[:, :, here] = masked


def settle(previous, coupling, inflow_of, corner, gain, sea, rounded, settled):
    for flag in range(4):
        pl.when(corner == flag)(
            functools.partial(
                settle_one, previous, coupling, inflow_of, gain, sea, rounded, settled,
                flag % 2 == 1, flag // 2 == 1,
            )
        )


def wet_field(wet_columns, wet):
    rows, columns = wet.shape
    row = lax.broadcasted_iota(jnp.int32, (rows, rows), 0)
    column = lax.broadcasted_iota(jnp.int32, (rows, rows), 1)
    for k in range(columns // BLOCK):
        flags = jnp.broadcast_to(wet_columns[k : k + 1].astype(f32), (rows, rows))
        flag = jnp.sum(jnp.where(row == column, flags, 0.0), axis=1, keepdims=True)
        wet[:, k * BLOCK : (k + 1) * BLOCK] = jnp.broadcast_to(flag, (rows, BLOCK))


def source(coef, own, onward_of, against_of, settled, rest, wet, result):
    bands = own.shape[0]
    wet_cells = wet[...]

    def one(f, onward, against):
        energy = own[f].astype(f32)
        value = coef[f] * (
            energy * energy * (onward + against) - 2.0 * energy * onward * against
        )
        base = settled[f] if rest is None else energy + rest[f].astype(f32)
        result[f] = (base + wet_cells * value.astype(bf16).astype(f32)).astype(bf16)

    def above(f):
        return onward_of[f + 1].astype(f32)

    def below(f):
        return against_of[f - 1].astype(f32)

    nothing = jnp.zeros(wet.shape, f32)
    one(0, above(0), nothing)
    one(bands - 1, nothing, below(bands - 1))

    def body(f, _):
        one(f, above(f), below(f))
        return 0

    lax.fori_loop(1, bands - 1, body, 0, unroll=True)


def source_kernel(
    halo_marks, coef, sea_in, wet_in, previous_in, entering_in, coupling_in, own_in, rest_in, inner_in,
    out, previous, incoming, entering, coupling, own, rest, halo, sea_mask, wet_tiles, sea, wet, result, bounce,
    load_sem, store_sem,
):
    dirs, bands, rows, columns = own.shape
    edge = [d for d in range(dirs) if d < SHIFT or d >= dirs - SHIFT]
    small = [
        pltpu.make_async_copy(src, dst, load_sem.at[i])
        for i, (src, dst) in enumerate(
            ((sea_in, sea_mask), (wet_in, wet_tiles), (coupling_in, coupling), (entering_in, incoming))
        )
    ]
    previous_load = pltpu.make_async_copy(previous_in, previous, load_sem.at[4])
    late = [
        pltpu.make_async_copy(own_in, own, load_sem.at[5]),
        pltpu.make_async_copy(rest_in, rest, load_sem.at[6]),
    ]
    runs = [(0, 0, len(edge))] if dirs <= 2 * SHIFT else [(0, 0, SHIFT), (SHIFT, dirs - SHIFT, SHIFT)]
    stores = [
        pltpu.make_async_copy(result.at[pl.ds(at, n)], out.at[pl.ds(d, n)], store_sem.at[k])
        for k, (at, d, n) in enumerate(runs)
    ]
    inner = []
    if dirs > 2 * SHIFT:
        middle = pl.ds(SHIFT, dirs - 2 * SHIFT)
        inner = [
            pltpu.make_async_copy(inner_in.at[middle], bounce, load_sem.at[7]),
            pltpu.make_async_copy(bounce, out.at[middle], store_sem.at[2]),
        ]
    for load in small:
        load.start()
    for load in [previous_load] + late + inner[:1]:
        load.start()
    for load in small:
        load.wait()
    sea[...] = sea_mask[...].astype(f32)
    wet_field(wet_tiles, wet)
    entering[...] = incoming[...].astype(f32)

    def one_halo(t, _):
        way, at = 1 - t // SHIFT, t % SHIFT
        settle(
            previous.at[t], coupling.at[way, at],
            lambda q, r, here: entering[way, q // 2, q % 2, at, r : r + 1, here],
            halo_marks[t, 1, 0].astype(jnp.int32), halo_marks[t, 0, 0], sea, halo.at[t], None,
        )
        return 0

    previous_load.wait()
    lax.fori_loop(0, 2 * SHIFT, one_halo, 0)
    if inner:
        inner[0].wait()
        inner[1].start()
    for load in late:
        load.wait()
    for i, d in enumerate(edge):
        source(
            coef, own.at[d],
            own.at[d + SHIFT] if d + SHIFT < dirs else halo.at[2 * SHIFT + d - dirs],
            own.at[d - SHIFT] if d >= SHIFT else halo.at[d],
            None, rest.at[i], wet, result.at[i],
        )
        for store, run in zip(stores, runs):
            if i == run[0] + run[2] - 1:
                store.start()
    for store in stores + inner[1:]:
        store.wait()


def add_source(
    halo_marks, quad_coef, sea_mask, wet_tiles, halo_previous, halo_entering, halo_coupling, own, rest, inner
):
    dirs, bands, rows, columns = own.shape
    smem = pl.BlockSpec(memory_space=pltpu.SMEM)
    anywhere = pl.BlockSpec(memory_space=pl.ANY)
    edges = min(dirs, 2 * SHIFT)
    dma = pltpu.SemaphoreType.DMA
    return pl.pallas_call(
        source_kernel,
        in_specs=[smem, smem] + [anywhere] * 8,
        out_specs=anywhere,
        out_shape=jax.ShapeDtypeStruct(own.shape, bf16),
        scratch_shapes=[
            pltpu.VMEM(halo_previous.shape, bf16),
            pltpu.VMEM(halo_entering.shape, bf16),
            pltpu.VMEM(halo_entering.shape, f32),
            pltpu.VMEM(halo_coupling.shape, f32),
            pltpu.VMEM(own.shape, bf16),
            pltpu.VMEM((edges, bands, rows, columns), bf16),
            pltpu.VMEM(halo_previous.shape, bf16),
            pltpu.VMEM(sea_mask.shape, jnp.int32),
            pltpu.VMEM(wet_tiles.shape, jnp.int32),
            pltpu.VMEM((rows, columns), f32),
            pltpu.VMEM((rows, columns), f32),
            pltpu.VMEM((edges, bands, rows, columns), bf16),
            pltpu.VMEM((max(dirs - 2 * SHIFT, 1), bands, rows, columns), bf16),
            dma((8,)), dma((3,)),
        ],
        compiler_params=pltpu.CompilerParams(vmem_limit_bytes=STEP_VMEM),
        cost_estimate=cost(6),
        name="add_source",
    )(halo_marks, quad_coef, sea_mask, wet_tiles, halo_previous, halo_entering, halo_coupling, own, rest, inner)


def on_device(
    row_devices, dir_devices,
    previous, boundary, row_coupling, cross_gain, block_inverse, quadrant, sea_mask, wet_tiles, quad_coef,
):
    wet_tiles = wet_tiles.T
    own, rest, inner, halo_previous, halo_entering, halo_coupling, halo_marks = scan_devices(
        row_devices, dir_devices, quadrant, cross_gain, quad_coef, boundary, sea_mask, previous, row_coupling,
        wet_tiles,
    )
    return add_source(
        halo_marks, quad_coef, sea_mask, wet_tiles, halo_previous, halo_entering, halo_coupling, own, rest, inner
    )


def solution(mesh):
    in_specs = (
        P("dirs", None, "rows", None),
        P("dirs", None, None),
        P("dirs", "rows", None),
        P("dirs"),
        P("dirs", None, None),
        P("dirs"),
        P("rows", None),
        P("rows", None),
        P(),
    )
    out_specs = P("dirs", None, "rows", None)
    return jax.shard_map(
        functools.partial(on_device, mesh.shape["rows"], mesh.shape["dirs"]),
        mesh=mesh, in_specs=in_specs, out_specs=out_specs, check_vma=False,
    )
```

```python
import functools

import jax
import jax.numpy as jnp
from jax import lax
from jax.experimental import pallas as pl
from jax.experimental.pallas import tpu as pltpu
from jax.sharding import PartitionSpec as P

SHIFT = 2
f32 = jnp.float32
bf16 = jnp.bfloat16
MESH = pl.DeviceIdType.MESH
SCAN_VMEM = 56 * 1024 * 1024
STEP_VMEM = 56 * 1024 * 1024
BLOCK = 128


def cost(microseconds):
    return pl.CostEstimate(
        flops=0, bytes_accessed=int(microseconds * 3_000_000), transcendentals=0
    )


def weights(coupling, sea):
    return coupling * sea, sea * (1.0 - coupling)


def visit_order(shape, backward):
    row = lax.broadcasted_iota(jnp.int32, shape, 0)
    return shape[0] - 1 - row if backward else row


def rolled(x, steps, backward):
    rows = x.shape[0]
    return pltpu.roll(x, (rows - steps if backward else steps) % rows, 0)


def row_weights(coupling, sea, backward):
    couple, weight = weights(coupling, sea)
    rows = couple.shape[0]
    order = visit_order(couple.shape, backward)
    after = jnp.where(order < rows - 1, rolled(couple, rows - 1, backward), 1.0)
    span = 1
    while span < rows - 1:
        after = after * jnp.where(order < rows - span, rolled(after, rows - span, backward), 1.0)
        span *= 2
    gain = jnp.sum(jnp.where(order == 0, couple * after, 0.0), axis=0, keepdims=True)
    return weight * after, gain


def scan_kernel(
    count, dir_count, chunks, quadrant, cross_gain, boundary_in, sea_in, previous_in, coupling_in,
    own_out, rest_out, halo_previous, halo_entering, halo_coupling, halo_marks,
    out, rest, inflow, edge_state, back_rows, cumulated, settled, rounded, sea_field,
    gain, state, shares, marks, boundary, sea_mask, previous, coupling,
    gains, got_core, half_total, got_pair, plane, chain_in, chain_out, pair_in, pair_out, core_out,
    load_sem, gain_send, gain_recv, core_send, core_recv, pair_send, pair_recv,
    chain_send, chain_recv, back_send, back_recv, last_send, last_recv, halo_send, halo_recv,
    edge_send, edge_recv, own_sem, rest_sem,
):
    me = lax.axis_index("rows")
    c, x, z = me % 2, (me // 2) % 2, me // 4
    depth = count // 4
    half = (c + x + z) % 2
    core_peer = me + 1 - 2 * c
    side_peer = me + 2 - 4 * x
    pair_peer = core_peer + 2 - 4 * x
    dirs = gain.shape[0]
    size = dirs // chunks
    peers = (core_peer, side_peer, pair_peer)

    def part(j):
        return pl.ds(j * size, size)

    barrier = pltpu.get_barrier_semaphore()
    for peer in peers:
        pl.semaphore_signal(barrier, inc=1, device_id={"rows": peer}, device_id_type=MESH)

    @pl.when(z > 0)
    def _():
        pl.semaphore_signal(barrier, inc=1, device_id={"rows": core_peer - 4}, device_id_type=MESH)

    @pl.when(z < depth - 1)
    def _():
        pl.semaphore_signal(barrier, inc=1, device_id={"rows": core_peer + 4}, device_id_type=MESH)

    mine = lax.axis_index("dirs")
    higher, lower = (mine + 1) % dir_count, (mine + dir_count - 1) % dir_count
    neighbours = (higher, lower) if dir_count > 2 else (higher,)
    for peer in neighbours:
        pl.semaphore_signal(barrier, inc=1, device_id={"dirs": peer}, device_id_type=MESH)

    order = [0] + list(range(chunks - 1, 0, -1))
    coupling_load = pltpu.make_async_copy(coupling_in, coupling, load_sem.at[0])
    sea_load = pltpu.make_async_copy(sea_in, sea_mask, load_sem.at[1])
    boundary_load = pltpu.make_async_copy(boundary_in, boundary, load_sem.at[2])
    previous_loads = [
        pltpu.make_async_copy(previous_in.at[part(j)], previous.at[part(j)], load_sem.at[3 + j])
        for j in range(chunks)
    ]
    sea_load.start()
    coupling_load.start()
    for j in order:
        previous_loads[j].start()
    boundary_load.start()
    for d in range(dirs):
        marks[d, 0:1] = jnp.full((1, marks.shape[2]), cross_gain[d], f32)
        marks[d, 1:2] = jnp.full((1, marks.shape[2]), quadrant[d].astype(f32), f32)
    def remote(src, dst, send, recv, peer):
        return pltpu.make_async_remote_copy(
            src_ref=src, dst_ref=dst, send_sem=send, recv_sem=recv,
            device_id={"rows": peer}, device_id_type=MESH,
        )

    gain_copies = [
        remote(gain, gains.at[i], gain_send.at[i], gain_recv.at[i], peer) for i, peer in enumerate(peers)
    ]
    core_copies = [
        remote(state.at[1 - half, :, part(j)], got_core.at[:, part(j)], core_send.at[j], core_recv.at[j], core_peer)
        for j in range(chunks)
    ]
    pair_copies = [
        remote(half_total.at[1 - x, part(j)], got_pair.at[part(j)], pair_send.at[j], pair_recv.at[j], pair_peer)
        for j in range(chunks)
    ]
    back_copies = [
        remote(pair_out.at[part(j)], pair_in.at[x, part(j)], back_send.at[j], back_recv.at[j], pair_peer)
        for j in range(chunks)
    ]
    last_copies = [
        remote(core_out.at[:, part(j)], out.at[half, :, part(j)], last_send.at[j], last_recv.at[j], core_peer)
        for j in range(chunks)
    ]

    flags = marks[:, 1:2, :]
    flags = flags - 2.0 * jnp.floor(0.5 * flags)
    back = jnp.concatenate([flags] * (gain.shape[-1] // flags.shape[-1]), axis=2)
    sea_load.wait()
    coupling_load.wait()
    sea = sea_mask[...].astype(f32)
    sea_field[...] = sea
    back_rows[...] = back
    for d in range(dirs):
        onward, onward_gain = row_weights(coupling[d], sea, False)
        against, _ = row_weights(coupling[d], sea, True)
        shares[d] = jnp.where(back[d] > 0.5, against, onward)
        gain[d] = onward_gain
    pl.semaphore_wait(
        barrier, 3 + len(neighbours) + (z > 0).astype(jnp.int32) + (z < depth - 1).astype(jnp.int32)
    )

    edge_copies = []
    for way, (peer, start) in enumerate(((lower, 0), (higher, dirs - SHIFT))):
        edge_copies.append(
            pltpu.make_async_remote_copy(
                src_ref=edge_state.at[way], dst_ref=halo_entering.at[way],
                send_sem=edge_send.at[way], recv_sem=edge_recv.at[way],
                device_id={"dirs": peer}, device_id_type=MESH,
            )
        )

    halo_copies = []
    for way, (peer, start, to) in enumerate(((lower, 0, SHIFT), (higher, dirs - SHIFT, 0))):
        bands = pl.ds(1 - way, previous.shape[1] - 1)
        for i, (src, dst) in enumerate(
            (
                (previous_in.at[pl.ds(start, SHIFT), bands], halo_previous.at[pl.ds(to, SHIFT), bands]),
                (marks.at[pl.ds(start, SHIFT)], halo_marks.at[pl.ds(to, SHIFT)]),
                (coupling_in.at[pl.ds(start, SHIFT)], halo_coupling.at[way]),
            )
        ):
            halo_copies.append(
                pltpu.make_async_remote_copy(
                    src_ref=src, dst_ref=dst,
                    send_sem=halo_send.at[way, i], recv_sem=halo_recv.at[way, i],
                    device_id={"dirs": peer}, device_id_type=MESH,
                )
            )
            halo_copies[-1].start()

    for copy in gain_copies:
        copy.start()

    def compose(h, d, _):
        share = shares[d]
        for q in range(2):
            values = previous[d, pl.ds((2 * h + q) * state.shape[3], state.shape[3])].astype(f32)
            state[h, q, d] = jnp.sum(values * share[None], axis=1)
        return 0

    for j in order:
        previous_loads[j].wait()
        lax.fori_loop(j * size, (j + 1) * size, functools.partial(compose, 1 - half), 0)
        core_copies[j].start()
    for j in order:
        lax.fori_loop(j * size, (j + 1) * size, functools.partial(compose, half), 0)
    boundary_load.wait()
    c_bit, x_bit = c.astype(f32), x.astype(f32)
    core_after = c_bit + back - 2.0 * c_bit * back
    pair_after = x_bit + back - 2.0 * x_bit * back
    for copy in gain_copies:
        copy.wait_recv()
    core_mine, core_theirs = gain[...], gains[0]
    pair_mine, pair_theirs = core_mine * core_theirs, gains[1] * gains[2]
    plane_gain = pair_mine * pair_theirs

    def total(after, mine, theirs):
        return after * mine + (1.0 - after), (1.0 - after) * theirs + after

    core_a, core_b = total(core_after, core_mine, core_theirs)
    pair_a, pair_b = total(pair_after, pair_mine, pair_theirs)

    def cut(v, j):
        return v[j * size : (j + 1) * size]

    for j in order:
        core_copies[j].wait_recv()
        half_total[:, part(j)] = (
            cut(core_a, j)[None] * got_core[:, part(j)] + cut(core_b, j)[None] * state[half, :, part(j)]
        )
        pair_copies[j].start()
    def local(d, _):
        side = jnp.where(marks[d, 1:2] > 1.5, 1.0, 0.0)
        local_sweep(
            previous.at[d], coupling.at[d], back_rows.at[d], side, sea_field, cumulated.at[d], settled.at[d]
        )
        return 0

    early = min(dirs, 7)
    at_end = (z == 0) | (z == depth - 1)
    middle = jnp.where(at_end, dirs, early)
    lax.fori_loop(0, early, local, 0)
    upper = (2 * z >= depth).astype(jnp.int32)
    mine_at = 2 * half + x

    def chain(j, way):
        step = 1 - 2 * way
        has_before = jnp.where(way == 0, z > 0, z < depth - 1)
        has_after = jnp.where(way == 0, z < depth - 1, z > 0)
        copy = remote(
            chain_out.at[way, part(j)], chain_in.at[way, part(j)],
            chain_send.at[way, j], chain_recv.at[way, j], core_peer + 4 * step,
        )

        @pl.when(has_before)
        def _():
            copy.wait_recv()

        @pl.when(jnp.logical_not(has_before))
        def _():
            chain_in[way, part(j)] = boundary[part(j), mine_at]

        @pl.when(has_after)
        def _():
            chain_out[way, part(j)] = cut(plane_gain, j) * chain_in[way, part(j)] + plane[part(j)]
            copy.start()

    def split(after, mine, theirs):
        return after * theirs + (1.0 - after), (1.0 - after) * mine + after

    pair_p, pair_q = split(pair_after, pair_mine, pair_theirs)
    core_p, core_q = split(core_after, core_mine, core_theirs)

    def leave(j):
        entering = jnp.where(cut(back, j) > 0.5, chain_in[1, part(j)], chain_in[0, part(j)])
        pair_out[part(j)] = cut(pair_q, j) * entering + (1.0 - cut(pair_after, j)) * half_total[x, part(j)]
        back_copies[j].start()
        pair_in[x, part(j)] = cut(pair_p, j) * entering + cut(pair_after, j) * got_pair[part(j)]

    def finish(j):
        back_copies[j].wait_recv()
        entering = pair_in[:, part(j)]
        core_out[:, part(j)] = (
            cut(core_q, j)[None] * entering + (1.0 - cut(core_after, j))[None] * state[half, :, part(j)]
        )
        last_copies[j].start()
        out[half, :, part(j)] = cut(core_p, j)[None] * entering + cut(core_after, j)[None] * got_core[:, part(j)]

    for i in range(2 * chunks + 2):
        if i == chunks:
            lax.fori_loop(early, middle, local, 0)
        if i < chunks:
            j = order[i]
            pair_copies[j].wait_recv()
            plane[part(j)] = cut(pair_a, j) * got_pair[part(j)] + cut(pair_b, j) * half_total[x, part(j)]
            chain(j, upper)
        if chunks <= i < 2 * chunks:
            chain(order[i - chunks], 1 - upper)
            leave(order[i - chunks])
        if chunks + 2 <= i:
            finish(order[i - chunks - 2])
    lax.fori_loop(middle, dirs, local, 0)
    def own_copy(j):
        return pltpu.make_async_copy(rounded.at[part(j)], own_out.at[part(j)], own_sem.at[j])

    def rest_copy(j):
        return pltpu.make_async_copy(rest.at[part(j)], rest_out.at[part(j)], rest_sem.at[j])

    def own(d, _):
        solve_free(
            out.at[:, :, d], inflow, cumulated.at[d], marks.at[d], sea_field, settled.at[d], rounded.at[d], rest.at[d]
        )
        return 0

    def chunk(i, _):
        j = (chunks - i) % chunks
        remote(
            core_out.at[:, part(j)], out.at[half, :, part(j)], last_send.at[j], last_recv.at[j], core_peer
        ).wait_recv()

        for way, (at, start) in enumerate(((0, 0), (chunks - 1, dirs - SHIFT))):

            @pl.when(j == at if size >= SHIFT else i == chunks - 1)
            def _(way=way, start=start):
                edge_state[way] = out[:, :, start : start + SHIFT].astype(bf16)
                edge_copies[way].start()

        lax.fori_loop(j * size, (j + 1) * size, own, 0)
        own_copy(j).start()
        rest_copy(j).start()
        return 0

    lax.fori_loop(0, chunks, chunk, 0)
    for j in range(chunks):
        own_copy(j).wait()
        rest_copy(j).wait()
    for copy in halo_copies + edge_copies:
        copy.wait_recv()
    for copy in halo_copies + edge_copies + gain_copies + core_copies + pair_copies + back_copies + last_copies:
        copy.wait_send()

    def drain(j, way):
        copy = remote(
            chain_out.at[way, part(j)], chain_in.at[way, part(j)],
            chain_send.at[way, j], chain_recv.at[way, j], core_peer + 4 * (1 - 2 * way),
        )

        @pl.when(z < depth - 1 if way == 0 else z > 0)
        def _():
            copy.wait_send()

    for j in range(chunks):
        drain(j, 0)
        drain(j, 1)


def scan_devices(
    count, dir_count, quadrant, cross_gain, boundary, sea_mask, previous, coupling
):
    dirs, bands, rows, columns = previous.shape
    chunks = 4 if dirs % 4 == 0 else 3 if dirs % 3 == 0 else 1
    quarter = bands // 4
    boundary = boundary.reshape(dirs, 4, quarter, columns)
    vmem = pl.BlockSpec(memory_space=pltpu.VMEM)
    smem = pl.BlockSpec(memory_space=pltpu.SMEM)
    part = (dirs, quarter, columns)
    dma = pltpu.SemaphoreType.DMA
    anywhere = pl.BlockSpec(memory_space=pl.ANY)
    hbm = pl.BlockSpec(memory_space=pltpu.HBM)
    marks = (dirs, 2, 128)

    def halo(a):
        return jax.ShapeDtypeStruct((2 * SHIFT,) + a.shape[1:], a.dtype)

    return pl.pallas_call(
        functools.partial(scan_kernel, count, dir_count, chunks),
        in_specs=[smem, smem] + [hbm] * 4,
        out_specs=[anywhere] * 6,
        out_shape=[
            jax.ShapeDtypeStruct(previous.shape, bf16),
            jax.ShapeDtypeStruct(previous.shape, bf16),
            halo(previous),
            jax.ShapeDtypeStruct((2, 2, 2, SHIFT, quarter, columns), bf16),
            jax.ShapeDtypeStruct((2, SHIFT, rows, columns), f32),
            jax.ShapeDtypeStruct((2 * SHIFT,) + marks[1:], f32),
        ],
        scratch_shapes=[
            pltpu.VMEM((2, 2) + part, f32),
            pltpu.VMEM(previous.shape, bf16),
            pltpu.VMEM((4, quarter, columns), f32),
            pltpu.VMEM((2, 2, 2, SHIFT, quarter, columns), bf16),
            pltpu.VMEM((dirs, 1, columns), f32),
            pltpu.VMEM(coupling.shape, f32),
            pltpu.VMEM(previous.shape, f32),
            pltpu.VMEM(previous.shape, bf16),
            pltpu.VMEM(sea_mask.shape, f32),
            pltpu.VMEM((dirs, 1, columns), f32),
            pltpu.VMEM((2, 2) + part, f32),
            pltpu.VMEM(coupling.shape, f32),
            pltpu.VMEM(marks, f32),
            pltpu.VMEM(boundary.shape, f32),
            pltpu.VMEM(sea_mask.shape, jnp.int32),
            pltpu.VMEM(previous.shape, bf16),
            pltpu.VMEM(coupling.shape, f32),
            pltpu.VMEM((3, dirs, 1, columns), f32),
            pltpu.VMEM((2,) + part, f32),
            pltpu.VMEM((2,) + part, f32),
            pltpu.VMEM(part, f32),
            pltpu.VMEM(part, f32),
            pltpu.VMEM((2,) + part, f32),
            pltpu.VMEM((2,) + part, f32),
            pltpu.VMEM((2,) + part, f32),
            pltpu.VMEM(part, f32),
            pltpu.VMEM((2,) + part, f32),
            dma((3 + chunks,)),
            dma((3,)), dma((3,)),
            dma((chunks,)), dma((chunks,)),
            dma((chunks,)), dma((chunks,)),
            dma((2, chunks)), dma((2, chunks)),
            dma((chunks,)), dma((chunks,)),
            dma((chunks,)), dma((chunks,)),
            dma((2, 3)), dma((2, 3)),
            dma((2,)), dma((2,)),
            dma((chunks,)), dma((chunks,)),
        ],
        compiler_params=pltpu.CompilerParams(
            collective_id=0, has_side_effects=True, vmem_limit_bytes=SCAN_VMEM
        ),
        cost_estimate=cost(30),
        name="scan_devices",
    )(quadrant, cross_gain, boundary, sea_mask, previous, coupling)


def spans_of(couple, backward):
    rows = couple.shape[0]
    order = visit_order(couple.shape, backward)
    spans, reach, span = [], couple, 1
    while span < rows:
        spans.append((span, jnp.where(order >= span, reach, 0.0)))
        reach = jnp.where(order >= span, reach * rolled(reach, span, backward), reach)
        span *= 2
    return spans, reach


def local_sweep(previous, coupling, back, side, sea, cumulated, local):
    bands, rows, columns = previous.shape
    pieces = columns // BLOCK

    def blocks(f, here, weight, ways, flag):
        start = weight * previous[f, :, here].astype(f32)
        values = []
        for backward in (False, True):
            value = start
            for span, factor in ways[backward][0]:
                value = value + factor * rolled(value, span, backward)
            values.append(value)
        return jnp.where(flag, values[1], values[0])

    shape = (rows, BLOCK)
    flag = jnp.broadcast_to(back[:, :BLOCK], shape) > 0.5
    sides = jnp.broadcast_to(side, shape) > 0.5
    for k in range(pieces // 2):
        pair = [slice(at * BLOCK, (at + 1) * BLOCK) for at in (k, pieces - 1 - k)]
        held = []
        for here in pair:
            couple, weight = weights(coupling[:, here], sea[:, here])
            ways = [spans_of(couple, backward) for backward in (False, True)]
            held.append((weight, ways, jnp.where(flag, ways[1][1], ways[0][1])))
        for at, here in enumerate(pair):
            cumulated[:, here] = jnp.where(sides, held[1 - at][2], held[at][2])
        for f in range(bands):
            values = [blocks(f, here, *held[at][:2], flag) for at, here in enumerate(pair)]
            for at, here in enumerate(pair):
                local[f, :, here] = jnp.where(sides, values[1 - at], values[at])


def solve_free(entering, inflow, cumulated, marks, sea, settled, rounded, rest):
    bands, rows, columns = settled.shape
    block = BLOCK
    quarter = bands // 4
    pieces = columns // block
    gains, corner = marks[0:1], marks[1:2]
    side = corner > 1.5
    slope, scale = jnp.log(gains / (1.0 + gains)), 1.0 / (1.0 + gains)
    row = lax.broadcasted_iota(jnp.int32, (block, block), 0)
    column = lax.broadcasted_iota(jnp.int32, (block, block), 1)
    sides = jnp.broadcast_to(side, (block, block))
    offset = jnp.where(sides, row - column, column - row)
    matrix = jnp.where(offset >= 0, jnp.exp(offset.astype(f32) * slope) * scale, 0.0)
    lane = lax.broadcasted_iota(jnp.int32, (1, block), 1)
    reach = jnp.where(side, block - 1 - lane, lane).astype(f32)
    carry = gains * scale * jnp.exp(reach * slope)
    carry_last = gains * scale * jnp.exp((block - 1) * slope)
    high = matrix.astype(bf16)
    low = (matrix - high.astype(f32)).astype(bf16)
    whole = jnp.concatenate(
        [
            jnp.concatenate([high, low], axis=1),
            jnp.concatenate([high, jnp.zeros_like(low)], axis=1),
        ],
        axis=0,
    )
    pairs = [
        [slice(at * block, (at + 1) * block) for at in (k, pieces - 1 - k)] for k in range(pieces // 2)
    ]
    flip = jnp.broadcast_to(side, (quarter, block))
    for q in range(4):
        for pair in pairs:
            values = [entering[q // 2, q % 2, :, here] for here in pair]
            for at, here in enumerate(pair):
                inflow[q, :, here] = jnp.where(flip, values[1 - at], values[at])
    before = None
    for k in range(pieces):
        here = slice(k * block, (k + 1) * block)
        growth = cumulated[:, here]
        x = jnp.concatenate(
            [
                settled[f, :, here] + growth * inflow[f // quarter, f % quarter : f % quarter + 1, here]
                for f in range(bands)
            ],
            axis=0,
        )
        upper = x.astype(bf16)
        lower = (x - upper.astype(f32)).astype(bf16)
        both = jnp.dot(
            jnp.concatenate([upper, lower], axis=1), whole, preferred_element_type=f32
        )
        y = both[:, :block] + both[:, block:]
        if k < pieces - 1:
            last = jnp.where(
                jnp.broadcast_to(side, y.shape),
                jnp.broadcast_to(y[:, :1], y.shape),
                jnp.broadcast_to(y[:, block - 1 :], y.shape),
            )
        if before is not None:
            y = y + before * carry
            last = last + before * carry_last
        before = last
        settled[:, :, here] = y.reshape(bands, rows, block)
    flip = jnp.broadcast_to(side, (rows, block))
    for pair in pairs:
        field = [sea[:, here] for here in pair]
        for f in range(bands):
            values = [settled[f, :, here] for here in pair]
            for at, here in enumerate(pair):
                masked = jnp.where(flip, values[1 - at], values[at]) * field[at]
                near = masked.astype(bf16)
                rounded[f, :, here] = near
                rest[f, :, here] = (masked - near.astype(f32)).astype(bf16)


def settle_one(previous, coupling, inflow_of, gain, sea, rounded, settled, backward, sideways):
    bands, rows, columns = previous.shape
    block = BLOCK
    quarter = bands // 4
    pieces = columns // block
    gains = jnp.full((1, block), gain, f32)
    slope, scale = jnp.log(gains / (1.0 + gains)), 1.0 / (1.0 + gains)
    row = lax.broadcasted_iota(jnp.int32, (block, block), 0)
    column = lax.broadcasted_iota(jnp.int32, (block, block), 1)
    offset = row - column if sideways else column - row
    matrix = jnp.where(offset >= 0, jnp.exp(offset.astype(f32) * slope) * scale, 0.0)
    carry = gains * (matrix[block - 1 :] if sideways else matrix[:1])
    carry_last = carry[:, :1] if sideways else carry[:, block - 1 :]
    high = matrix.astype(bf16)
    low = (matrix - high.astype(f32)).astype(bf16)
    whole = jnp.concatenate(
        [
            jnp.concatenate([high, low], axis=1),
            jnp.concatenate([high, jnp.zeros_like(low)], axis=1),
        ],
        axis=0,
    )
    order = visit_order((rows, block), backward)
    before = None
    for k in range(pieces - 1, -1, -1) if sideways else range(pieces):
        here = slice(k * block, (k + 1) * block)
        couple, weight = weights(coupling[:, here], sea[:, here])
        first = jnp.where(order == 0, couple, 0.0)
        spans, reach, span = [], couple, 1
        while span < rows:
            spans.append((span, jnp.where(order >= span, reach, 0.0)))
            reach = jnp.where(order >= span, reach * rolled(reach, span, backward), reach)
            span *= 2
        values = []
        for f in range(bands):
            value = weight * previous[f, :, here].astype(f32) + first * inflow_of(
                f // quarter, f % quarter, here
            )
            for span, factor in spans:
                value = value + factor * rolled(value, span, backward)
            values.append(value)
        x = jnp.concatenate(values, axis=0)
        upper = x.astype(bf16)
        lower = (x - upper.astype(f32)).astype(bf16)
        both = jnp.dot(
            jnp.concatenate([upper, lower], axis=1), whole, preferred_element_type=f32
        )
        y = both[:, :block] + both[:, block:]
        last = jnp.broadcast_to(y[:, :1] if sideways else y[:, block - 1 :], y.shape)
        if before is not None:
            y = y + before * carry
            last = last + before * carry_last
        before = last
        masked = y.reshape(bands, rows, block) * sea[:, here][None]
        rounded[:, :, here] = masked.astype(bf16)
        if settled is not None:
            settled[:, :, here] = masked


def settle(previous, coupling, inflow_of, corner, gain, sea, rounded, settled):
    for flag in range(4):
        pl.when(corner == flag)(
            functools.partial(
                settle_one, previous, coupling, inflow_of, gain, sea, rounded, settled,
                flag % 2 == 1, flag // 2 == 1,
            )
        )


def wet_field(wet_columns, wet):
    rows, columns = wet.shape
    row = lax.broadcasted_iota(jnp.int32, (rows, rows), 0)
    column = lax.broadcasted_iota(jnp.int32, (rows, rows), 1)
    for k in range(columns // BLOCK):
        flags = jnp.broadcast_to(wet_columns[k : k + 1].astype(f32), (rows, rows))
        flag = jnp.sum(jnp.where(row == column, flags, 0.0), axis=1, keepdims=True)
        wet[:, k * BLOCK : (k + 1) * BLOCK] = jnp.broadcast_to(flag, (rows, BLOCK))


def source(coef, own, onward_of, against_of, rest, wet, result):
    bands = own.shape[0]
    wet_cells = wet[...]

    def one(f, onward, against):
        energy = own[f].astype(f32)
        value = coef[f] * (
            energy * energy * (onward + against) - 2.0 * energy * onward * against
        )
        base = energy + rest[f].astype(f32)
        result[f] = (base + wet_cells * value.astype(bf16).astype(f32)).astype(bf16)

    def above(f):
        return onward_of[f + 1].astype(f32)

    def below(f):
        return against_of[f - 1].astype(f32)

    nothing = jnp.zeros(wet.shape, f32)
    one(0, above(0), nothing)
    one(bands - 1, nothing, below(bands - 1))

    def body(f, _):
        one(f, above(f), below(f))
        return 0

    lax.fori_loop(1, bands - 1, body, 0, unroll=True)


def source_kernel(
    marks_in, coef_in, sea_in, wet_in, previous_in, entering_in, coupling_in, own_in, rest_in,
    out, halo_marks, coef, previous, incoming, entering, coupling, own, rest, halo, sea_mask, wet_tiles, sea, wet, result,
    load_sem, scalar_sem, store_sem,
):
    dirs, bands, rows, columns = own.shape
    scalars = [
        pltpu.make_async_copy(marks_in, halo_marks, scalar_sem.at[0]),
        pltpu.make_async_copy(coef_in, coef, scalar_sem.at[1]),
    ]
    small = [
        pltpu.make_async_copy(src, dst, load_sem.at[i])
        for i, (src, dst) in enumerate(
            ((sea_in, sea_mask), (wet_in, wet_tiles), (coupling_in, coupling), (entering_in, incoming))
        )
    ]
    previous_load = pltpu.make_async_copy(previous_in, previous, load_sem.at[4])
    cut = dirs // 2 if dirs > 2 * SHIFT else dirs
    late = [
        pltpu.make_async_copy(whole.at[pl.ds(0, to)], held.at[pl.ds(0, to)], load_sem.at[i])
        for i, (whole, held, to) in enumerate(((own_in, own, min(cut + SHIFT, dirs)), (rest_in, rest, cut)), 5)
    ]
    latest = [
        pltpu.make_async_copy(whole.at[pl.ds(at, dirs - at)], held.at[pl.ds(at, dirs - at)], load_sem.at[i])
        for i, (whole, held, at) in enumerate(((own_in, own, cut + SHIFT), (rest_in, rest, cut)), 7)
        if at < dirs
    ]
    if dirs > 2 * SHIFT:
        bounds = [0, SHIFT, dirs // 2, dirs - SHIFT, dirs - 1, dirs]
    else:
        bounds = list(range(dirs + 1))
    stores = [
        pltpu.make_async_copy(
            result.at[pl.ds(at, to - at)], out.at[pl.ds(at, to - at)], store_sem.at[k]
        )
        for k, (at, to) in enumerate(zip(bounds, bounds[1:]))
    ]
    for load in small + scalars:
        load.start()
    for load in [previous_load] + late + latest:
        load.start()
    for load in small + scalars:
        load.wait()
    sea[...] = sea_mask[...].astype(f32)
    wet_field(wet_tiles, wet)
    entering[...] = incoming[...].astype(f32)

    def one_halo(t, _):
        way, at = 1 - t // SHIFT, t % SHIFT
        settle(
            previous.at[t], coupling.at[way, at],
            lambda q, r, here: entering[way, q // 2, q % 2, at, r : r + 1, here],
            halo_marks[t, 1, 0].astype(jnp.int32), halo_marks[t, 0, 0], sea, halo.at[t], None,
        )
        return 0

    previous_load.wait()
    lax.fori_loop(0, 2 * SHIFT, one_halo, 0)
    for load in late:
        load.wait()

    def inner(d, _):
        source(
            coef, own.at[d], own.at[d + SHIFT], own.at[d - SHIFT], rest.at[d], wet, result.at[d]
        )
        return 0

    for store, at, to in zip(stores, bounds, bounds[1:]):
        if at == cut:
            for load in latest:
                load.wait()
        if at >= SHIFT and to <= dirs - SHIFT:
            lax.fori_loop(at, to, inner, 0)
        else:
            for d in range(at, to):
                source(
                    coef, own.at[d],
                    own.at[d + SHIFT] if d + SHIFT < dirs else halo.at[2 * SHIFT + d - dirs],
                    own.at[d - SHIFT] if d >= SHIFT else halo.at[d],
                    rest.at[d], wet, result.at[d],
                )
        store.start()
    for store in stores:
        store.wait()


def add_source(
    halo_marks, quad_coef, sea_mask, wet_tiles, halo_previous, halo_entering, halo_coupling, own, rest
):
    dirs, bands, rows, columns = own.shape
    anywhere = pl.BlockSpec(memory_space=pl.ANY)
    dma = pltpu.SemaphoreType.DMA
    return pl.pallas_call(
        source_kernel,
        in_specs=[anywhere] * 9,
        out_specs=anywhere,
        out_shape=jax.ShapeDtypeStruct(own.shape, bf16),
        scratch_shapes=[
            pltpu.SMEM(halo_marks.shape, f32),
            pltpu.SMEM(quad_coef.shape, f32),
            pltpu.VMEM(halo_previous.shape, bf16),
            pltpu.VMEM(halo_entering.shape, bf16),
            pltpu.VMEM(halo_entering.shape, f32),
            pltpu.VMEM(halo_coupling.shape, f32),
            pltpu.VMEM(own.shape, bf16),
            pltpu.VMEM(own.shape, bf16),
            pltpu.VMEM(halo_previous.shape, bf16),
            pltpu.VMEM(sea_mask.shape, jnp.int32),
            pltpu.VMEM(wet_tiles.shape, jnp.int32),
            pltpu.VMEM((rows, columns), f32),
            pltpu.VMEM((rows, columns), f32),
            pltpu.VMEM(own.shape, bf16),
            dma((9,)), dma((2,)), dma((max(dirs, 5),)),
        ],
        compiler_params=pltpu.CompilerParams(vmem_limit_bytes=STEP_VMEM),
        cost_estimate=cost(6),
        name="add_source",
    )(halo_marks, quad_coef, sea_mask, wet_tiles, halo_previous, halo_entering, halo_coupling, own, rest)


def on_device(
    row_devices, dir_devices,
    previous, boundary, row_coupling, cross_gain, block_inverse, quadrant, sea_mask, wet_tiles, quad_coef,
):
    wet_tiles = wet_tiles.T
    own, rest, halo_previous, halo_entering, halo_coupling, halo_marks = scan_devices(
        row_devices, dir_devices, quadrant, cross_gain, boundary, sea_mask, previous, row_coupling
    )
    return add_source(
        halo_marks, quad_coef, sea_mask, wet_tiles, halo_previous, halo_entering, halo_coupling, own, rest
    )


def solution(mesh):
    in_specs = (
        P("dirs", None, "rows", None),
        P("dirs", None, None),
        P("dirs", "rows", None),
        P("dirs"),
        P("dirs", None, None),
        P("dirs"),
        P("rows", None),
        P("rows", None),
        P(),
    )
    out_specs = P("dirs", None, "rows", None)
    return jax.shard_map(
        functools.partial(on_device, mesh.shape["rows"], mesh.shape["dirs"]),
        mesh=mesh, in_specs=in_specs, out_specs=out_specs, check_vma=False,
    )
```

```python
import functools

import jax
import jax.numpy as jnp
from jax import lax
from jax.experimental import pallas as pl
from jax.experimental.pallas import tpu as pltpu
from jax.sharding import PartitionSpec as P

SHIFT = 2
f32 = jnp.float32
bf16 = jnp.bfloat16
MESH = pl.DeviceIdType.MESH
SCAN_VMEM = 56 * 1024 * 1024
STEP_VMEM = 56 * 1024 * 1024
BLOCK = 128


def cost(microseconds):
    return pl.CostEstimate(
        flops=0, bytes_accessed=int(microseconds * 3_000_000), transcendentals=0
    )


def weights(coupling, sea):
    return coupling * sea, sea * (1.0 - coupling)


def visit_order(shape, backward):
    row = lax.broadcasted_iota(jnp.int32, shape, 0)
    return shape[0] - 1 - row if backward else row


def rolled(x, steps, backward):
    rows = x.shape[0]
    return pltpu.roll(x, (rows - steps if backward else steps) % rows, 0)


def row_weights(coupling, sea, backward):
    couple, weight = weights(coupling, sea)
    rows = couple.shape[0]
    order = visit_order(couple.shape, backward)
    after = jnp.where(order < rows - 1, rolled(couple, rows - 1, backward), 1.0)
    span = 1
    while span < rows - 1:
        after = after * jnp.where(order < rows - span, rolled(after, rows - span, backward), 1.0)
        span *= 2
    gain = jnp.sum(jnp.where(order == 0, couple * after, 0.0), axis=0, keepdims=True)
    return weight * after, gain


def scan_kernel(
    count, dir_count, chunks, quadrant_in, cross_gain_in, boundary_in, sea_in, previous_in, coupling_in,
    own_out, rest_out, halo_previous, halo_entering, halo_coupling, halo_marks,
    quadrant, cross_gain, out, rest, inflow, edge_state, back_rows, cumulated, settled, rounded, sea_field,
    gain, state, shares, marks, boundary, sea_mask, previous, coupling,
    gains, got_core, half_total, got_pair, plane, chain_in, chain_out, pair_in, pair_out, core_out,
    load_sem, gain_send, gain_recv, core_send, core_recv, pair_send, pair_recv,
    chain_send, chain_recv, back_send, back_recv, last_send, last_recv, halo_send, halo_recv,
    edge_send, edge_recv, own_sem, rest_sem,
):
    me = lax.axis_index("rows")
    c, x, z = me % 2, (me // 2) % 2, me // 4
    depth = count // 4
    half = (c + x + z) % 2
    core_peer = me + 1 - 2 * c
    side_peer = me + 2 - 4 * x
    pair_peer = core_peer + 2 - 4 * x
    dirs = gain.shape[0]
    size = dirs // chunks
    peers = (core_peer, side_peer, pair_peer)

    def part(j):
        return pl.ds(j * size, size)

    barrier = pltpu.get_barrier_semaphore()
    for peer in peers:
        pl.semaphore_signal(barrier, inc=1, device_id={"rows": peer}, device_id_type=MESH)

    @pl.when(z > 0)
    def _():
        pl.semaphore_signal(barrier, inc=1, device_id={"rows": core_peer - 4}, device_id_type=MESH)

    @pl.when(z < depth - 1)
    def _():
        pl.semaphore_signal(barrier, inc=1, device_id={"rows": core_peer + 4}, device_id_type=MESH)

    mine = lax.axis_index("dirs")
    higher, lower = (mine + 1) % dir_count, (mine + dir_count - 1) % dir_count
    neighbours = (higher, lower) if dir_count > 2 else (higher,)
    for peer in neighbours:
        pl.semaphore_signal(barrier, inc=1, device_id={"dirs": peer}, device_id_type=MESH)

    order = [0] + list(range(chunks - 1, 0, -1))
    coupling_load = pltpu.make_async_copy(coupling_in, coupling, load_sem.at[0])
    sea_load = pltpu.make_async_copy(sea_in, sea_mask, load_sem.at[1])
    boundary_load = pltpu.make_async_copy(boundary_in, boundary, load_sem.at[2])
    previous_loads = [
        pltpu.make_async_copy(previous_in.at[part(j)], previous.at[part(j)], load_sem.at[3 + j])
        for j in range(chunks)
    ]
    scalar_loads = [
        pltpu.make_async_copy(quadrant_in, quadrant, load_sem.at[3 + chunks]),
        pltpu.make_async_copy(cross_gain_in, cross_gain, load_sem.at[4 + chunks]),
    ]
    for load in scalar_loads:
        load.start()
    sea_load.start()
    coupling_load.start()
    for j in order:
        previous_loads[j].start()
    boundary_load.start()
    for load in scalar_loads:
        load.wait()
    for d in range(dirs):
        marks[d, 0:1] = jnp.full((1, marks.shape[2]), cross_gain[d], f32)
        marks[d, 1:2] = jnp.full((1, marks.shape[2]), quadrant[d].astype(f32), f32)
    def remote(src, dst, send, recv, peer):
        return pltpu.make_async_remote_copy(
            src_ref=src, dst_ref=dst, send_sem=send, recv_sem=recv,
            device_id={"rows": peer}, device_id_type=MESH,
        )

    gain_copies = [
        remote(gain, gains.at[i], gain_send.at[i], gain_recv.at[i], peer) for i, peer in enumerate(peers)
    ]
    core_copies = [
        remote(state.at[1 - half, :, part(j)], got_core.at[:, part(j)], core_send.at[j], core_recv.at[j], core_peer)
        for j in range(chunks)
    ]
    pair_copies = [
        remote(half_total.at[1 - x, part(j)], got_pair.at[part(j)], pair_send.at[j], pair_recv.at[j], pair_peer)
        for j in range(chunks)
    ]
    back_copies = [
        remote(pair_out.at[part(j)], pair_in.at[x, part(j)], back_send.at[j], back_recv.at[j], pair_peer)
        for j in range(chunks)
    ]
    last_copies = [
        remote(core_out.at[:, part(j)], out.at[half, :, part(j)], last_send.at[j], last_recv.at[j], core_peer)
        for j in range(chunks)
    ]

    flags = marks[:, 1:2, :]
    flags = flags - 2.0 * jnp.floor(0.5 * flags)
    back = jnp.concatenate([flags] * (gain.shape[-1] // flags.shape[-1]), axis=2)
    sea_load.wait()
    coupling_load.wait()
    sea = sea_mask[...].astype(f32)
    sea_field[...] = sea
    back_rows[...] = back
    for d in range(dirs):
        onward, onward_gain = row_weights(coupling[d], sea, False)
        against, _ = row_weights(coupling[d], sea, True)
        shares[d] = jnp.where(back[d] > 0.5, against, onward)
        gain[d] = onward_gain
    pl.semaphore_wait(
        barrier, 3 + len(neighbours) + (z > 0).astype(jnp.int32) + (z < depth - 1).astype(jnp.int32)
    )

    edge_copies = []
    for way, (peer, start) in enumerate(((lower, 0), (higher, dirs - SHIFT))):
        edge_copies.append(
            pltpu.make_async_remote_copy(
                src_ref=edge_state.at[way], dst_ref=halo_entering.at[way],
                send_sem=edge_send.at[way], recv_sem=edge_recv.at[way],
                device_id={"dirs": peer}, device_id_type=MESH,
            )
        )

    halo_copies = []
    for way, (peer, start, to) in enumerate(((lower, 0, SHIFT), (higher, dirs - SHIFT, 0))):
        bands = pl.ds(1 - way, previous.shape[1] - 1)
        for i, (src, dst) in enumerate(
            (
                (previous_in.at[pl.ds(start, SHIFT), bands], halo_previous.at[pl.ds(to, SHIFT), bands]),
                (marks.at[pl.ds(start, SHIFT)], halo_marks.at[pl.ds(to, SHIFT)]),
                (coupling_in.at[pl.ds(start, SHIFT)], halo_coupling.at[way]),
            )
        ):
            halo_copies.append(
                pltpu.make_async_remote_copy(
                    src_ref=src, dst_ref=dst,
                    send_sem=halo_send.at[way, i], recv_sem=halo_recv.at[way, i],
                    device_id={"dirs": peer}, device_id_type=MESH,
                )
            )
            halo_copies[-1].start()

    for copy in gain_copies:
        copy.start()

    def compose(h, d, _):
        share = shares[d]
        for q in range(2):
            values = previous[d, pl.ds((2 * h + q) * state.shape[3], state.shape[3])].astype(f32)
            state[h, q, d] = jnp.sum(values * share[None], axis=1)
        return 0

    for j in order:
        previous_loads[j].wait()
        lax.fori_loop(j * size, (j + 1) * size, functools.partial(compose, 1 - half), 0)
        core_copies[j].start()
    for j in order:
        lax.fori_loop(j * size, (j + 1) * size, functools.partial(compose, half), 0)
    boundary_load.wait()
    c_bit, x_bit = c.astype(f32), x.astype(f32)
    core_after = c_bit + back - 2.0 * c_bit * back
    pair_after = x_bit + back - 2.0 * x_bit * back
    for copy in gain_copies:
        copy.wait_recv()
    core_mine, core_theirs = gain[...], gains[0]
    pair_mine, pair_theirs = core_mine * core_theirs, gains[1] * gains[2]
    plane_gain = pair_mine * pair_theirs

    def total(after, mine, theirs):
        return after * mine + (1.0 - after), (1.0 - after) * theirs + after

    core_a, core_b = total(core_after, core_mine, core_theirs)
    pair_a, pair_b = total(pair_after, pair_mine, pair_theirs)

    def cut(v, j):
        return v[j * size : (j + 1) * size]

    for j in order:
        core_copies[j].wait_recv()
        half_total[:, part(j)] = (
            cut(core_a, j)[None] * got_core[:, part(j)] + cut(core_b, j)[None] * state[half, :, part(j)]
        )
        pair_copies[j].start()
    def local(d, _):
        side = jnp.where(marks[d, 1:2] > 1.5, 1.0, 0.0)
        local_sweep(
            previous.at[d], coupling.at[d], back_rows.at[d], side, sea_field, cumulated.at[d], settled.at[d]
        )
        return 0

    early = min(dirs, 7)
    at_end = (z == 0) | (z == depth - 1)
    middle = jnp.where(at_end, dirs, early)
    lax.fori_loop(0, early, local, 0)
    upper = (2 * z >= depth).astype(jnp.int32)
    mine_at = 2 * half + x

    def chain(j, way):
        step = 1 - 2 * way
        has_before = jnp.where(way == 0, z > 0, z < depth - 1)
        has_after = jnp.where(way == 0, z < depth - 1, z > 0)
        copy = remote(
            chain_out.at[way, part(j)], chain_in.at[way, part(j)],
            chain_send.at[way, j], chain_recv.at[way, j], core_peer + 4 * step,
        )

        @pl.when(has_before)
        def _():
            copy.wait_recv()

        @pl.when(jnp.logical_not(has_before))
        def _():
            chain_in[way, part(j)] = boundary[part(j), mine_at]

        @pl.when(has_after)
        def _():
            chain_out[way, part(j)] = cut(plane_gain, j) * chain_in[way, part(j)] + plane[part(j)]
            copy.start()

    def split(after, mine, theirs):
        return after * theirs + (1.0 - after), (1.0 - after) * mine + after

    pair_p, pair_q = split(pair_after, pair_mine, pair_theirs)
    core_p, core_q = split(core_after, core_mine, core_theirs)

    def leave(j):
        entering = jnp.where(cut(back, j) > 0.5, chain_in[1, part(j)], chain_in[0, part(j)])
        pair_out[part(j)] = cut(pair_q, j) * entering + (1.0 - cut(pair_after, j)) * half_total[x, part(j)]
        back_copies[j].start()
        pair_in[x, part(j)] = cut(pair_p, j) * entering + cut(pair_after, j) * got_pair[part(j)]

    def finish(j):
        back_copies[j].wait_recv()
        entering = pair_in[:, part(j)]
        core_out[:, part(j)] = (
            cut(core_q, j)[None] * entering + (1.0 - cut(core_after, j))[None] * state[half, :, part(j)]
        )
        last_copies[j].start()
        out[half, :, part(j)] = cut(core_p, j)[None] * entering + cut(core_after, j)[None] * got_core[:, part(j)]

    for i in range(2 * chunks + 2):
        if i == chunks:
            lax.fori_loop(early, middle, local, 0)
        if i < chunks:
            j = order[i]
            pair_copies[j].wait_recv()
            plane[part(j)] = cut(pair_a, j) * got_pair[part(j)] + cut(pair_b, j) * half_total[x, part(j)]
            chain(j, upper)
        if chunks <= i < 2 * chunks:
            chain(order[i - chunks], 1 - upper)
            leave(order[i - chunks])
        if chunks + 2 <= i:
            finish(order[i - chunks - 2])
    lax.fori_loop(middle, dirs, local, 0)
    def own_copy(j):
        return pltpu.make_async_copy(rounded.at[part(j)], own_out.at[part(j)], own_sem.at[j])

    def rest_copy(j):
        return pltpu.make_async_copy(rest.at[part(j)], rest_out.at[part(j)], rest_sem.at[j])

    def own(d, _):
        solve_free(
            out.at[:, :, d], inflow, cumulated.at[d], marks.at[d], sea_field, settled.at[d], rounded.at[d], rest.at[d]
        )
        return 0

    def chunk(i, _):
        j = (chunks - i) % chunks
        remote(
            core_out.at[:, part(j)], out.at[half, :, part(j)], last_send.at[j], last_recv.at[j], core_peer
        ).wait_recv()

        for way, (at, start) in enumerate(((0, 0), (chunks - 1, dirs - SHIFT))):

            @pl.when(j == at if size >= SHIFT else i == chunks - 1)
            def _(way=way, start=start):
                edge_state[way] = out[:, :, start : start + SHIFT].astype(bf16)
                edge_copies[way].start()

        lax.fori_loop(j * size, (j + 1) * size, own, 0)
        own_copy(j).start()
        rest_copy(j).start()
        return 0

    lax.fori_loop(0, chunks, chunk, 0)
    for j in range(chunks):
        own_copy(j).wait()
        rest_copy(j).wait()
    for copy in halo_copies + edge_copies:
        copy.wait_recv()
    for copy in halo_copies + edge_copies + gain_copies + core_copies + pair_copies + back_copies + last_copies:
        copy.wait_send()

    def drain(j, way):
        copy = remote(
            chain_out.at[way, part(j)], chain_in.at[way, part(j)],
            chain_send.at[way, j], chain_recv.at[way, j], core_peer + 4 * (1 - 2 * way),
        )

        @pl.when(z < depth - 1 if way == 0 else z > 0)
        def _():
            copy.wait_send()

    for j in range(chunks):
        drain(j, 0)
        drain(j, 1)


def scan_devices(
    count, dir_count, quadrant, cross_gain, boundary, sea_mask, previous, coupling
):
    dirs, bands, rows, columns = previous.shape
    chunks = 4 if dirs % 4 == 0 else 3 if dirs % 3 == 0 else 1
    quarter = bands // 4
    boundary = boundary.reshape(dirs, 4, quarter, columns)
    vmem = pl.BlockSpec(memory_space=pltpu.VMEM)
    part = (dirs, quarter, columns)
    dma = pltpu.SemaphoreType.DMA
    anywhere = pl.BlockSpec(memory_space=pl.ANY)
    hbm = pl.BlockSpec(memory_space=pltpu.HBM)
    marks = (dirs, 2, 128)

    def halo(a):
        return jax.ShapeDtypeStruct((2 * SHIFT,) + a.shape[1:], a.dtype)

    return pl.pallas_call(
        functools.partial(scan_kernel, count, dir_count, chunks),
        in_specs=[hbm] * 6,
        out_specs=[anywhere] * 6,
        out_shape=[
            jax.ShapeDtypeStruct(previous.shape, bf16),
            jax.ShapeDtypeStruct(previous.shape, bf16),
            halo(previous),
            jax.ShapeDtypeStruct((2, 2, 2, SHIFT, quarter, columns), bf16),
            jax.ShapeDtypeStruct((2, SHIFT, rows, columns), f32),
            jax.ShapeDtypeStruct((2 * SHIFT,) + marks[1:], f32),
        ],
        scratch_shapes=[
            pltpu.SMEM((dirs,), jnp.int32),
            pltpu.SMEM((dirs,), f32),
            pltpu.VMEM((2, 2) + part, f32),
            pltpu.VMEM(previous.shape, bf16),
            pltpu.VMEM((4, quarter, columns), f32),
            pltpu.VMEM((2, 2, 2, SHIFT, quarter, columns), bf16),
            pltpu.VMEM((dirs, 1, columns), f32),
            pltpu.VMEM(coupling.shape, f32),
            pltpu.VMEM(previous.shape, f32),
            pltpu.VMEM(previous.shape, bf16),
            pltpu.VMEM(sea_mask.shape, f32),
            pltpu.VMEM((dirs, 1, columns), f32),
            pltpu.VMEM((2, 2) + part, f32),
            pltpu.VMEM(coupling.shape, f32),
            pltpu.VMEM(marks, f32),
            pltpu.VMEM(boundary.shape, f32),
            pltpu.VMEM(sea_mask.shape, jnp.int32),
            pltpu.VMEM(previous.shape, bf16),
            pltpu.VMEM(coupling.shape, f32),
            pltpu.VMEM((3, dirs, 1, columns), f32),
            pltpu.VMEM((2,) + part, f32),
            pltpu.VMEM((2,) + part, f32),
            pltpu.VMEM(part, f32),
            pltpu.VMEM(part, f32),
            pltpu.VMEM((2,) + part, f32),
            pltpu.VMEM((2,) + part, f32),
            pltpu.VMEM((2,) + part, f32),
            pltpu.VMEM(part, f32),
            pltpu.VMEM((2,) + part, f32),
            dma((5 + chunks,)),
            dma((3,)), dma((3,)),
            dma((chunks,)), dma((chunks,)),
            dma((chunks,)), dma((chunks,)),
            dma((2, chunks)), dma((2, chunks)),
            dma((chunks,)), dma((chunks,)),
            dma((chunks,)), dma((chunks,)),
            dma((2, 3)), dma((2, 3)),
            dma((2,)), dma((2,)),
            dma((chunks,)), dma((chunks,)),
        ],
        compiler_params=pltpu.CompilerParams(
            collective_id=0, has_side_effects=True, vmem_limit_bytes=SCAN_VMEM
        ),
        cost_estimate=cost(30),
        name="scan_devices",
    )(quadrant, cross_gain, boundary, sea_mask, previous, coupling)


def spans_of(couple, backward):
    rows = couple.shape[0]
    order = visit_order(couple.shape, backward)
    spans, reach, span = [], couple, 1
    while span < rows:
        spans.append((span, jnp.where(order >= span, reach, 0.0)))
        reach = jnp.where(order >= span, reach * rolled(reach, span, backward), reach)
        span *= 2
    return spans, reach


def local_sweep(previous, coupling, back, side, sea, cumulated, local):
    bands, rows, columns = previous.shape
    pieces = columns // BLOCK

    def blocks(f, here, weight, ways, flag):
        start = weight * previous[f, :, here].astype(f32)
        values = []
        for backward in (False, True):
            value = start
            for span, factor in ways[backward][0]:
                value = value + factor * rolled(value, span, backward)
            values.append(value)
        return jnp.where(flag, values[1], values[0])

    shape = (rows, BLOCK)
    flag = jnp.broadcast_to(back[:, :BLOCK], shape) > 0.5
    sides = jnp.broadcast_to(side, shape) > 0.5
    for k in range(pieces // 2):
        pair = [slice(at * BLOCK, (at + 1) * BLOCK) for at in (k, pieces - 1 - k)]
        held = []
        for here in pair:
            couple, weight = weights(coupling[:, here], sea[:, here])
            ways = [spans_of(couple, backward) for backward in (False, True)]
            held.append((weight, ways, jnp.where(flag, ways[1][1], ways[0][1])))
        for at, here in enumerate(pair):
            cumulated[:, here] = jnp.where(sides, held[1 - at][2], held[at][2])
        for f in range(bands):
            values = [blocks(f, here, *held[at][:2], flag) for at, here in enumerate(pair)]
            for at, here in enumerate(pair):
                local[f, :, here] = jnp.where(sides, values[1 - at], values[at])


def solve_free(entering, inflow, cumulated, marks, sea, settled, rounded, rest):
    bands, rows, columns = settled.shape
    block = BLOCK
    quarter = bands // 4
    pieces = columns // block
    gains, corner = marks[0:1], marks[1:2]
    side = corner > 1.5
    slope, scale = jnp.log(gains / (1.0 + gains)), 1.0 / (1.0 + gains)
    row = lax.broadcasted_iota(jnp.int32, (block, block), 0)
    column = lax.broadcasted_iota(jnp.int32, (block, block), 1)
    sides = jnp.broadcast_to(side, (block, block))
    offset = jnp.where(sides, row - column, column - row)
    matrix = jnp.where(offset >= 0, jnp.exp(offset.astype(f32) * slope) * scale, 0.0)
    lane = lax.broadcasted_iota(jnp.int32, (1, block), 1)
    reach = jnp.where(side, block - 1 - lane, lane).astype(f32)
    carry = gains * scale * jnp.exp(reach * slope)
    carry_last = gains * scale * jnp.exp((block - 1) * slope)
    high = matrix.astype(bf16)
    low = (matrix - high.astype(f32)).astype(bf16)
    whole = jnp.concatenate(
        [
            jnp.concatenate([high, low], axis=1),
            jnp.concatenate([high, jnp.zeros_like(low)], axis=1),
        ],
        axis=0,
    )
    pairs = [
        [slice(at * block, (at + 1) * block) for at in (k, pieces - 1 - k)] for k in range(pieces // 2)
    ]
    flip = jnp.broadcast_to(side, (quarter, block))
    for q in range(4):
        for pair in pairs:
            values = [entering[q // 2, q % 2, :, here] for here in pair]
            for at, here in enumerate(pair):
                inflow[q, :, here] = jnp.where(flip, values[1 - at], values[at])
    before = None
    for k in range(pieces):
        here = slice(k * block, (k + 1) * block)
        growth = cumulated[:, here]
        x = jnp.concatenate(
            [
                settled[f, :, here] + growth * inflow[f // quarter, f % quarter : f % quarter + 1, here]
                for f in range(bands)
            ],
            axis=0,
        )
        upper = x.astype(bf16)
        lower = (x - upper.astype(f32)).astype(bf16)
        both = jnp.dot(
            jnp.concatenate([upper, lower], axis=1), whole, preferred_element_type=f32
        )
        y = both[:, :block] + both[:, block:]
        if k < pieces - 1:
            last = jnp.where(
                jnp.broadcast_to(side, y.shape),
                jnp.broadcast_to(y[:, :1], y.shape),
                jnp.broadcast_to(y[:, block - 1 :], y.shape),
            )
        if before is not None:
            y = y + before * carry
            last = last + before * carry_last
        before = last
        settled[:, :, here] = y.reshape(bands, rows, block)
    flip = jnp.broadcast_to(side, (rows, block))
    for pair in pairs:
        field = [sea[:, here] for here in pair]
        for f in range(bands):
            values = [settled[f, :, here] for here in pair]
            for at, here in enumerate(pair):
                masked = jnp.where(flip, values[1 - at], values[at]) * field[at]
                near = masked.astype(bf16)
                rounded[f, :, here] = near
                rest[f, :, here] = (masked - near.astype(f32)).astype(bf16)


def settle_one(previous, coupling, inflow_of, gain, sea, rounded, settled, backward, sideways):
    bands, rows, columns = previous.shape
    block = BLOCK
    quarter = bands // 4
    pieces = columns // block
    gains = jnp.full((1, block), gain, f32)
    slope, scale = jnp.log(gains / (1.0 + gains)), 1.0 / (1.0 + gains)
    row = lax.broadcasted_iota(jnp.int32, (block, block), 0)
    column = lax.broadcasted_iota(jnp.int32, (block, block), 1)
    offset = row - column if sideways else column - row
    matrix = jnp.where(offset >= 0, jnp.exp(offset.astype(f32) * slope) * scale, 0.0)
    carry = gains * (matrix[block - 1 :] if sideways else matrix[:1])
    carry_last = carry[:, :1] if sideways else carry[:, block - 1 :]
    high = matrix.astype(bf16)
    low = (matrix - high.astype(f32)).astype(bf16)
    whole = jnp.concatenate(
        [
            jnp.concatenate([high, low], axis=1),
            jnp.concatenate([high, jnp.zeros_like(low)], axis=1),
        ],
        axis=0,
    )
    order = visit_order((rows, block), backward)
    before = None
    for k in range(pieces - 1, -1, -1) if sideways else range(pieces):
        here = slice(k * block, (k + 1) * block)
        couple, weight = weights(coupling[:, here], sea[:, here])
        first = jnp.where(order == 0, couple, 0.0)
        spans, reach, span = [], couple, 1
        while span < rows:
            spans.append((span, jnp.where(order >= span, reach, 0.0)))
            reach = jnp.where(order >= span, reach * rolled(reach, span, backward), reach)
            span *= 2
        values = []
        for f in range(bands):
            value = weight * previous[f, :, here].astype(f32) + first * inflow_of(
                f // quarter, f % quarter, here
            )
            for span, factor in spans:
                value = value + factor * rolled(value, span, backward)
            values.append(value)
        x = jnp.concatenate(values, axis=0)
        upper = x.astype(bf16)
        lower = (x - upper.astype(f32)).astype(bf16)
        both = jnp.dot(
            jnp.concatenate([upper, lower], axis=1), whole, preferred_element_type=f32
        )
        y = both[:, :block] + both[:, block:]
        last = jnp.broadcast_to(y[:, :1] if sideways else y[:, block - 1 :], y.shape)
        if before is not None:
            y = y + before * carry
            last = last + before * carry_last
        before = last
        masked = y.reshape(bands, rows, block) * sea[:, here][None]
        rounded[:, :, here] = masked.astype(bf16)
        if settled is not None:
            settled[:, :, here] = masked


def settle(previous, coupling, inflow_of, corner, gain, sea, rounded, settled):
    for flag in range(4):
        pl.when(corner == flag)(
            functools.partial(
                settle_one, previous, coupling, inflow_of, gain, sea, rounded, settled,
                flag % 2 == 1, flag // 2 == 1,
            )
        )


def wet_field(wet_columns, wet):
    rows, columns = wet.shape
    row = lax.broadcasted_iota(jnp.int32, (rows, rows), 0)
    column = lax.broadcasted_iota(jnp.int32, (rows, rows), 1)
    for k in range(columns // BLOCK):
        flags = jnp.broadcast_to(wet_columns[k : k + 1].astype(f32), (rows, rows))
        flag = jnp.sum(jnp.where(row == column, flags, 0.0), axis=1, keepdims=True)
        wet[:, k * BLOCK : (k + 1) * BLOCK] = jnp.broadcast_to(flag, (rows, BLOCK))


def source(coef, own, onward_of, against_of, rest, wet, result):
    bands = own.shape[0]
    wet_cells = wet[...]

    def one(f, onward, against):
        energy = own[f].astype(f32)
        value = coef[f] * (
            energy * energy * (onward + against) - 2.0 * energy * onward * against
        )
        base = energy + rest[f].astype(f32)
        result[f] = (base + wet_cells * value.astype(bf16).astype(f32)).astype(bf16)

    def above(f):
        return onward_of[f + 1].astype(f32)

    def below(f):
        return against_of[f - 1].astype(f32)

    nothing = jnp.zeros(wet.shape, f32)
    one(0, above(0), nothing)
    one(bands - 1, nothing, below(bands - 1))

    def body(f, _):
        one(f, above(f), below(f))
        return 0

    lax.fori_loop(1, bands - 1, body, 0, unroll=True)


def source_kernel(
    marks_in, coef_in, sea_in, wet_in, previous_in, entering_in, coupling_in, own_in, rest_in,
    out, halo_marks, coef, previous, incoming, entering, coupling, own, rest, halo, sea_mask, wet_tiles, sea, wet, result,
    load_sem, scalar_sem, store_sem,
):
    dirs, bands, rows, columns = own.shape
    scalars = [
        pltpu.make_async_copy(marks_in, halo_marks, scalar_sem.at[0]),
        pltpu.make_async_copy(coef_in, coef, scalar_sem.at[1]),
    ]
    small = [
        pltpu.make_async_copy(src, dst, load_sem.at[i])
        for i, (src, dst) in enumerate(
            ((sea_in, sea_mask), (wet_in, wet_tiles), (coupling_in, coupling), (entering_in, incoming))
        )
    ]
    previous_load = pltpu.make_async_copy(previous_in, previous, load_sem.at[4])
    cut = dirs // 2 if dirs > 2 * SHIFT else dirs
    late = [
        pltpu.make_async_copy(whole.at[pl.ds(0, to)], held.at[pl.ds(0, to)], load_sem.at[i])
        for i, (whole, held, to) in enumerate(((own_in, own, min(cut + SHIFT, dirs)), (rest_in, rest, cut)), 5)
    ]
    latest = [
        pltpu.make_async_copy(whole.at[pl.ds(at, dirs - at)], held.at[pl.ds(at, dirs - at)], load_sem.at[i])
        for i, (whole, held, at) in enumerate(((own_in, own, cut + SHIFT), (rest_in, rest, cut)), 7)
        if at < dirs
    ]
    if dirs > 2 * SHIFT:
        bounds = [0, SHIFT, dirs // 2, dirs - SHIFT, dirs - 1, dirs]
    else:
        bounds = list(range(dirs + 1))
    stores = [
        pltpu.make_async_copy(
            result.at[pl.ds(at, to - at)], out.at[pl.ds(at, to - at)], store_sem.at[k]
        )
        for k, (at, to) in enumerate(zip(bounds, bounds[1:]))
    ]
    for load in small + scalars:
        load.start()
    for load in [previous_load] + late + latest:
        load.start()
    for load in small + scalars:
        load.wait()
    sea[...] = sea_mask[...].astype(f32)
    wet_field(wet_tiles, wet)
    entering[...] = incoming[...].astype(f32)

    def one_halo(t, _):
        way, at = 1 - t // SHIFT, t % SHIFT
        settle(
            previous.at[t], coupling.at[way, at],
            lambda q, r, here: entering[way, q // 2, q % 2, at, r : r + 1, here],
            halo_marks[t, 1, 0].astype(jnp.int32), halo_marks[t, 0, 0], sea, halo.at[t], None,
        )
        return 0

    previous_load.wait()
    lax.fori_loop(0, 2 * SHIFT, one_halo, 0)
    for load in late:
        load.wait()

    def inner(d, _):
        source(
            coef, own.at[d], own.at[d + SHIFT], own.at[d - SHIFT], rest.at[d], wet, result.at[d]
        )
        return 0

    for store, at, to in zip(stores, bounds, bounds[1:]):
        if at == cut:
            for load in latest:
                load.wait()
        if at >= SHIFT and to <= dirs - SHIFT:
            lax.fori_loop(at, to, inner, 0)
        else:
            for d in range(at, to):
                source(
                    coef, own.at[d],
                    own.at[d + SHIFT] if d + SHIFT < dirs else halo.at[2 * SHIFT + d - dirs],
                    own.at[d - SHIFT] if d >= SHIFT else halo.at[d],
                    rest.at[d], wet, result.at[d],
                )
        store.start()
    for store in stores:
        store.wait()


def add_source(
    halo_marks, quad_coef, sea_mask, wet_tiles, halo_previous, halo_entering, halo_coupling, own, rest
):
    dirs, bands, rows, columns = own.shape
    anywhere = pl.BlockSpec(memory_space=pl.ANY)
    dma = pltpu.SemaphoreType.DMA
    return pl.pallas_call(
        source_kernel,
        in_specs=[anywhere] * 9,
        out_specs=anywhere,
        out_shape=jax.ShapeDtypeStruct(own.shape, bf16),
        scratch_shapes=[
            pltpu.SMEM(halo_marks.shape, f32),
            pltpu.SMEM(quad_coef.shape, f32),
            pltpu.VMEM(halo_previous.shape, bf16),
            pltpu.VMEM(halo_entering.shape, bf16),
            pltpu.VMEM(halo_entering.shape, f32),
            pltpu.VMEM(halo_coupling.shape, f32),
            pltpu.VMEM(own.shape, bf16),
            pltpu.VMEM(own.shape, bf16),
            pltpu.VMEM(halo_previous.shape, bf16),
            pltpu.VMEM(sea_mask.shape, jnp.int32),
            pltpu.VMEM(wet_tiles.shape, jnp.int32),
            pltpu.VMEM((rows, columns), f32),
            pltpu.VMEM((rows, columns), f32),
            pltpu.VMEM(own.shape, bf16),
            dma((9,)), dma((2,)), dma((max(dirs, 5),)),
        ],
        compiler_params=pltpu.CompilerParams(vmem_limit_bytes=STEP_VMEM),
        cost_estimate=cost(6),
        name="add_source",
    )(halo_marks, quad_coef, sea_mask, wet_tiles, halo_previous, halo_entering, halo_coupling, own, rest)


def on_device(
    row_devices, dir_devices,
    previous, boundary, row_coupling, cross_gain, block_inverse, quadrant, sea_mask, wet_tiles, quad_coef,
):
    wet_tiles = wet_tiles.T
    own, rest, halo_previous, halo_entering, halo_coupling, halo_marks = scan_devices(
        row_devices, dir_devices, quadrant, cross_gain, boundary, sea_mask, previous, row_coupling
    )
    return add_source(
        halo_marks, quad_coef, sea_mask, wet_tiles, halo_previous, halo_entering, halo_coupling, own, rest
    )


def solution(mesh):
    in_specs = (
        P("dirs", None, "rows", None),
        P("dirs", None, None),
        P("dirs", "rows", None),
        P("dirs"),
        P("dirs", None, None),
        P("dirs"),
        P("rows", None),
        P("rows", None),
        P(),
    )
    out_specs = P("dirs", None, "rows", None)
    return jax.shard_map(
        functools.partial(on_device, mesh.shape["rows"], mesh.shape["dirs"]),
        mesh=mesh, in_specs=in_specs, out_specs=out_specs, check_vma=False,
    )
```
